32 devices in a mesh: kx: 8 (over z, x), ky: 4 (over y, core).
Axes of the slice: x: 2, y: 2, z: 4, core: 2. Of those that a mesh axis runs over, the one named last changes fastest.
Arguments:
- slip_rate: float32 [3, 2048, 2048], P(None, ('kx', 'ky')), may hold values from -6 to 6
- slip_field: float32 [3, 2048, 2048], P(None, ('kx', 'ky')), may hold values from -6 to 6
- prestress: float32 [3, 2048, 2048], P(None, ('kx', 'ky')), may hold values from -6 to 6
- history: bfloat16 [6, 3, 2, 2048, 2048], P(None, None, None, ('kx', 'ky')), may hold values from -6 to 6
- kernel: float32 [8, 8, 3], replicated, may hold values from -3 to 3
- band_len: int32 [8], replicated, may hold values from 2 to 8, as said below
- mode_band: int32 [2048, 2048], P(('kx', 'ky')), may hold values from 0 to 7
Outputs:
- new_rate: float32 [3, 2048, 2048], P(None, ('kx', 'ky'))
- new_slip: float32 [3, 2048, 2048], P(None, ('kx', 'ky'))
The draws below stay inside these ranges and needn't reach their ends.
Inputs may be any that keep to these rules, and one draw needn't show every extreme that they name: `band_len`: entry 0 equals 8; every other entry lies between 2 and 4.
All inputs are finite; a program needn't handle non-finite values.
Results may differ from the reference program's by a relative error of at most 0.0003.
Values sent between devices are 32-bit elements; how exact they have to be, the bound alone decides.
No kernel may reach another device: no remote copies, remote signals or barrier semaphores. Data moves between devices by JAX's collectives and lax.ppermute only.
A program may use at most 128 MiB of HBM per device.

```python
import jax
import jax.numpy as jnp

NX = 2048
NY = 2048
BANDS = 8
LAGS = 8
STEPS = 1
HIST = 6


def draw_band_len(key, part):
    others = jax.random.randint(key, (BANDS,), 2, LAGS // 2 + 1)
    position = jnp.arange(BANDS, dtype=jnp.int32)
    return jnp.where(position == 0, LAGS, others).astype(jnp.int32)


def draw_mode_band(key, part):
    ymode = jnp.arange(NY, dtype=jnp.int32)[:, None]
    xmode = jnp.arange(NX, dtype=jnp.int32)[None, :]
    ysigned = jnp.where(ymode < NY // 2, ymode, ymode - NY)
    xsigned = jnp.where(xmode < NX // 2, xmode, xmode - NX)
    radius_sq = xsigned * xsigned + ysigned * ysigned
    base = jnp.zeros((NY, NX), jnp.int32)
    for band_index in range(1, BANDS):
        threshold = max(NX * NY // 4 ** (BANDS + 1 - band_index), 1)
        base = base + (radius_sq >= threshold).astype(jnp.int32)
    jitter = jax.random.randint(key, (NY, NX), 0, 3) - 1
    return jnp.clip(base + jitter, 0, BANDS - 1).astype(jnp.int32)


def shard_levels(stream_key, dims, shards, least, largest):
    loudness, own = 1.0, jax.random.fold_in(stream_key, 6)
    for axis_at, parts in shards:
        heights = jnp.exp(jax.random.uniform(jax.random.fold_in(own, axis_at), (parts,), jnp.float32, least / len(shards), largest / len(shards)))
        loudness = loudness * jnp.repeat(heights, dims[axis_at] // parts).reshape([-1 if axis == axis_at else 1 for axis in range(len(dims))])
    return loudness


def gaussian(rng, dims, scale, reach, cuts=(), held_as=jnp.bfloat16):
    result = scale * jax.random.normal(rng, dims, jnp.float32)
    if cuts:
        result = result * shard_levels(rng, dims, cuts, -0.22, 0.18)
    return jnp.clip(result, -reach, reach).astype(held_as)


def setup_inputs(seed: int = 0) -> dict:
    key_of = jax.random.split(jax.random.key(seed), 8)
    slip_rate = gaussian(key_of[0], (3, NX, NY), 1.0, 6.0, ((1, 32),), jnp.float32)
    slip_field = gaussian(key_of[1], (3, NX, NY), 1.0, 6.0, ((1, 32),), jnp.float32)
    prestress = gaussian(key_of[2], (3, NX, NY), 1.0, 6.0, ((1, 32),), jnp.float32)
    history = gaussian(key_of[3], (HIST, 3, 2, NY, NX), 1.0, 6.0, ((3, 32),))
    kernel = gaussian(key_of[4], (BANDS, LAGS, 3), 0.5, 3.0, (), jnp.float32)
    band_len = draw_band_len(jax.random.fold_in(key_of[7], 71), 0)
    mode_band = draw_mode_band(jax.random.fold_in(key_of[7], 71), 0)
    return {"slip_rate": slip_rate, "slip_field": slip_field, "prestress": prestress, "history": history, "kernel": kernel, "band_len": band_len, "mode_band": mode_band}


static_fric = 0.7
dynamic_fric = 0.35
weaken_slip = 0.5

def friction(stress, total):
    worn = jnp.sqrt(total[0] * total[0] + total[1] * total[1] + 1.0) - 1.0
    coeff = dynamic_fric + (static_fric - dynamic_fric) * jnp.exp(-worn / weaken_slip)
    strength = coeff * jax.nn.softplus(-stress[2])
    magnitude = jnp.sqrt(stress[0] * stress[0] + stress[1] * stress[1] + 1.0)
    glide = jax.nn.softplus(magnitude - strength)
    return jnp.stack([glide * stress[0] / magnitude, glide * stress[1] / magnitude, jax.nn.softplus(stress[2])])

def lag_weights(kernel, band_len, mode_band, lag_index):
    live = (lag_index < band_len).astype(jnp.float32)
    table = kernel[:, lag_index, :] * live[:, None]
    picked = table[mode_band]
    return jnp.transpose(picked, (2, 0, 1))[:, None]

def spectrum(field_real):
    whole = jnp.fft.fft2(field_real, norm='ortho')
    whole = jnp.transpose(whole, (0, 2, 1))
    return jnp.stack([jnp.real(whole), jnp.imag(whole)], axis=1).astype(jnp.float32)

def surface(spectra):
    whole = spectra[:, 0] + 1j * spectra[:, 1]
    whole = jnp.transpose(whole, (0, 2, 1))
    return jnp.real(jnp.fft.ifft2(whole, norm='ortho')).astype(jnp.float32)

def reference(slip_rate, slip_field, prestress, history, kernel, band_len, mode_band):
    computed = [spectrum(slip_rate)]
    speed = slip_rate
    total = slip_field
    for step_index in range(STEPS):
        carried = jnp.zeros_like(computed[0])
        for lag_index in range(1, LAGS):
            weight = lag_weights(kernel, band_len, mode_band, lag_index)
            if lag_index <= len(computed):
                source = computed[lag_index - 1]
            else:
                source = history[lag_index - len(computed) - 1].astype(jnp.float32)
            carried = carried + weight * source
        now = computed[0]
        instant = lag_weights(kernel, band_len, mode_band, 0)
        first_rate = friction(prestress + surface(carried + instant * now), total)
        tried = 0.5 * (now + spectrum(first_rate))
        second_rate = friction(prestress + surface(carried + instant * tried), total)
        total = total + 0.25 * (speed + second_rate)
        speed = second_rate
        if step_index + 1 < STEPS:
            computed = [spectrum(speed)] + computed
    return (speed, total)
```

```python
import functools
import math

import jax
import jax.numpy as jnp
import numpy as np
from jax import lax
from jax.experimental import pallas as pl
from jax.experimental.pallas import tpu as pltpu
from jax.sharding import Mesh, PartitionSpec as P


LANES = 128
RADIX = 8
SHORT = 4
AXES = ("half", "part", "ky")
NEAR = ("part", "ky")
F32 = jnp.float32
BF16 = jnp.bfloat16
ROOT = math.sqrt(0.5)

static_fric = 0.7
dynamic_fric = 0.35
weaken_slip = 0.5


def softplus(value):
    return jnp.maximum(value, 0.0) + jnp.log1p(jnp.exp(-jnp.abs(value)))


def friction(s0, s1, s2, u0, u1):
    worn = jnp.sqrt(u0 * u0 + u1 * u1 + 1.0) - 1.0
    coeff = dynamic_fric + (static_fric - dynamic_fric) * jnp.exp(worn * (-1.0 / weaken_slip))
    tail = jnp.log1p(jnp.exp(-jnp.abs(s2)))
    strength = coeff * (jnp.maximum(-s2, 0.0) + tail)
    magnitude = jnp.sqrt(s0 * s0 + s1 * s1 + 1.0)
    ratio = softplus(magnitude - strength) / magnitude
    return ratio * s0, ratio * s1, jnp.maximum(s2, 0.0) + tail


def split_table(values):
    high = values.astype(BF16)
    low = (values - high.astype(np.float64)).astype(BF16)
    return np.concatenate([high, low], axis=-1)


def tables(length):
    count = length // RADIX
    outer = np.arange(count)
    spots = RADIX * outer[None, :, None] + np.arange(RADIX)[:, None, None]
    angle = 2.0 * np.pi / length * ((spots * outer[None, None, :]) % length)
    cos = np.cos(angle) / math.sqrt(length)
    sin = np.sin(angle) / math.sqrt(length)
    forward = np.concatenate([cos.transpose(0, 2, 1), -sin.transpose(0, 2, 1)], axis=1)
    inverse = np.concatenate([cos, sin], axis=1)
    return forward, inverse


def dot3(table, values):
    depth = values.shape[0]
    high = values.astype(BF16)
    low = (values - high.astype(F32)).astype(BF16)
    left = jnp.concatenate([table, table[:, :depth]], axis=1)
    right = jnp.concatenate([high, high, low], axis=0)
    return jnp.dot(left, right, preferred_element_type=F32)


def c_add(a, b):
    return a[0] + b[0], a[1] + b[1]


def c_sub(a, b):
    return a[0] - b[0], a[1] - b[1]


def forward_eight(a, wanted):
    def four(p, q, r, s):
        t0, t1, t2 = c_add(p, r), c_sub(p, r), c_add(q, s)
        d = c_sub(q, s)
        t3 = (d[1], -d[0])
        return c_add(t0, t2), c_add(t1, t3), c_sub(t0, t2), c_sub(t1, t3)

    even = four(a[0], a[2], a[4], a[6])
    odd = four(a[1], a[3], a[5], a[7])
    o1 = ((odd[1][0] + odd[1][1]) * ROOT, (odd[1][1] - odd[1][0]) * ROOT)
    o2 = (odd[2][1], -odd[2][0])
    o3 = ((odd[3][1] - odd[3][0]) * ROOT, (odd[3][0] + odd[3][1]) * -ROOT)
    turned = (odd[0], o1, o2, o3)
    first = [c_add(even[k], turned[k]) for k in range(4)]
    if wanted <= 4:
        return first
    return first + [c_sub(even[k], turned[k]) for k in range(4)]


def forward_rows(turned, table, flag, sections, packed, out):
    tiles, length, _ = turned.shape
    count = length // RADIX
    owners, comps, rows, _ = out.shape
    modes = packed.shape[1] // 2
    for j in range(RADIX):
        piece = jnp.concatenate([turned[t, pl.ds(j, count, stride=RADIX), :] for t in range(tiles)], axis=1)
        if j % 2:
            piece = piece * flag
        sections[j] = dot3(table[j], piece)
    per = modes // 8

    def chunk(q, carry):
        at = q // per
        off = pl.multiple_of((q % per) * 8, 8)
        row = pl.multiple_of(q * 8, 8)
        parts = [(sections[j, pl.ds(row, 8), :], sections[j, pl.ds(row + count, 8), :]) for j in range(RADIX)]
        outs = forward_eight(parts, 4)
        for k2 in range(RADIX // 2):
            owner = at + k2 * (count // modes)
            packed[owner, pl.ds(off, 8), :] = outs[k2][0]
            packed[owner, pl.ds(off + modes, 8), :] = outs[k2][1]
        return carry

    lax.fori_loop(0, count // 8, chunk, 0)
    top = sections[0, 0:1, :]
    for j in range(1, RADIX):
        top = top - sections[j, 0:1, :] if j % 2 else top + sections[j, 0:1, :]
    packed[0, modes : modes + 1, :] = top

    def send(owner, carry):
        for c in range(comps):
            if c % 2 == 0:
                block = packed[owner, :, pl.ds(c * rows, LANES)].T
            out[owner, c] = block[(c % 2) * rows : (c % 2) * rows + rows]
        return carry

    lax.fori_loop(0, owners, send, 0)


def inverse_rows(arrived, table, even, odd, mixed, turned):
    owners, comps, rows, _ = arrived.shape
    near = owners // 2
    modes = even.shape[1] // 2
    tiles, length, _ = turned.shape
    count = length // RADIX

    def gather(owner, carry):
        sums, differences = [], []
        for c in range(comps):
            mine, other = arrived[owner, c], arrived[owner + near, c]
            sums.append(mine + other)
            differences.append(mine - other)
        blank = jnp.zeros((LANES * tiles - comps * rows, LANES), F32)
        for store, pieces in ((even, sums), (odd, differences)):
            whole = jnp.concatenate(pieces + [blank], axis=0)
            for t in range(tiles):
                store[owner, :, t * LANES : (t + 1) * LANES] = whole[t * LANES : (t + 1) * LANES].T
        return carry

    lax.fori_loop(0, near, gather, 0)
    per = modes // 8

    def chunk(q, carry):
        at = q // per
        off = pl.multiple_of((q % per) * 8, 8)
        row = pl.multiple_of(q * 8, 8)

        def four(s):
            t0, t1, t2 = c_add(s[0], s[2]), c_sub(s[0], s[2]), c_add(s[1], s[3])
            d = c_sub(s[1], s[3])
            t3 = (-d[1], d[0])
            return c_add(t0, t2), c_add(t1, t3), c_sub(t0, t2), c_sub(t1, t3)

        for first, store in ((0, even), (1, odd)):
            parts = []
            for k2 in range(RADIX // 2):
                owner = at + k2 * (count // modes)
                parts.append((store[owner, pl.ds(off, 8), :], store[owner, pl.ds(off + modes, 8), :]))
            if first:
                p1, p2, p3 = parts[1:]
                parts[1] = ((p1[0] - p1[1]) * ROOT, (p1[0] + p1[1]) * ROOT)
                parts[2] = (-p2[1], p2[0])
                parts[3] = ((p3[0] + p3[1]) * -ROOT, (p3[0] - p3[1]) * ROOT)
            for index, value in enumerate(four(parts)):
                mixed[2 * index + first, pl.ds(row, 8), :] = value[0]
                mixed[2 * index + first, pl.ds(row + count, 8), :] = value[1]
        return carry

    lax.fori_loop(0, count // 8, chunk, 0)
    scale = 1.0 / math.sqrt(length)
    for j in range(RADIX):
        piece = dot3(table[j, :count], mixed[j, :count, :]) - dot3(table[j, count:], mixed[j, count:, :])
        if j % 2:
            piece = piece - odd[0, modes : modes + 1, :] * scale
        else:
            piece = piece + even[0, modes : modes + 1, :] * scale
        for t in range(tiles):
            turned[t, pl.ds(j, count, stride=RADIX), :] = piece[:, t * LANES : (t + 1) * LANES]


def turn_in(parts, turned, start):
    tiles = turned.shape[0]
    used = sum(part.shape[0] for part in parts)
    blank = jnp.zeros((LANES * tiles - used, LANES), F32)
    whole = jnp.concatenate(list(parts) + [blank], axis=0)
    for t in range(tiles):
        turned[t, pl.ds(start, LANES), :] = whole[t * LANES : (t + 1) * LANES].T


def turn_out(turned, start, rows, comps):
    tiles = turned.shape[0]
    whole = jnp.concatenate([turned[t, pl.ds(start, LANES), :].T for t in range(tiles)], axis=0)
    return [whole[c * rows : (c + 1) * rows] for c in range(comps)]


def y_forward_kernel(flags, field, table, out, turned, sections, packed):
    length = field.shape[2]

    def load(q, carry):
        start = pl.multiple_of(q * LANES, LANES)
        turn_in([field[c, :, pl.ds(start, LANES)] for c in range(field.shape[0])], turned, start)
        return carry

    lax.fori_loop(0, length // LANES, load, 0)
    forward_rows(turned, table, flags[0], sections, packed, out)


def y_middle_kernel(
    flags, arrived, prestress, slip, rate, inverse, forward, out, stress, turned, even, odd, mixed, sections, packed
):
    comps, rows, length = prestress.shape
    inverse_rows(arrived, inverse, even, odd, mixed, turned)

    def step(q, carry):
        start = pl.multiple_of(q * LANES, LANES)
        lanes = pl.ds(start, LANES)
        parts = turn_out(turned, start, rows, comps)
        s = [prestress[c, :, lanes] + parts[c] for c in range(comps)]
        for c in range(comps):
            stress[c, :, lanes] = s[c]
        first = friction(*s, slip[0, :, lanes], slip[1, :, lanes])
        turn_in([(first[c] - rate[c, :, lanes]) * 0.5 for c in range(comps)], turned, start)
        return carry

    lax.fori_loop(0, length // LANES, step, 0)
    forward_rows(turned, forward, flags[0], sections, packed, out)


def y_final_kernel(arrived, stress, slip, rate, inverse, new_rate, new_slip, turned, even, odd, mixed):
    comps, rows, length = stress.shape
    inverse_rows(arrived, inverse, even, odd, mixed, turned)

    def step(q, carry):
        start = pl.multiple_of(q * LANES, LANES)
        lanes = pl.ds(start, LANES)
        parts = turn_out(turned, start, rows, comps)
        s = [stress[c, :, lanes] + parts[c] for c in range(comps)]
        second = friction(*s, slip[0, :, lanes], slip[1, :, lanes])
        for c in range(comps):
            new_rate[c, :, lanes] = second[c]
            new_slip[c, :, lanes] = slip[c, :, lanes] + 0.25 * (rate[c, :, lanes] + second[c])
        return carry

    lax.fori_loop(0, length // LANES, step, 0)


def x_kernel(has_past, arrived, forward, inverse, weight, *rest):
    if has_past:
        past, out, sections, mixed = rest
    else:
        out, sections, mixed = rest
    near, _, rows, _ = arrived.shape
    far = out.shape[0]
    count = inverse.shape[2] // 2
    for j in range(RADIX):
        piece = jnp.concatenate(
            [arrived[src, 0, pl.ds(j, rows // RADIX, stride=RADIX), :] for src in range(near)], axis=0
        )
        sections[j] = dot3(forward[j], piece)
    sign = jnp.where(lax.broadcasted_iota(jnp.int32, (8, LANES), 1) < LANES // 2, -1.0, 1.0).astype(F32)

    def turn(value):
        return sign * pltpu.roll(value, LANES // 2, 1)

    def chunk(q, carry):
        row = pl.multiple_of(q * 8, 8)
        parts = [(sections[j, pl.ds(row, 8), :], sections[j, pl.ds(row + count, 8), :]) for j in range(RADIX)]
        outs = forward_eight(parts, RADIX)
        z = []
        for k2 in range(RADIX):
            spot = pl.ds(row + k2 * count, 8)
            w = weight[0, spot, :]
            value = w * outs[k2][0] + turn(w * outs[k2][1])
            if has_past:
                value = value + past[0, spot, :]
            z.append(value)

        def four(a, b, c, d):
            t0, t1, t2, t3 = a + c, a - c, b + d, turn(b - d)
            return t0 + t2, t1 + t3, t0 - t2, t1 - t3

        e = four(z[0], z[2], z[4], z[6])
        o = four(z[1], z[3], z[5], z[7])
        o1 = (o[1] + turn(o[1])) * ROOT
        o3 = (turn(o[3]) - o[3]) * ROOT
        turned = (o[0], o1, turn(o[2]), o3)
        for k in range(4):
            mixed[k, pl.ds(row, 8), :] = e[k] + turned[k]
            mixed[k + 4, pl.ds(row, 8), :] = e[k] - turned[k]
        return carry

    lax.fori_loop(0, count // 8, chunk, 0)
    lanes = lax.broadcasted_iota(jnp.int32, (count, LANES), 1)
    wide = jnp.where(lanes < LANES // 2, -1.0, 1.0).astype(F32)
    step = rows // RADIX
    for j in range(RADIX):
        both = dot3(inverse[j], mixed[j])
        value = both[:count] + wide * pltpu.roll(both[count:], LANES // 2, 1)
        for dest in range(far):
            out[dest, 0, pl.ds(j, step, stride=RADIX), :] = value[dest * step : (dest + 1) * step]


def pick(values, bits):
    level = 0
    while len(values) > 1:
        if len(values) % 2:
            values = values + [values[-1]]
        values = [jnp.where(bits[level], values[k + 1], values[k]) for k in range(0, len(values), 2)]
        level += 1
    return values[0]


def bits_of(band, bands):
    return [(band & (1 << level)) != 0 for level in range(max((bands - 1).bit_length(), 1))]


def history_kernel(
    flags, table, band, mirror, extra, history, row_back, now_weight, later_weight, past, stacked, heavy, light
):
    bands, lags, comps = table.shape[0], table.shape[1] // 3, 3
    depth = history.shape[0]
    rows, width = band.shape
    odd = (lax.broadcasted_iota(jnp.int32, (1, width), 1) & 1) == 1
    parity = jnp.where(odd, flags[0], 1.0).astype(F32)

    def entry(b, lag, c):
        return table[b, lag * comps + c]

    def weights_past(own, bits, c):
        found = []
        none = own == 0
        for at in range(depth):
            lag = lags - depth + at
            if lag < SHORT:
                found.append(pick([entry(b, lag, c) for b in range(bands)], bits))
            else:
                found.append(jnp.where(none, entry(0, lag, c), 0.0))
        return found

    def both(bits_own, bits_mirror, c):
        total = [entry(b, 0, c) + entry(b, 1, c) for b in range(bands)]
        only = [entry(b, 0, c) for b in range(bands)]
        return pick(total, bits_own) + pick(total, bits_mirror), pick(only, bits_own) + pick(only, bits_mirror)

    def group(q, carry):
        row = pl.multiple_of(q * 16, 16)
        spot = pl.ds(row, 16)
        own = band[spot, :]
        bits = bits_of(own, bands)
        back = bits_of(mirror[spot, :], bands)
        for c in range(comps):
            sums = [jnp.zeros((16, width), F32) for _ in range(2)]
            for at, w in enumerate(weights_past(own, bits, c)):
                for p in range(2):
                    sums[p] = sums[p] + w * history[at, c, p, spot, :].astype(F32)
            for p in range(2):
                stacked[c, pl.ds(row + p * rows, 16), :] = sums[p]
            first, later = both(bits, back, c)
            for store, value in ((heavy, first * parity), (light, later * parity)):
                store[c, spot, :] = value
                store[c, pl.ds(row + rows, 16), :] = value
        return carry

    lax.fori_loop(0, rows // 16, group, 0)

    edge = flags[1] > 0.0
    own = band[0:1, :]
    back = mirror[0:1, :]
    ex_bits, ex_back = bits_of(extra[0:1, :], bands), bits_of(extra[1:2, :], bands)
    back_bits = bits_of(back, bands)
    for c in range(comps):
        found = weights_past(back, back_bits, c)
        for p in range(2):
            reverse = jnp.zeros((1, width), F32)
            for at, w in enumerate(found):
                spot = (at * comps + c) * 2 + p
                reverse = reverse + w * row_back[spot : spot + 1, :]
            if p:
                reverse = -reverse
            mine = stacked[c, p * rows : p * rows + 1, :]
            stacked[c, p * rows : p * rows + 1, :] = jnp.where(edge, 0.5 * (mine + reverse), mine)
        first, later = both(ex_bits, ex_back, c)
        for store, value in ((heavy, first * parity), (light, later * parity)):
            mine = store[c, 0:1, :]
            store[c, 0:1, :] = jnp.where(edge, 0.5 * mine, mine)
            store[c, rows : rows + 1, :] = jnp.where(edge, 0.5 * value, mine)
    for c in range(comps):
        for t in range(width // LANES):
            spot = pl.ds(t * LANES, LANES)
            past[c, spot, :] = stacked[c, :, spot].T
            now_weight[c, spot, :] = heavy[c, :, spot].T
            later_weight[c, spot, :] = light[c, :, spot].T


VMEM = pl.BlockSpec(memory_space=pltpu.VMEM)
SMEM = pl.BlockSpec(memory_space=pltpu.SMEM)
PARAMS = pltpu.CompilerParams(vmem_limit_bytes=56 * 1024 * 1024)


def y_scratch(length, modes):
    count = length // RADIX
    near = length // 2 // modes
    wide = 2 * LANES
    turned = pltpu.VMEM((2, length, LANES), F32)
    halves = pltpu.VMEM((near, 2 * modes, wide), F32)
    sections = pltpu.VMEM((RADIX, 2 * count, wide), F32)
    return turned, halves, sections


def struct(*shape):
    return jax.ShapeDtypeStruct(shape, F32)


def with_kernels(slip_rate, slip_field, prestress, history, kernel, band_len, mode_band):
    comps, rows, length = slip_rate.shape
    modes, wide = mode_band.shape
    far = lax.axis_size(AXES)
    near = lax.axis_size(NEAR)
    bands, lags = kernel.shape[:2]
    depth = history.shape[0]
    flags, coded, extra, mirror, row_back = prepare(history, kernel, band_len, mode_band)

    y_forward, y_inverse = (jnp.asarray(split_table(t)) for t in tables(length))
    x_forward, x_inverse = tables(wide)
    x_forward = jnp.asarray(split_table(x_forward[:, :, : wide // RADIX // 2]))
    x_inverse = jnp.asarray(split_table(x_inverse))

    turned, halves, sections = y_scratch(length, modes)
    sent = pl.pallas_call(
        y_forward_kernel,
        out_shape=struct(near, comps, rows, 2 * modes),
        in_specs=[SMEM, VMEM, VMEM],
        out_specs=VMEM,
        scratch_shapes=[turned, sections, halves],
        compiler_params=PARAMS,
        name="y_forward",
    )(flags, slip_rate, y_forward)
    here = lax.all_to_all(sent, NEAR, 0, 0, tiled=True)

    chunk = 2 * LANES
    blocks = [
        SMEM,
        SMEM,
        pl.BlockSpec((modes, chunk), lambda g: (0, g)),
        pl.BlockSpec((modes, chunk), lambda g: (0, g)),
        pl.BlockSpec((2, chunk), lambda g: (0, g)),
        pl.BlockSpec((depth, comps, 2, modes, chunk), lambda g: (0, 0, 0, 0, g)),
        pl.BlockSpec((depth * comps * 2, chunk), lambda g: (0, g)),
    ]
    out_block = pl.BlockSpec((comps, chunk, 2 * modes), lambda g: (0, g, 0))
    now_weight, later_weight, past = pl.pallas_call(
        history_kernel,
        grid=(wide // chunk,),
        out_shape=[struct(comps, wide, 2 * modes)] * 3,
        in_specs=blocks,
        out_specs=[out_block] * 3,
        scratch_shapes=[pltpu.VMEM((comps, 2 * modes, chunk), F32)] * 3,
        compiler_params=PARAMS,
        name="history",
    )(flags, coded, mode_band, mirror, extra, history, row_back)

    def x_stage(given, weight, added):
        whole = pl.BlockSpec((1, wide, 2 * modes), lambda c: (c, 0, 0))
        fixed = [
            pl.BlockSpec(x_forward.shape, lambda c: (0, 0, 0)),
            pl.BlockSpec(x_inverse.shape, lambda c: (0, 0, 0)),
        ]
        operands = [given, x_forward, x_inverse, weight] + ([] if added is None else [added])
        count = wide // RADIX
        return pl.pallas_call(
            functools.partial(x_kernel, added is not None),
            grid=(comps,),
            out_shape=struct(far, comps, rows, 2 * modes),
            in_specs=[pl.BlockSpec((near, 1, rows, 2 * modes), lambda c: (0, c, 0, 0))]
            + fixed
            + [whole] * (len(operands) - 3),
            out_specs=pl.BlockSpec((far, 1, rows, 2 * modes), lambda c: (0, c, 0, 0)),
            scratch_shapes=[
                pltpu.VMEM((RADIX, 2 * count, LANES), F32),
                pltpu.VMEM((RADIX, count, LANES), F32),
            ],
            compiler_params=PARAMS,
            name="x_stage",
        )(*operands)

    back = lax.all_to_all(x_stage(here, now_weight, past), AXES, 0, 0, tiled=True)
    sent, stress = pl.pallas_call(
        y_middle_kernel,
        out_shape=[struct(near, comps, rows, 2 * modes), struct(comps, rows, length)],
        in_specs=[SMEM] + [VMEM] * 6,
        out_specs=[VMEM] * 2,
        scratch_shapes=[turned, halves, halves, sections, sections, halves],
        compiler_params=PARAMS,
        name="y_middle",
    )(flags, back, prestress, slip_field, slip_rate, y_inverse, y_forward)
    here = lax.all_to_all(sent, NEAR, 0, 0, tiled=True)
    back = lax.all_to_all(x_stage(here, later_weight, None), AXES, 0, 0, tiled=True)
    return tuple(
        pl.pallas_call(
            y_final_kernel,
            out_shape=[struct(comps, rows, length)] * 2,
            in_specs=[VMEM] * 5,
            out_specs=[VMEM] * 2,
            scratch_shapes=[turned, halves, halves, sections],
            compiler_params=PARAMS,
            name="y_final",
        )(back, stress, slip_field, slip_rate, y_inverse)
    )


def reverse_modes(values):
    return jnp.roll(jnp.flip(values, -1), 1, -1)


def prepare(history, kernel, band_len, mode_band):
    bands, lags, comps = kernel.shape
    modes, wide = mode_band.shape
    far = lax.axis_size(AXES)
    near = lax.axis_size(NEAR)
    me = lax.axis_index(AXES)
    first = me % near == 0
    flags = jnp.stack([jnp.where(me < near, 1.0, -1.0), jnp.where(first, 1.0, 0.0)]).astype(F32)
    live = (jnp.arange(lags, dtype=jnp.int32)[None, :] < band_len[:, None]).astype(F32)
    coded = (kernel * live[:, :, None]).reshape(bands, lags * comps)
    block = lax.ppermute(mode_band, AXES, [(d, far - 1 - d) for d in range(far)])
    edge = lax.ppermute(mode_band[:1], AXES, [(d, (far - d) % far) for d in range(far)])
    opposite = lax.ppermute(mode_band[:1], AXES, [(d, (d + near) % far) for d in range(far)])
    mirror = jnp.concatenate([edge, jnp.flip(block[1:], 0)], axis=0)
    mirror = reverse_modes(mirror)
    extra = jnp.concatenate([opposite, reverse_modes(opposite)], axis=0)
    row_back = reverse_modes(history[:, :, :, 0, :].astype(F32).reshape(-1, wide))
    return flags, coded, extra, mirror, row_back


def plain(slip_rate, slip_field, prestress, history, kernel, band_len, mode_band):
    comps, rows, length = slip_rate.shape
    modes, wide = mode_band.shape
    far = lax.axis_size(AXES)
    near = lax.axis_size(NEAR)
    bands, lags = kernel.shape[:2]
    depth = history.shape[0]
    flags, coded, extra, mirror, row_back = prepare(history, kernel, band_len, mode_band)
    table = coded.reshape(bands, lags, comps)
    edge = flags[1] > 0.0
    top = (jnp.arange(modes) == 0)[None, :, None] & edge

    def dot(spec, a, b):
        return jnp.einsum(spec, a, b, precision=lax.Precision.HIGHEST)

    def angles(first, second, size):
        product = (first[:, None] * second[None, :]) % size
        angle = product.astype(F32) * (2.0 * math.pi / size)
        return jnp.cos(angle) / math.sqrt(size), jnp.sin(angle) / math.sqrt(size)

    def weights(band, values):
        result = jnp.zeros(values.shape[1:] + band.shape, F32)
        for b in range(bands):
            result = jnp.where(band == b, values[b][..., None, None], result)
        return result

    past = []
    for at in range(depth):
        w = weights(mode_band, table[:, lags - depth + at])[:, None]
        past.append(w * history[at].astype(F32))
    past = sum(past)
    back = row_back.reshape(depth, comps, 2, 1, wide)
    w = weights(mirror[:1], table[:, lags - depth :])
    back = jnp.sum(w[:, :, None] * back, axis=0) * jnp.array([1.0, -1.0], F32)[:, None, None]
    past = jnp.where(top, 0.5 * (past + back), past)
    parity = jnp.where(jnp.arange(wide) % 2 == 1, flags[0], 1.0)

    def filters(values):
        whole = (weights(mode_band, values) + weights(mirror, values)) * parity
        other = (weights(extra[:1], values) + weights(extra[1:], values)) * parity
        return jnp.where(top, 0.5 * whole, whole), jnp.where(top, 0.5 * other, whole)

    own = jnp.arange(length, dtype=jnp.int32)
    y_cos, y_sin = angles(own, own[: length // 2], length)
    nyquist = jnp.where(own % 2 == 1, -1.0, 1.0).astype(F32) / math.sqrt(length)
    y_sin = y_sin.at[:, 0].set(-nyquist)
    across = jnp.arange(wide, dtype=jnp.int32)
    x_cos, x_sin = angles(across, across, wide)
    flip = jnp.where(own % 2 == 1, flags[0], 1.0)

    def y_forward(field):
        field = field * flip
        both = jnp.stack([dot("cxy,yk->ckx", field, y_cos), -dot("cxy,yk->ckx", field, y_sin)], 1)
        both = both.reshape(comps, 2, near, modes, rows).transpose(2, 0, 4, 1, 3)
        return lax.all_to_all(both, NEAR, 0, 0, tiled=True)

    def x_stage(given, filt, added):
        given = given.transpose(1, 3, 4, 0, 2).reshape(comps, 2, modes, near * rows)
        real = dot("cpkx,xm->cpkm", given, x_cos[: near * rows])
        imag = -dot("cpkx,xm->cpkm", given, x_sin[: near * rows])
        a, b = filt
        out_real = a * real[:, 0] - b * imag[:, 1]
        out_imag = a * imag[:, 0] + b * real[:, 1]
        if added is not None:
            out_real, out_imag = out_real + added[:, 0], out_imag + added[:, 1]
        first = dot("ckm,mx->ckx", out_real, x_cos) - dot("ckm,mx->ckx", out_imag, x_sin)
        second = dot("ckm,mx->ckx", out_real, x_sin) + dot("ckm,mx->ckx", out_imag, x_cos)
        both = jnp.stack([first, second], 1).reshape(comps, 2, modes, far, rows).transpose(3, 0, 4, 1, 2)
        return lax.all_to_all(both, AXES, 0, 0, tiled=True)

    def y_inverse(given):
        given = given.reshape(2, near, comps, rows, 2, modes).transpose(0, 4, 2, 3, 1, 5)
        given = given.reshape(2, 2, comps, rows, length // 2)
        half = dot("hcxk,yk->hcxy", given[:, 0], y_cos) - dot("hcxk,yk->hcxy", given[:, 1], y_sin)
        return half[0] + half[1] * jnp.where(own % 2 == 1, -1.0, 1.0)

    def phi(s):
        return jnp.stack(friction(s[0], s[1], s[2], slip_field[0], slip_field[1]))

    now = filters(table[:, 0] + table[:, 1])
    later = filters(table[:, 0])
    stress = prestress + y_inverse(x_stage(y_forward(slip_rate), now, past))
    shift = 0.5 * (phi(stress) - slip_rate)
    second = phi(stress + y_inverse(x_stage(y_forward(shift), later, None)))
    return second, slip_field + 0.25 * (slip_rate + second)


def solution(mesh):
    shape = mesh.devices.shape
    ours = Mesh(mesh.devices.reshape(2, shape[0] // 2, shape[1]), AXES)

    def on_device(slip_rate, slip_field, prestress, history, kernel, band_len, mode_band):
        args = (slip_rate, slip_field, prestress, history, kernel, band_len, mode_band)
        rows, modes = slip_rate.shape[1], mode_band.shape[0]
        if 2 * modes == LANES and 2 * rows == LANES:
            return with_kernels(*args)
        return plain(*args)

    rows = P(None, AXES, None)
    return jax.shard_map(
        on_device,
        mesh=ours,
        in_specs=(rows, rows, rows, P(None, None, None, AXES, None), P(), P(), P(AXES, None)),
        out_specs=(rows, rows),
        check_vma=False,
    )
```

```python
import functools
import math

import jax
import jax.numpy as jnp
import numpy as np
from jax import lax
from jax.experimental import pallas as pl
from jax.experimental.pallas import tpu as pltpu
from jax.sharding import Mesh, PartitionSpec as P


LANES = 128
RADIX = 8
SHORT = 4
AXES = ("half", "part", "ky")
NEAR = ("part", "ky")
F32 = jnp.float32
BF16 = jnp.bfloat16
ROOT = math.sqrt(0.5)

static_fric = 0.7
dynamic_fric = 0.35
weaken_slip = 0.5


def softplus(value):
    return jnp.maximum(value, 0.0) + jnp.log1p(jnp.exp(-jnp.abs(value)))


def friction(s0, s1, s2, u0, u1):
    worn = jnp.sqrt(u0 * u0 + u1 * u1 + 1.0) - 1.0
    coeff = dynamic_fric + (static_fric - dynamic_fric) * jnp.exp(worn * (-1.0 / weaken_slip))
    tail = jnp.log1p(jnp.exp(-jnp.abs(s2)))
    strength = coeff * (jnp.maximum(-s2, 0.0) + tail)
    magnitude = jnp.sqrt(s0 * s0 + s1 * s1 + 1.0)
    ratio = softplus(magnitude - strength) / magnitude
    return ratio * s0, ratio * s1, jnp.maximum(s2, 0.0) + tail


def split_table(values):
    high = values.astype(BF16)
    low = (values - high.astype(np.float64)).astype(BF16)
    return np.concatenate([high, low], axis=-1)


def tables(length):
    count = length // RADIX
    outer = np.arange(count)
    spots = RADIX * outer[None, :, None] + np.arange(RADIX)[:, None, None]
    angle = 2.0 * np.pi / length * ((spots * outer[None, None, :]) % length)
    cos = np.cos(angle) / math.sqrt(length)
    sin = np.sin(angle) / math.sqrt(length)
    forward = np.concatenate([cos.transpose(0, 2, 1), -sin.transpose(0, 2, 1)], axis=1)
    inverse = np.concatenate([cos, sin], axis=1)
    return forward, inverse


def dot3(table, values):
    depth = values.shape[0]
    high = values.astype(BF16)
    low = (values - high.astype(F32)).astype(BF16)
    left = jnp.concatenate([table, table[:, :depth]], axis=1)
    right = jnp.concatenate([high, high, low], axis=0)
    return jnp.dot(left, right, preferred_element_type=F32)


def c_add(a, b):
    return a[0] + b[0], a[1] + b[1]


def c_sub(a, b):
    return a[0] - b[0], a[1] - b[1]


def forward_eight(a, wanted):
    def four(p, q, r, s):
        t0, t1, t2 = c_add(p, r), c_sub(p, r), c_add(q, s)
        d = c_sub(q, s)
        t3 = (d[1], -d[0])
        return c_add(t0, t2), c_add(t1, t3), c_sub(t0, t2), c_sub(t1, t3)

    even = four(a[0], a[2], a[4], a[6])
    odd = four(a[1], a[3], a[5], a[7])
    o1 = ((odd[1][0] + odd[1][1]) * ROOT, (odd[1][1] - odd[1][0]) * ROOT)
    o2 = (odd[2][1], -odd[2][0])
    o3 = ((odd[3][1] - odd[3][0]) * ROOT, (odd[3][0] + odd[3][1]) * -ROOT)
    turned = (odd[0], o1, o2, o3)
    first = [c_add(even[k], turned[k]) for k in range(4)]
    if wanted <= 4:
        return first
    return first + [c_sub(even[k], turned[k]) for k in range(4)]


def forward_rows(turned, table, flag, sections, packed, out):
    tiles, length, _ = turned.shape
    count = length // RADIX
    owners, comps, rows, _ = out.shape
    modes = packed.shape[1] // 2
    for j in range(RADIX):
        piece = jnp.concatenate([turned[t, pl.ds(j, count, stride=RADIX), :] for t in range(tiles)], axis=1)
        if j % 2:
            piece = piece * flag
        sections[j] = dot3(table[j], piece)
    per = modes // 8

    def chunk(q, carry):
        at = q // per
        off = pl.multiple_of((q % per) * 8, 8)
        row = pl.multiple_of(q * 8, 8)
        parts = [(sections[j, pl.ds(row, 8), :], sections[j, pl.ds(row + count, 8), :]) for j in range(RADIX)]
        found = forward_eight(parts, 4)
        for k2 in range(RADIX // 2):
            owner = at + k2 * (count // modes)
            packed[owner, pl.ds(off, 8), :] = found[k2][0]
            packed[owner, pl.ds(off + modes, 8), :] = found[k2][1]
        return carry

    lax.fori_loop(0, count // 8, chunk, 0, unroll=8)
    top = sections[0, 0:1, :]
    for j in range(1, RADIX):
        top = top - sections[j, 0:1, :] if j % 2 else top + sections[j, 0:1, :]
    packed[0, modes : modes + 1, :] = top

    def send(owner, carry):
        for c in range(comps):
            if c % 2 == 0:
                block = packed[owner, :, pl.ds(c * rows, LANES)].T
            out[owner, c] = block[(c % 2) * rows : (c % 2) * rows + rows]
        return carry

    lax.fori_loop(0, owners, send, 0, unroll=4)


def inverse_rows(arrived, table, even, odd, mixed, turned):
    owners, comps, rows, _ = arrived.shape
    near = owners // 2
    modes = even.shape[1] // 2
    tiles, length, _ = turned.shape
    count = length // RADIX

    def gather(owner, carry):
        sums, differences = [], []
        for c in range(comps):
            mine, other = arrived[owner, c], arrived[owner + near, c]
            sums.append(mine + other)
            differences.append(mine - other)
        blank = jnp.zeros((LANES * tiles - comps * rows, LANES), F32)
        for store, pieces in ((even, sums), (odd, differences)):
            whole = jnp.concatenate(pieces + [blank], axis=0)
            for t in range(tiles):
                store[owner, :, t * LANES : (t + 1) * LANES] = whole[t * LANES : (t + 1) * LANES].T
        return carry

    lax.fori_loop(0, near, gather, 0, unroll=4)
    per = modes // 8

    def chunk(q, carry):
        at = q // per
        off = pl.multiple_of((q % per) * 8, 8)
        row = pl.multiple_of(q * 8, 8)

        def four(s):
            t0, t1, t2 = c_add(s[0], s[2]), c_sub(s[0], s[2]), c_add(s[1], s[3])
            d = c_sub(s[1], s[3])
            t3 = (-d[1], d[0])
            return c_add(t0, t2), c_add(t1, t3), c_sub(t0, t2), c_sub(t1, t3)

        for first, store in ((0, even), (1, odd)):
            parts = []
            for k2 in range(RADIX // 2):
                owner = at + k2 * (count // modes)
                parts.append((store[owner, pl.ds(off, 8), :], store[owner, pl.ds(off + modes, 8), :]))
            if first:
                p1, p2, p3 = parts[1:]
                parts[1] = ((p1[0] - p1[1]) * ROOT, (p1[0] + p1[1]) * ROOT)
                parts[2] = (-p2[1], p2[0])
                parts[3] = ((p3[0] + p3[1]) * -ROOT, (p3[0] - p3[1]) * ROOT)
            for index, value in enumerate(four(parts)):
                mixed[2 * index + first, pl.ds(row, 8), :] = value[0]
                mixed[2 * index + first, pl.ds(row + count, 8), :] = value[1]
        return carry

    lax.fori_loop(0, count // 8, chunk, 0, unroll=8)
    scale = 1.0 / math.sqrt(length)
    for j in range(RADIX):
        piece = dot3(table[j, :count], mixed[j, :count, :]) - dot3(table[j, count:], mixed[j, count:, :])
        if j % 2:
            piece = piece - odd[0, modes : modes + 1, :] * scale
        else:
            piece = piece + even[0, modes : modes + 1, :] * scale
        for t in range(tiles):
            turned[t, pl.ds(j, count, stride=RADIX), :] = piece[:, t * LANES : (t + 1) * LANES]


def turn_in(parts, turned, start):
    tiles = turned.shape[0]
    used = sum(part.shape[0] for part in parts)
    blank = jnp.zeros((LANES * tiles - used, LANES), F32)
    whole = jnp.concatenate(list(parts) + [blank], axis=0)
    for t in range(tiles):
        turned[t, pl.ds(start, LANES), :] = whole[t * LANES : (t + 1) * LANES].T


def turn_out(turned, start, rows, comps):
    tiles = turned.shape[0]
    whole = jnp.concatenate([turned[t, pl.ds(start, LANES), :].T for t in range(tiles)], axis=0)
    return [whole[c * rows : (c + 1) * rows] for c in range(comps)]


def y_forward_kernel(flags, field, table, out, turned, sections, packed):
    comps, _, length = field.shape

    def load(q, carry):
        start = pl.multiple_of(q * LANES, LANES)
        turn_in([field[c, :, pl.ds(start, LANES)] for c in range(comps)], turned, start)
        return carry

    lax.fori_loop(0, length // LANES, load, 0, unroll=4)
    forward_rows(turned, table, flags[0], sections, packed, out)


def y_middle_kernel(
    flags, prestress, slip, rate, inverse, forward, arrived, out, stress, turned, even, odd, mixed, sections, packed
):
    comps, rows, length = prestress.shape
    inverse_rows(arrived, inverse, even, odd, mixed, turned)

    def step(q, carry):
        start = pl.multiple_of(q * LANES, LANES)
        lanes = pl.ds(start, LANES)
        parts = turn_out(turned, start, rows, comps)
        s = [prestress[c, :, lanes] + parts[c] for c in range(comps)]
        for c in range(comps):
            stress[c, :, lanes] = s[c]
        first = friction(*s, slip[0, :, lanes], slip[1, :, lanes])
        turn_in([(first[c] - rate[c, :, lanes]) * 0.5 for c in range(comps)], turned, start)
        return carry

    lax.fori_loop(0, length // LANES, step, 0, unroll=2)
    forward_rows(turned, forward, flags[0], sections, packed, out)


def y_final_kernel(stress, slip, rate, inverse, arrived, new_rate, new_slip, turned, even, odd, mixed):
    comps, rows, length = stress.shape
    inverse_rows(arrived, inverse, even, odd, mixed, turned)

    def step(q, carry):
        start = pl.multiple_of(q * LANES, LANES)
        lanes = pl.ds(start, LANES)
        parts = turn_out(turned, start, rows, comps)
        s = [stress[c, :, lanes] + parts[c] for c in range(comps)]
        second = friction(*s, slip[0, :, lanes], slip[1, :, lanes])
        for c in range(comps):
            new_rate[c, :, lanes] = second[c]
            new_slip[c, :, lanes] = slip[c, :, lanes] + 0.25 * (rate[c, :, lanes] + second[c])
        return carry

    lax.fori_loop(0, length // LANES, step, 0, unroll=2)


def x_kernel(has_past, arrived, forward, inverse, weight, *rest):
    if has_past:
        past, out, sections, mixed = rest
    else:
        out, sections, mixed = rest
    near, _, rows, _ = arrived.shape
    far = out.shape[0]
    count = inverse.shape[2] // 2
    for j in range(RADIX):
        piece = jnp.concatenate(
            [arrived[src, 0, pl.ds(j, rows // RADIX, stride=RADIX), :] for src in range(near)], axis=0
        )
        sections[j] = dot3(forward[j], piece)
    sign = jnp.where(lax.broadcasted_iota(jnp.int32, (8, LANES), 1) < LANES // 2, -1.0, 1.0).astype(F32)

    def turn(value):
        return sign * pltpu.roll(value, LANES // 2, 1)

    def chunk(q, carry):
        row = pl.multiple_of(q * 8, 8)
        parts = [(sections[j, pl.ds(row, 8), :], sections[j, pl.ds(row + count, 8), :]) for j in range(RADIX)]
        outs = forward_eight(parts, RADIX)
        z = []
        for k2 in range(RADIX):
            spot = pl.ds(row + k2 * count, 8)
            w = weight[0, spot, :]
            value = w * outs[k2][0] + turn(w * outs[k2][1])
            if has_past:
                value = value + past[0, spot, :]
            z.append(value)

        def four(a, b, c, d):
            t0, t1, t2, t3 = a + c, a - c, b + d, turn(b - d)
            return t0 + t2, t1 + t3, t0 - t2, t1 - t3

        e = four(z[0], z[2], z[4], z[6])
        o = four(z[1], z[3], z[5], z[7])
        o1 = (o[1] + turn(o[1])) * ROOT
        o3 = (turn(o[3]) - o[3]) * ROOT
        turned = (o[0], o1, turn(o[2]), o3)
        for k in range(4):
            mixed[k, pl.ds(row, 8), :] = e[k] + turned[k]
            mixed[k + 4, pl.ds(row, 8), :] = e[k] - turned[k]
        return carry

    lax.fori_loop(0, count // 8, chunk, 0, unroll=8)
    lanes = lax.broadcasted_iota(jnp.int32, (count, LANES), 1)
    wide = jnp.where(lanes < LANES // 2, -1.0, 1.0).astype(F32)
    step = rows // RADIX
    for j in range(RADIX):
        both = dot3(inverse[j], mixed[j])
        value = both[:count] + wide * pltpu.roll(both[count:], LANES // 2, 1)
        for dest in range(far):
            out[dest, 0, pl.ds(j, step, stride=RADIX), :] = value[dest * step : (dest + 1) * step]


def pick(values, bits):
    level = 0
    while len(values) > 1:
        if len(values) % 2:
            values = values + [values[-1]]
        values = [jnp.where(bits[level], values[k + 1], values[k]) for k in range(0, len(values), 2)]
        level += 1
    return values[0]


def bits_of(band, bands):
    return [(band & (1 << level)) != 0 for level in range(max((bands - 1).bit_length(), 1))]


def weights_past(table, band, bits, c, depth):
    bands, lags, comps = table.shape[0], table.shape[1] // 3, 3
    found = []
    for at in range(depth):
        spot = (lags - depth + at) * comps + c
        if lags - depth + at < SHORT:
            found.append(pick([table[b, spot] for b in range(bands)], bits))
        else:
            found.append(jnp.where(band == 0, table[0, spot], 0.0))
    return found


def history_kernel(flags, table, band, row_mirror, history, row_back, past, stacked):
    bands, comps = table.shape[0], 3
    depth = history.shape[0]
    rows, width = band.shape

    def group(q, carry):
        spot = pl.ds(pl.multiple_of(q * 16, 16), 16)
        own = band[spot, :]
        bits = bits_of(own, bands)
        for c in range(comps):
            sums = [jnp.zeros((16, width), F32) for _ in range(2)]
            for at, w in enumerate(weights_past(table, own, bits, c, depth)):
                for p in range(2):
                    sums[p] = sums[p] + w * history[at, c, p, spot, :].astype(F32)
            for p in range(2):
                stacked[c, pl.ds(pl.multiple_of(q * 16 + p * rows, 16), 16), :] = sums[p]
        return carry

    lax.fori_loop(0, rows // 16, group, 0)

    edge = flags[1] > 0.0
    back = row_mirror[...]
    bits = bits_of(back, bands)
    for c in range(comps):
        found = weights_past(table, back, bits, c, depth)
        for p in range(2):
            reverse = jnp.zeros((1, width), F32)
            for at, w in enumerate(found):
                spot = (at * comps + c) * 2 + p
                reverse = reverse + w * row_back[spot : spot + 1, :]
            if p:
                reverse = -reverse
            mine = stacked[c, p * rows : p * rows + 1, :]
            stacked[c, p * rows : p * rows + 1, :] = jnp.where(edge, 0.5 * (mine + reverse), mine)
        for t in range(width // LANES):
            spot = pl.ds(t * LANES, LANES)
            past[c, spot, :] = stacked[c, :, spot].T


def weight_kernel(flags, table, band, few, block, few_back, block_edge, few_edge, flip, swap, out, stacked):
    bands, comps = table.shape
    rows, width = band.shape
    odd = (lax.broadcasted_iota(jnp.int32, (1, width), 1) & 1) == 1
    parity = jnp.where(odd, flags[0], 1.0).astype(F32)
    edge = flags[1] > 0.0

    def exact(values):
        return values.astype(F32).astype(BF16)

    there = jnp.concatenate([exact(block[...]), exact(few_back[...])], axis=0)
    beyond = jnp.concatenate([exact(block_edge[...]), exact(few_edge[...])], axis=0)
    turned = jnp.dot(jnp.concatenate([there, beyond], axis=1), flip[...], preferred_element_type=F32)
    turned = jnp.dot(swap[...], turned.astype(BF16), preferred_element_type=F32).astype(jnp.int32)
    for c in range(comps):
        values = [table[b, c] for b in range(bands)]
        for q in range(rows // 8):
            spot = slice(q * 8, q * 8 + 8)
            value = pick(values, bits_of(band[spot, :], bands)) + pick(values, bits_of(turned[spot], bands))
            value = value * parity
            if q == 0:
                first = lax.broadcasted_iota(jnp.int32, (8, width), 0) == 0
                other = pick(values, bits_of(few[1:2, :], bands))
                other = other + pick(values, bits_of(turned[rows : rows + 1], bands))
                other = jnp.where(edge, 0.5 * (other * parity), value[:1])
                value = jnp.where(first & edge, 0.5 * value, value)
                stacked[rows : rows + 8, :] = jnp.where(first, other, value)
            else:
                stacked[rows + q * 8 : rows + q * 8 + 8, :] = value
            stacked[spot, :] = value
        for t in range(width // LANES):
            spot = slice(t * LANES, (t + 1) * LANES)
            out[c, spot, :] = stacked[:, spot].T


VMEM = pl.BlockSpec(memory_space=pltpu.VMEM)
SMEM = pl.BlockSpec(memory_space=pltpu.SMEM)
PARAMS = pltpu.CompilerParams(vmem_limit_bytes=60 * 1024 * 1024)
SMALL = pltpu.CompilerParams(vmem_limit_bytes=60 * 1024 * 1024)


def y_scratch(length, modes):
    count = length // RADIX
    near = length // 2 // modes
    wide = 2 * LANES
    turned = pltpu.VMEM((2, length, LANES), F32)
    halves = pltpu.VMEM((near, 2 * modes, wide), F32)
    sections = pltpu.VMEM((RADIX, 2 * count, wide), F32)
    return turned, halves, sections


def took(microseconds):
    return pl.CostEstimate(flops=int(microseconds * 1e9), bytes_accessed=1, transcendentals=0)


def struct(*shape):
    return jax.ShapeDtypeStruct(shape, F32)


def weight_tables(modes, wide, chunk):
    flip = np.zeros((2 * chunk, chunk), np.float32)
    flip[chunk - np.arange(1, chunk), np.arange(1, chunk)] = 1.0
    flip[chunk, 0] = 1.0
    swap = np.zeros((modes + 16, modes + 16), np.float32)
    swap[np.arange(1, modes), modes - np.arange(1, modes)] = 1.0
    swap[0, modes] = 1.0
    swap[modes, modes + 1] = 1.0
    return jnp.asarray(flip.astype(BF16)), jnp.asarray(swap.astype(BF16))


def with_kernels(slip_rate, slip_field, prestress, history, kernel, band_len, mode_band):
    comps, rows, length = slip_rate.shape
    modes, wide = mode_band.shape
    far = lax.axis_size(AXES)
    near = lax.axis_size(NEAR)
    bands, lags = kernel.shape[:2]
    depth = history.shape[0]
    flags, coded, block, few = exchange_bands(kernel, band_len, mode_band)
    row_back, row_mirror = reverse_first(history, mode_band)

    y_forward, y_inverse = (jnp.asarray(split_table(t)) for t in tables(length))
    x_forward, x_inverse = tables(wide)
    x_forward = jnp.asarray(split_table(x_forward[:, :, : wide // RADIX // 2]))
    x_inverse = jnp.asarray(split_table(x_inverse))

    turned, halves, sections = y_scratch(length, modes)
    sent = pl.pallas_call(
        y_forward_kernel,
        out_shape=struct(near, comps, rows, 2 * modes),
        in_specs=[SMEM, VMEM, VMEM],
        out_specs=VMEM,
        scratch_shapes=[turned, sections, halves],
        compiler_params=PARAMS,
        cost_estimate=took(6),
        name="y_forward",
    )(flags, slip_rate, y_forward)
    here = lax.all_to_all(sent, NEAR, 0, 0, tiled=True)

    chunk = 2 * LANES
    steps = wide // chunk
    past = pl.pallas_call(
        history_kernel,
        grid=(steps,),
        out_shape=struct(comps, wide, 2 * modes),
        in_specs=[
            SMEM,
            SMEM,
            pl.BlockSpec((modes, chunk), lambda g: (0, g)),
            pl.BlockSpec((1, chunk), lambda g: (0, g)),
            pl.BlockSpec((depth, comps, 2, modes, chunk), lambda g: (0, 0, 0, 0, g)),
            pl.BlockSpec((depth * comps * 2, chunk), lambda g: (0, g)),
        ],
        out_specs=pl.BlockSpec((comps, chunk, 2 * modes), lambda g: (0, g, 0)),
        scratch_shapes=[pltpu.VMEM((comps, 2 * modes, chunk), F32)],
        compiler_params=SMALL,
        cost_estimate=took(7),
        name="history",
    )(flags, coded, mode_band, row_mirror, history, row_back)

    flip, swap = weight_tables(modes, wide, chunk)

    def weights(table):
        own = lambda g: (0, g)
        back = lambda g: (0, steps - 1 - g)
        after = lambda g: (0, (steps - g) % steps)
        return pl.pallas_call(
            weight_kernel,
            grid=(steps,),
            out_shape=struct(comps, wide, 2 * modes),
            in_specs=[
                SMEM,
                SMEM,
                pl.BlockSpec((modes, chunk), own),
                pl.BlockSpec((16, chunk), own),
                pl.BlockSpec((modes, chunk), back),
                pl.BlockSpec((16, chunk), back),
                pl.BlockSpec((modes, chunk), after),
                pl.BlockSpec((16, chunk), after),
                pl.BlockSpec(flip.shape, lambda g: (0, 0)),
                pl.BlockSpec(swap.shape, lambda g: (0, 0)),
            ],
            out_specs=pl.BlockSpec((comps, chunk, 2 * modes), lambda g: (0, g, 0)),
            scratch_shapes=[pltpu.VMEM((2 * modes, chunk), F32)],
            compiler_params=SMALL,
            cost_estimate=took(40),
            name="weights",
        )(flags, table, mode_band, few, block, few, block, few, flip, swap)

    now_weight = weights(coded[:, :comps] + coded[:, comps : 2 * comps])
    later_weight = weights(coded[:, :comps])

    def x_stage(given, weight, added):
        whole = pl.BlockSpec((1, wide, 2 * modes), lambda c: (c, 0, 0))
        fixed = [pl.BlockSpec(t.shape, lambda c: (0, 0, 0)) for t in (x_forward, x_inverse)]
        operands = [given, x_forward, x_inverse, weight] + ([] if added is None else [added])
        count = wide // RADIX
        return pl.pallas_call(
            functools.partial(x_kernel, added is not None),
            grid=(comps,),
            out_shape=struct(far, comps, rows, 2 * modes),
            in_specs=[pl.BlockSpec((near, 1, rows, 2 * modes), lambda c: (0, c, 0, 0))]
            + fixed
            + [whole] * (len(operands) - 3),
            out_specs=pl.BlockSpec((far, 1, rows, 2 * modes), lambda c: (0, c, 0, 0)),
            scratch_shapes=[
                pltpu.VMEM((RADIX, 2 * count, LANES), F32),
                pltpu.VMEM((RADIX, count, LANES), F32),
            ],
            compiler_params=SMALL,
            cost_estimate=took(12),
            name="x_stage",
        )(*operands)

    back = lax.all_to_all(x_stage(here, now_weight, past), AXES, 0, 0, tiled=True)
    sent, stress = pl.pallas_call(
        y_middle_kernel,
        out_shape=[struct(near, comps, rows, 2 * modes), struct(comps, rows, length)],
        in_specs=[SMEM] + [VMEM] * 6,
        out_specs=[VMEM] * 2,
        scratch_shapes=[turned, halves, halves, sections, sections, halves],
        compiler_params=PARAMS,
        cost_estimate=took(14),
        name="y_middle",
    )(flags, prestress, slip_field, slip_rate, y_inverse, y_forward, back)
    here = lax.all_to_all(sent, NEAR, 0, 0, tiled=True)
    back = lax.all_to_all(x_stage(here, later_weight, None), AXES, 0, 0, tiled=True)
    return tuple(
        pl.pallas_call(
            y_final_kernel,
            out_shape=[struct(comps, rows, length)] * 2,
            in_specs=[VMEM] * 5,
            out_specs=[VMEM] * 2,
            scratch_shapes=[turned, halves, halves, sections],
            compiler_params=PARAMS,
            cost_estimate=took(10),
            name="y_final",
        )(stress, slip_field, slip_rate, y_inverse, back)
    )


def reverse_modes(values):
    return jnp.roll(jnp.flip(values, -1), 1, -1)


def exchange_bands(kernel, band_len, mode_band):
    bands, lags, comps = kernel.shape
    far = lax.axis_size(AXES)
    near = lax.axis_size(NEAR)
    me = lax.axis_index(AXES)
    first = me % near == 0
    flags = jnp.stack([jnp.where(me < near, 1.0, -1.0), jnp.where(first, 1.0, 0.0)]).astype(F32)
    live = (jnp.arange(lags, dtype=jnp.int32)[None, :] < band_len[:, None]).astype(F32)
    coded = (kernel * live[:, :, None]).reshape(bands, lags * comps)
    block = lax.ppermute(mode_band, AXES, [(d, far - 1 - d) for d in range(far)])
    edge = lax.ppermute(mode_band[:1], AXES, [(d, (far - d) % far) for d in range(far)])
    opposite = lax.ppermute(mode_band[:1], AXES, [(d, (d + near) % far) for d in range(far)])
    few = jnp.concatenate([edge, opposite, jnp.zeros((14, mode_band.shape[1]), jnp.int32)], axis=0)
    return flags, coded, block, few


def reverse_first(history, mode_band):
    row_back = reverse_modes(history[:, :, :, 0, :].astype(F32).reshape(-1, mode_band.shape[1]))
    return row_back, reverse_modes(mode_band[:1])


def plain(slip_rate, slip_field, prestress, history, kernel, band_len, mode_band):
    comps, rows, length = slip_rate.shape
    modes, wide = mode_band.shape
    far = lax.axis_size(AXES)
    near = lax.axis_size(NEAR)
    bands, lags = kernel.shape[:2]
    depth = history.shape[0]
    flags, coded, block, few = exchange_bands(kernel, band_len, mode_band)
    row_back, row_mirror = reverse_first(history, mode_band)
    mirror = reverse_modes(jnp.concatenate([few[:1], jnp.flip(block[1:], 0)], axis=0))
    extra = jnp.concatenate([few[1:2], reverse_modes(few[1:2])], axis=0)
    table = coded.reshape(bands, lags, comps)
    edge = flags[1] > 0.0
    top = (jnp.arange(modes) == 0)[None, :, None] & edge

    def dot(spec, a, b):
        return jnp.einsum(spec, a, b, precision=lax.Precision.HIGHEST)

    def angles(first, second, size):
        product = (first[:, None] * second[None, :]) % size
        angle = product.astype(F32) * (2.0 * math.pi / size)
        return jnp.cos(angle) / math.sqrt(size), jnp.sin(angle) / math.sqrt(size)

    def weights(band, values):
        result = jnp.zeros(values.shape[1:] + band.shape, F32)
        for b in range(bands):
            result = jnp.where(band == b, values[b][..., None, None], result)
        return result

    past = []
    for at in range(depth):
        w = weights(mode_band, table[:, lags - depth + at])[:, None]
        past.append(w * history[at].astype(F32))
    past = sum(past)
    back = row_back.reshape(depth, comps, 2, 1, wide)
    w = weights(row_mirror, table[:, lags - depth :])
    back = jnp.sum(w[:, :, None] * back, axis=0) * jnp.array([1.0, -1.0], F32)[:, None, None]
    past = jnp.where(top, 0.5 * (past + back), past)
    parity = jnp.where(jnp.arange(wide) % 2 == 1, flags[0], 1.0)

    def filters(values):
        whole = (weights(mode_band, values) + weights(mirror, values)) * parity
        other = (weights(extra[:1], values) + weights(extra[1:], values)) * parity
        return jnp.where(top, 0.5 * whole, whole), jnp.where(top, 0.5 * other, whole)

    own = jnp.arange(length, dtype=jnp.int32)
    y_cos, y_sin = angles(own, own[: length // 2], length)
    nyquist = jnp.where(own % 2 == 1, -1.0, 1.0).astype(F32) / math.sqrt(length)
    y_sin = y_sin.at[:, 0].set(-nyquist)
    across = jnp.arange(wide, dtype=jnp.int32)
    x_cos, x_sin = angles(across, across, wide)
    flip = jnp.where(own % 2 == 1, flags[0], 1.0)

    def y_forward(field):
        field = field * flip
        both = jnp.stack([dot("cxy,yk->ckx", field, y_cos), -dot("cxy,yk->ckx", field, y_sin)], 1)
        both = both.reshape(comps, 2, near, modes, rows).transpose(2, 0, 4, 1, 3)
        return lax.all_to_all(both, NEAR, 0, 0, tiled=True)

    def x_stage(given, filt, added):
        given = given.transpose(1, 3, 4, 0, 2).reshape(comps, 2, modes, near * rows)
        real = dot("cpkx,xm->cpkm", given, x_cos[: near * rows])
        imag = -dot("cpkx,xm->cpkm", given, x_sin[: near * rows])
        a, b = filt
        out_real = a * real[:, 0] - b * imag[:, 1]
        out_imag = a * imag[:, 0] + b * real[:, 1]
        if added is not None:
            out_real, out_imag = out_real + added[:, 0], out_imag + added[:, 1]
        first = dot("ckm,mx->ckx", out_real, x_cos) - dot("ckm,mx->ckx", out_imag, x_sin)
        second = dot("ckm,mx->ckx", out_real, x_sin) + dot("ckm,mx->ckx", out_imag, x_cos)
        both = jnp.stack([first, second], 1).reshape(comps, 2, modes, far, rows).transpose(3, 0, 4, 1, 2)
        return lax.all_to_all(both, AXES, 0, 0, tiled=True)

    def y_inverse(given):
        given = given.reshape(2, near, comps, rows, 2, modes).transpose(0, 4, 2, 3, 1, 5)
        given = given.reshape(2, 2, comps, rows, length // 2)
        half = dot("hcxk,yk->hcxy", given[:, 0], y_cos) - dot("hcxk,yk->hcxy", given[:, 1], y_sin)
        return half[0] + half[1] * jnp.where(own % 2 == 1, -1.0, 1.0)

    def phi(s):
        return jnp.stack(friction(s[0], s[1], s[2], slip_field[0], slip_field[1]))

    now = filters(table[:, 0] + table[:, 1])
    later = filters(table[:, 0])
    stress = prestress + y_inverse(x_stage(y_forward(slip_rate), now, past))
    shift = 0.5 * (phi(stress) - slip_rate)
    second = phi(stress + y_inverse(x_stage(y_forward(shift), later, None)))
    return second, slip_field + 0.25 * (slip_rate + second)


def solution(mesh):
    shape = mesh.devices.shape
    ours = Mesh(mesh.devices.reshape(2, shape[0] // 2, shape[1]), AXES)

    def on_device(slip_rate, slip_field, prestress, history, kernel, band_len, mode_band):
        args = (slip_rate, slip_field, prestress, history, kernel, band_len, mode_band)
        rows, modes = slip_rate.shape[1], mode_band.shape[0]
        if 2 * modes == LANES and 2 * rows == LANES:
            return with_kernels(*args)
        return plain(*args)

    rows = P(None, AXES, None)
    return jax.shard_map(
        on_device,
        mesh=ours,
        in_specs=(rows, rows, rows, P(None, None, None, AXES, None), P(), P(), P(AXES, None)),
        out_specs=(rows, rows),
        check_vma=False,
    )
```

```python
import functools
import math

import jax
import jax.numpy as jnp
import numpy as np
from jax import lax
from jax.experimental import pallas as pl
from jax.experimental.pallas import tpu as pltpu
from jax.sharding import Mesh, PartitionSpec as P


LANES = 128
RADIX = 8
SHORT = 4
AXES = ("half", "part", "ky")
NEAR = ("part", "ky")
F32 = jnp.float32
BF16 = jnp.bfloat16
ROOT = math.sqrt(0.5)

static_fric = 0.7
dynamic_fric = 0.35
weaken_slip = 0.5


def softplus(value):
    return jnp.maximum(value, 0.0) + jnp.log1p(jnp.exp(-jnp.abs(value)))


def friction(s0, s1, s2, u0, u1):
    worn = jnp.sqrt(u0 * u0 + u1 * u1 + 1.0) - 1.0
    coeff = dynamic_fric + (static_fric - dynamic_fric) * jnp.exp(worn * (-1.0 / weaken_slip))
    tail = jnp.log1p(jnp.exp(-jnp.abs(s2)))
    strength = coeff * (jnp.maximum(-s2, 0.0) + tail)
    magnitude = jnp.sqrt(s0 * s0 + s1 * s1 + 1.0)
    ratio = softplus(magnitude - strength) / magnitude
    return ratio * s0, ratio * s1, jnp.maximum(s2, 0.0) + tail


def split_table(values):
    high = values.astype(BF16)
    low = (values - high.astype(np.float64)).astype(BF16)
    return np.concatenate([high, low], axis=-1)


def tables(length):
    count = length // RADIX
    outer = np.arange(count)
    spots = RADIX * outer[None, :, None] + np.arange(RADIX)[:, None, None]
    angle = 2.0 * np.pi / length * ((spots * outer[None, None, :]) % length)
    cos = np.cos(angle) / math.sqrt(length)
    sin = np.sin(angle) / math.sqrt(length)
    forward = np.concatenate([cos.transpose(0, 2, 1), -sin.transpose(0, 2, 1)], axis=1)
    inverse = np.concatenate([cos, sin], axis=1)
    return forward, inverse


def dot3(table, values):
    depth = values.shape[0]
    high = values.astype(BF16)
    low = (values - high.astype(F32)).astype(BF16)
    left = jnp.concatenate([table, table[:, :depth]], axis=1)
    right = jnp.concatenate([high, high, low], axis=0)
    return jnp.dot(left, right, preferred_element_type=F32)


def c_add(a, b):
    return a[0] + b[0], a[1] + b[1]


def c_sub(a, b):
    return a[0] - b[0], a[1] - b[1]


def forward_eight(a, wanted):
    def four(p, q, r, s):
        t0, t1, t2 = c_add(p, r), c_sub(p, r), c_add(q, s)
        d = c_sub(q, s)
        t3 = (d[1], -d[0])
        return c_add(t0, t2), c_add(t1, t3), c_sub(t0, t2), c_sub(t1, t3)

    even = four(a[0], a[2], a[4], a[6])
    odd = four(a[1], a[3], a[5], a[7])
    o1 = ((odd[1][0] + odd[1][1]) * ROOT, (odd[1][1] - odd[1][0]) * ROOT)
    o2 = (odd[2][1], -odd[2][0])
    o3 = ((odd[3][1] - odd[3][0]) * ROOT, (odd[3][0] + odd[3][1]) * -ROOT)
    turned = (odd[0], o1, o2, o3)
    first = [c_add(even[k], turned[k]) for k in range(4)]
    if wanted <= 4:
        return first
    return first + [c_sub(even[k], turned[k]) for k in range(4)]


def forward_rows(turned, table, flag, sections, packed, out, ready):
    tiles, length, _ = turned.shape
    count = length // RADIX
    owners, comps, rows, _ = out.shape
    modes = packed.shape[1] // 2
    ready()
    for j in range(RADIX):
        piece = jnp.concatenate([turned[t, pl.ds(j, count, stride=RADIX), :] for t in range(tiles)], axis=1)
        if j % 2:
            piece = piece * flag
        sections[j] = dot3(table[j], piece)
    per = modes // 8

    def chunk(q, carry):
        at = q // per
        off = pl.multiple_of((q % per) * 8, 8)
        row = pl.multiple_of(q * 8, 8)
        parts = [(sections[j, pl.ds(row, 8), :], sections[j, pl.ds(row + count, 8), :]) for j in range(RADIX)]
        found = forward_eight(parts, 4)
        for k2 in range(RADIX // 2):
            owner = at + k2 * (count // modes)
            packed[owner, pl.ds(off, 8), :] = found[k2][0]
            packed[owner, pl.ds(off + modes, 8), :] = found[k2][1]
        return carry

    lax.fori_loop(0, count // 8, chunk, 0, unroll=8)
    top = sections[0, 0:1, :]
    for j in range(1, RADIX):
        top = top - sections[j, 0:1, :] if j % 2 else top + sections[j, 0:1, :]
    packed[0, modes : modes + 1, :] = top

    def send(owner, carry):
        for c in range(comps):
            if c % 2 == 0:
                block = packed[owner, :, pl.ds(c * rows, LANES)].T
            out[owner, c] = block[(c % 2) * rows : (c % 2) * rows + rows]
        return carry

    lax.fori_loop(0, owners, send, 0, unroll=4)


def inverse_rows(arrived, table, even, odd, mixed, turned, ready):
    owners, comps, rows, _ = arrived.shape
    near = owners // 2
    modes = even.shape[1] // 2
    tiles, length, _ = turned.shape
    count = length // RADIX

    def gather(owner, carry):
        sums, differences = [], []
        for c in range(comps):
            mine, other = arrived[owner, c], arrived[owner + near, c]
            sums.append(mine + other)
            differences.append(mine - other)
        blank = jnp.zeros((LANES * tiles - comps * rows, LANES), F32)
        for store, pieces in ((even, sums), (odd, differences)):
            whole = jnp.concatenate(pieces + [blank], axis=0)
            for t in range(tiles):
                store[owner, :, t * LANES : (t + 1) * LANES] = whole[t * LANES : (t + 1) * LANES].T
        return carry

    lax.fori_loop(0, near, gather, 0, unroll=4)
    per = modes // 8

    def chunk(q, carry):
        at = q // per
        off = pl.multiple_of((q % per) * 8, 8)
        row = pl.multiple_of(q * 8, 8)

        def four(s):
            t0, t1, t2 = c_add(s[0], s[2]), c_sub(s[0], s[2]), c_add(s[1], s[3])
            d = c_sub(s[1], s[3])
            t3 = (-d[1], d[0])
            return c_add(t0, t2), c_add(t1, t3), c_sub(t0, t2), c_sub(t1, t3)

        for first, store in ((0, even), (1, odd)):
            parts = []
            for k2 in range(RADIX // 2):
                owner = at + k2 * (count // modes)
                parts.append((store[owner, pl.ds(off, 8), :], store[owner, pl.ds(off + modes, 8), :]))
            if first:
                p1, p2, p3 = parts[1:]
                parts[1] = ((p1[0] - p1[1]) * ROOT, (p1[0] + p1[1]) * ROOT)
                parts[2] = (-p2[1], p2[0])
                parts[3] = ((p3[0] + p3[1]) * -ROOT, (p3[0] - p3[1]) * ROOT)
            for index, value in enumerate(four(parts)):
                mixed[2 * index + first, pl.ds(row, 8), :] = value[0]
                mixed[2 * index + first, pl.ds(row + count, 8), :] = value[1]
        return carry

    lax.fori_loop(0, count // 8, chunk, 0, unroll=8)
    scale = 1.0 / math.sqrt(length)
    ready()
    for j in range(RADIX):
        piece = dot3(table[j, :count], mixed[j, :count, :]) - dot3(table[j, count:], mixed[j, count:, :])
        if j % 2:
            piece = piece - odd[0, modes : modes + 1, :] * scale
        else:
            piece = piece + even[0, modes : modes + 1, :] * scale
        for t in range(tiles):
            turned[t, pl.ds(j, count, stride=RADIX), :] = piece[:, t * LANES : (t + 1) * LANES]


def turn_in(parts, turned, start):
    tiles = turned.shape[0]
    used = sum(part.shape[0] for part in parts)
    blank = jnp.zeros((LANES * tiles - used, LANES), F32)
    whole = jnp.concatenate(list(parts) + [blank], axis=0)
    for t in range(tiles):
        turned[t, pl.ds(start, LANES), :] = whole[t * LANES : (t + 1) * LANES].T


def turn_out(turned, start, rows, comps):
    tiles = turned.shape[0]
    whole = jnp.concatenate([turned[t, pl.ds(start, LANES), :].T for t in range(tiles)], axis=0)
    return [whole[c * rows : (c + 1) * rows] for c in range(comps)]


def fetch(sems, *pairs):
    copies = [pltpu.make_async_copy(source, target, sems.at[k]) for k, (source, target) in enumerate(pairs)]
    for copy in copies:
        copy.start()
    return copies


def y_forward_kernel(flags, field, table_far, out, turned, sections, packed, table, sems):
    comps, _, length = field.shape
    (got_table,) = fetch(sems, (table_far, table))

    def load(q, carry):
        start = pl.multiple_of(q * LANES, LANES)
        turn_in([field[c, :, pl.ds(start, LANES)] for c in range(comps)], turned, start)
        return carry

    lax.fori_loop(0, length // LANES, load, 0, unroll=4)
    forward_rows(turned, table, flags[0], sections, packed, out, got_table.wait)


def y_middle_kernel(flags, prestress_far, slip_far, rate_far, inverse_far, forward_far, arrived, out, stress_far, *rest):
    turned, even, odd, mixed, sections, packed, inverse, forward, prestress, slip, rate, stress, sems = rest
    comps, rows, length = prestress.shape
    slip_used = slip_far.at[: slip.shape[0]]
    got_inverse, got_prestress, got_slip, got_rate, got_forward = fetch(
        sems,
        (inverse_far, inverse),
        (prestress_far, prestress),
        (slip_used, slip),
        (rate_far, rate),
        (forward_far, forward),
    )
    inverse_rows(arrived, inverse, even, odd, mixed, turned, got_inverse.wait)
    got_prestress.wait()
    got_slip.wait()
    got_rate.wait()

    def step(q, carry):
        start = pl.multiple_of(q * LANES, LANES)
        lanes = pl.ds(start, LANES)
        parts = turn_out(turned, start, rows, comps)
        s = [prestress[c, :, lanes] + parts[c] for c in range(comps)]
        for c in range(comps):
            stress[c, :, lanes] = s[c]
        first = friction(*s, slip[0, :, lanes], slip[1, :, lanes])
        turn_in([(first[c] - rate[c, :, lanes]) * 0.5 for c in range(comps)], turned, start)
        return carry

    lax.fori_loop(0, length // LANES, step, 0, unroll=2)
    give_stress = pltpu.make_async_copy(stress, stress_far, sems.at[5])
    give_stress.start()
    forward_rows(turned, forward, flags[0], sections, packed, out, got_forward.wait)
    give_stress.wait()


def y_final_kernel(stress_far, slip_far, rate_far, inverse_far, arrived, new_rate, new_slip, *rest):
    turned, even, odd, mixed, inverse, stress, slip, rate, sems = rest
    comps, rows, length = stress.shape
    got_inverse, *got = fetch(sems, (inverse_far, inverse), (stress_far, stress), (slip_far, slip), (rate_far, rate))
    inverse_rows(arrived, inverse, even, odd, mixed, turned, got_inverse.wait)
    for copy in got:
        copy.wait()

    def step(q, carry):
        start = pl.multiple_of(q * LANES, LANES)
        lanes = pl.ds(start, LANES)
        parts = turn_out(turned, start, rows, comps)
        s = [stress[c, :, lanes] + parts[c] for c in range(comps)]
        second = friction(*s, slip[0, :, lanes], slip[1, :, lanes])
        for c in range(comps):
            new_rate[c, :, lanes] = second[c]
            new_slip[c, :, lanes] = slip[c, :, lanes] + 0.25 * (rate[c, :, lanes] + second[c])
        return carry

    lax.fori_loop(0, length // LANES, step, 0, unroll=2)


def x_kernel(has_past, arrived, forward_far, inverse_far, weight, *rest):
    if has_past:
        past, out, sections, mixed, forward, inverse, sems = rest
    else:
        out, sections, mixed, forward, inverse, sems = rest
    got_forward = pltpu.make_async_copy(forward_far, forward, sems.at[0])
    got_inverse = pltpu.make_async_copy(inverse_far, inverse, sems.at[1])

    @pl.when(pl.program_id(0) == 0)
    def _():
        got_forward.start()
        got_inverse.start()
        got_forward.wait()

    near, _, rows, _ = arrived.shape
    far = out.shape[0]
    count = inverse.shape[2] // 2
    for j in range(RADIX):
        piece = jnp.concatenate(
            [arrived[src, 0, pl.ds(j, rows // RADIX, stride=RADIX), :] for src in range(near)], axis=0
        )
        sections[j] = dot3(forward[j], piece)
    sign = jnp.where(lax.broadcasted_iota(jnp.int32, (8, LANES), 1) < LANES // 2, -1.0, 1.0).astype(F32)

    def turn(value):
        return sign * pltpu.roll(value, LANES // 2, 1)

    def chunk(q, carry):
        row = pl.multiple_of(q * 8, 8)
        parts = [(sections[j, pl.ds(row, 8), :], sections[j, pl.ds(row + count, 8), :]) for j in range(RADIX)]
        outs = forward_eight(parts, RADIX)
        z = []
        for k2 in range(RADIX):
            spot = pl.ds(row + k2 * count, 8)
            w = weight[0, spot, :]
            value = w * outs[k2][0] + turn(w * outs[k2][1])
            if has_past:
                value = value + past[0, spot, :]
            z.append(value)

        def four(a, b, c, d):
            t0, t1, t2, t3 = a + c, a - c, b + d, turn(b - d)
            return t0 + t2, t1 + t3, t0 - t2, t1 - t3

        e = four(z[0], z[2], z[4], z[6])
        o = four(z[1], z[3], z[5], z[7])
        o1 = (o[1] + turn(o[1])) * ROOT
        o3 = (turn(o[3]) - o[3]) * ROOT
        turned = (o[0], o1, turn(o[2]), o3)
        for k in range(4):
            mixed[k, pl.ds(row, 8), :] = e[k] + turned[k]
            mixed[k + 4, pl.ds(row, 8), :] = e[k] - turned[k]
        return carry

    lax.fori_loop(0, count // 8, chunk, 0, unroll=8)

    @pl.when(pl.program_id(0) == 0)
    def _():
        got_inverse.wait()

    lanes = lax.broadcasted_iota(jnp.int32, (count, LANES), 1)
    wide = jnp.where(lanes < LANES // 2, -1.0, 1.0).astype(F32)
    step = rows // RADIX
    for j in range(RADIX):
        both = dot3(inverse[j], mixed[j])
        value = both[:count] + wide * pltpu.roll(both[count:], LANES // 2, 1)
        for dest in range(far):
            out[dest, 0, pl.ds(j, step, stride=RADIX), :] = value[dest * step : (dest + 1) * step]


def pick(values, bits):
    level = 0
    while len(values) > 1:
        if len(values) % 2:
            values = values + [values[-1]]
        values = [jnp.where(bits[level], values[k + 1], values[k]) for k in range(0, len(values), 2)]
        level += 1
    return values[0]


def bits_of(band, bands):
    return [(band & (1 << level)) != 0 for level in range(max((bands - 1).bit_length(), 1))]


def weights_past(table, band, bits, c, depth):
    bands, lags, comps = table.shape[0], table.shape[1] // 3, 3
    found = []
    for at in range(depth):
        spot = (lags - depth + at) * comps + c
        if lags - depth + at < SHORT:
            found.append(pick([table[b, spot] for b in range(bands)], bits))
        else:
            found.append(jnp.where(band == 0, table[0, spot], 0.0))
    return found


def history_kernel(flags, table, band, band_back, band_edge, history, past_back, past_edge, flip, past, stacked):
    bands, comps = table.shape[0], 3
    depth = history.shape[0]
    rows, width = band.shape

    def group(q, carry):
        spot = pl.ds(pl.multiple_of(q * 16, 16), 16)
        own = band[spot, :]
        bits = bits_of(own, bands)
        for c in range(comps):
            sums = [jnp.zeros((16, width), F32) for _ in range(2)]
            for at, w in enumerate(weights_past(table, own, bits, c, depth)):
                for p in range(2):
                    sums[p] = sums[p] + w * history[at, c, p, spot, :].astype(F32)
            for p in range(2):
                stacked[c, pl.ds(pl.multiple_of(q * 16 + p * rows, 16), 16), :] = sums[p]
        return carry

    lax.fori_loop(0, rows // 16, group, 0)

    edge = flags[1] > 0.0
    there, beyond = [], []
    for at in range(depth):
        for c in range(comps):
            for p in range(2):
                there.append(past_back[at, c, p].astype(F32)[:1])
                beyond.append(past_edge[at, c, p].astype(F32)[:1])
    count = len(there)
    blank = -(count + 1) % 16
    there += [band_back[...].astype(F32)[:1], jnp.zeros((blank, width), F32)]
    beyond += [band_edge[...].astype(F32)[:1], jnp.zeros((blank, LANES), F32)]
    both = [jnp.concatenate(rows_of, axis=0).astype(BF16) for rows_of in (there, beyond)]
    row_back = jnp.dot(jnp.concatenate(both, axis=1), flip[...], preferred_element_type=F32)
    back = row_back[count : count + 1].astype(jnp.int32)
    bits = bits_of(back, bands)
    for c in range(comps):
        found = weights_past(table, back, bits, c, depth)
        for p in range(2):
            reverse = jnp.zeros((1, width), F32)
            for at, w in enumerate(found):
                spot = (at * comps + c) * 2 + p
                reverse = reverse + w * row_back[spot : spot + 1, :]
            if p:
                reverse = -reverse
            mine = stacked[c, p * rows : p * rows + 1, :]
            stacked[c, p * rows : p * rows + 1, :] = jnp.where(edge, 0.5 * (mine + reverse), mine)
        for t in range(width // LANES):
            spot = pl.ds(t * LANES, LANES)
            past[c, spot, :] = stacked[c, :, spot].T


def weight_kernel(flags, table, band, few, block, few_back, block_edge, few_edge, flip, swap, out, stacked):
    bands, comps = table.shape
    rows, width = band.shape
    odd = (lax.broadcasted_iota(jnp.int32, (1, width), 1) & 1) == 1
    parity = jnp.where(odd, flags[0], 1.0).astype(F32)
    edge = flags[1] > 0.0

    def exact(values):
        return values.astype(F32).astype(BF16)

    there = jnp.concatenate([exact(block[...]), exact(few_back[...])], axis=0)
    beyond = jnp.concatenate([exact(block_edge[...]), exact(few_edge[...])], axis=0)
    turned = jnp.dot(jnp.concatenate([there, beyond], axis=1), flip[...], preferred_element_type=F32)
    turned = jnp.dot(swap[...], turned.astype(BF16), preferred_element_type=F32).astype(jnp.int32)
    for c in range(comps):
        values = [table[b, c] for b in range(bands)]
        for q in range(rows // 8):
            spot = slice(q * 8, q * 8 + 8)
            value = pick(values, bits_of(band[spot, :], bands)) + pick(values, bits_of(turned[spot], bands))
            value = value * parity
            if q == 0:
                first = lax.broadcasted_iota(jnp.int32, (8, width), 0) == 0
                other = pick(values, bits_of(few[1:2, :], bands))
                other = other + pick(values, bits_of(turned[rows : rows + 1], bands))
                other = jnp.where(edge, 0.5 * (other * parity), value[:1])
                value = jnp.where(first & edge, 0.5 * value, value)
                stacked[rows : rows + 8, :] = jnp.where(first, other, value)
            else:
                stacked[rows + q * 8 : rows + q * 8 + 8, :] = value
            stacked[spot, :] = value
        for t in range(width // LANES):
            spot = slice(t * LANES, (t + 1) * LANES)
            out[c, spot, :] = stacked[:, spot].T


VMEM = pl.BlockSpec(memory_space=pltpu.VMEM)
SMEM = pl.BlockSpec(memory_space=pltpu.SMEM)
ANY = pl.BlockSpec(memory_space=pl.ANY)
PARAMS = pltpu.CompilerParams(vmem_limit_bytes=60 * 1024 * 1024)
SMALL = pltpu.CompilerParams(vmem_limit_bytes=60 * 1024 * 1024)


def y_scratch(length, modes):
    count = length // RADIX
    near = length // 2 // modes
    wide = 2 * LANES
    turned = pltpu.VMEM((2, length, LANES), F32)
    halves = pltpu.VMEM((near, 2 * modes, wide), F32)
    sections = pltpu.VMEM((RADIX, 2 * count, wide), F32)
    return turned, halves, sections


def took(microseconds):
    return pl.CostEstimate(flops=int(microseconds * 1e9), bytes_accessed=1, transcendentals=0)


def struct(*shape):
    return jax.ShapeDtypeStruct(shape, F32)


def weight_tables(modes, wide, chunk):
    flip = np.zeros((chunk + LANES, chunk), np.float32)
    flip[chunk - np.arange(1, chunk), np.arange(1, chunk)] = 1.0
    flip[chunk, 0] = 1.0
    swap = np.zeros((modes + 16, modes + 16), np.float32)
    swap[np.arange(1, modes), modes - np.arange(1, modes)] = 1.0
    swap[0, modes] = 1.0
    swap[modes, modes + 1] = 1.0
    return jnp.asarray(flip.astype(BF16)), jnp.asarray(swap.astype(BF16))


def with_kernels(slip_rate, slip_field, prestress, history, kernel, band_len, mode_band):
    comps, rows, length = slip_rate.shape
    modes, wide = mode_band.shape
    far = lax.axis_size(AXES)
    near = lax.axis_size(NEAR)
    bands, lags = kernel.shape[:2]
    depth = history.shape[0]
    flags, coded, block, few = exchange_bands(kernel, band_len, mode_band)

    y_forward, y_inverse = (jnp.asarray(split_table(t)) for t in tables(length))
    x_forward, x_inverse = tables(wide)
    x_forward = jnp.asarray(split_table(x_forward[:, :, : wide // RADIX // 2]))
    x_inverse = jnp.asarray(split_table(x_inverse))

    turned, halves, sections = y_scratch(length, modes)
    y_table = pltpu.VMEM(y_forward.shape, BF16)
    field = pltpu.VMEM((comps, rows, length), F32)
    sent = pl.pallas_call(
        y_forward_kernel,
        out_shape=struct(near, comps, rows, 2 * modes),
        in_specs=[SMEM, VMEM, ANY],
        out_specs=VMEM,
        scratch_shapes=[turned, sections, halves, y_table, pltpu.SemaphoreType.DMA((1,))],
        compiler_params=PARAMS,
        cost_estimate=took(6),
        name="y_forward",
    )(flags, slip_rate, y_forward)
    here = lax.all_to_all(sent, NEAR, 0, 0, tiled=True)

    chunk = 4 * LANES
    steps = wide // chunk
    back = lambda g: steps - 1 - g
    after = lambda g: (steps - g) % steps * (chunk // LANES)
    flip, swap = weight_tables(modes, wide, chunk)
    flip_spec = pl.BlockSpec(flip.shape, lambda g: (0, 0))
    past = pl.pallas_call(
        history_kernel,
        grid=(steps,),
        out_shape=struct(comps, wide, 2 * modes),
        in_specs=[
            SMEM,
            SMEM,
            pl.BlockSpec((modes, chunk), lambda g: (0, g)),
            pl.BlockSpec((8, chunk), lambda g: (0, back(g))),
            pl.BlockSpec((8, LANES), lambda g: (0, after(g))),
            pl.BlockSpec((depth, comps, 2, modes, chunk), lambda g: (0, 0, 0, 0, g)),
            pl.BlockSpec((depth, comps, 2, 16, chunk), lambda g: (0, 0, 0, 0, back(g))),
            pl.BlockSpec((depth, comps, 2, 16, LANES), lambda g: (0, 0, 0, 0, after(g))),
            flip_spec,
        ],
        out_specs=pl.BlockSpec((comps, chunk, 2 * modes), lambda g: (0, g, 0)),
        scratch_shapes=[pltpu.VMEM((comps, 2 * modes, chunk), F32)],
        compiler_params=SMALL,
        cost_estimate=took(7),
        name="history",
    )(flags, coded, mode_band, mode_band, mode_band, history, history, history, flip)

    def weights(table):
        own = lambda g: (0, g)
        return pl.pallas_call(
            weight_kernel,
            grid=(steps,),
            out_shape=struct(comps, wide, 2 * modes),
            in_specs=[
                SMEM,
                SMEM,
                pl.BlockSpec((modes, chunk), own),
                pl.BlockSpec((16, chunk), own),
                pl.BlockSpec((modes, chunk), lambda g: (0, back(g))),
                pl.BlockSpec((16, chunk), lambda g: (0, back(g))),
                pl.BlockSpec((modes, LANES), lambda g: (0, after(g))),
                pl.BlockSpec((16, LANES), lambda g: (0, after(g))),
                flip_spec,
                pl.BlockSpec(swap.shape, lambda g: (0, 0)),
            ],
            out_specs=pl.BlockSpec((comps, chunk, 2 * modes), lambda g: (0, g, 0)),
            scratch_shapes=[pltpu.VMEM((2 * modes, chunk), F32)],
            compiler_params=SMALL,
            cost_estimate=took(40),
            name="weights",
        )(flags, table, mode_band, few, block, few, block, few, flip, swap)

    now_weight = weights(coded[:, :comps] + coded[:, comps : 2 * comps])
    later_weight = weights(coded[:, :comps])

    def x_stage(given, weight, added):
        whole = pl.BlockSpec((1, wide, 2 * modes), lambda c: (c, 0, 0))
        operands = [given, x_forward, x_inverse, weight] + ([] if added is None else [added])
        count = wide // RADIX
        return pl.pallas_call(
            functools.partial(x_kernel, added is not None),
            grid=(comps,),
            out_shape=struct(far, comps, rows, 2 * modes),
            in_specs=[pl.BlockSpec((near, 1, rows, 2 * modes), lambda c: (0, c, 0, 0)), ANY, ANY]
            + [whole] * (len(operands) - 3),
            out_specs=pl.BlockSpec((far, 1, rows, 2 * modes), lambda c: (0, c, 0, 0)),
            scratch_shapes=[
                pltpu.VMEM((RADIX, 2 * count, LANES), F32),
                pltpu.VMEM((RADIX, count, LANES), F32),
                pltpu.VMEM(x_forward.shape, BF16),
                pltpu.VMEM(x_inverse.shape, BF16),
                pltpu.SemaphoreType.DMA((2,)),
            ],
            compiler_params=SMALL,
            cost_estimate=took(12),
            name="x_stage",
        )(*operands)

    fields = lax.all_to_all(x_stage(here, now_weight, past), AXES, 0, 0, tiled=True)
    sent, stress = pl.pallas_call(
        y_middle_kernel,
        out_shape=[struct(near, comps, rows, 2 * modes), struct(comps, rows, length)],
        in_specs=[SMEM] + [ANY] * 5 + [VMEM],
        out_specs=[VMEM, ANY],
        scratch_shapes=[turned, halves, halves, sections, sections, halves, y_table, y_table]
        + [field, pltpu.VMEM((2, rows, length), F32), field, field, pltpu.SemaphoreType.DMA((6,))],
        compiler_params=PARAMS,
        cost_estimate=took(14),
        name="y_middle",
    )(flags, prestress, slip_field, slip_rate, y_inverse, y_forward, fields)
    here = lax.all_to_all(sent, NEAR, 0, 0, tiled=True)
    fields = lax.all_to_all(x_stage(here, later_weight, None), AXES, 0, 0, tiled=True)
    return tuple(
        pl.pallas_call(
            y_final_kernel,
            out_shape=[struct(comps, rows, length)] * 2,
            in_specs=[ANY] * 4 + [VMEM],
            out_specs=[VMEM] * 2,
            scratch_shapes=[turned, halves, halves, sections, y_table, field, field, field]
            + [pltpu.SemaphoreType.DMA((4,))],
            compiler_params=PARAMS,
            cost_estimate=took(10),
            name="y_final",
        )(stress, slip_field, slip_rate, y_inverse, fields)
    )


def reverse_modes(values):
    return jnp.roll(jnp.flip(values, -1), 1, -1)


def exchange_bands(kernel, band_len, mode_band):
    bands, lags, comps = kernel.shape
    far = lax.axis_size(AXES)
    near = lax.axis_size(NEAR)
    me = lax.axis_index(AXES)
    first = me % near == 0
    flags = jnp.stack([jnp.where(me < near, 1.0, -1.0), jnp.where(first, 1.0, 0.0)]).astype(F32)
    live = (jnp.arange(lags, dtype=jnp.int32)[None, :] < band_len[:, None]).astype(F32)
    coded = (kernel * live[:, :, None]).reshape(bands, lags * comps)
    block = lax.ppermute(mode_band, AXES, [(d, far - 1 - d) for d in range(far)])
    pairs = [(d, (d + near) % far if d % near == 0 else far - d) for d in range(far)]
    row = lax.ppermute(mode_band[:1], AXES, pairs)
    edge = jnp.where(first, mode_band[:1], row)
    few = jnp.concatenate([edge, row, jnp.zeros((14, mode_band.shape[1]), jnp.int32)], axis=0)
    return flags, coded, block, few


def reverse_first(history, mode_band):
    row_back = reverse_modes(history[:, :, :, 0, :].astype(F32).reshape(-1, mode_band.shape[1]))
    return row_back, reverse_modes(mode_band[:1])


def plain(slip_rate, slip_field, prestress, history, kernel, band_len, mode_band):
    comps, rows, length = slip_rate.shape
    modes, wide = mode_band.shape
    far = lax.axis_size(AXES)
    near = lax.axis_size(NEAR)
    bands, lags = kernel.shape[:2]
    depth = history.shape[0]
    flags, coded, block, few = exchange_bands(kernel, band_len, mode_band)
    row_back, row_mirror = reverse_first(history, mode_band)
    mirror = reverse_modes(jnp.concatenate([few[:1], jnp.flip(block[1:], 0)], axis=0))
    extra = jnp.concatenate([few[1:2], reverse_modes(few[1:2])], axis=0)
    table = coded.reshape(bands, lags, comps)
    edge = flags[1] > 0.0
    top = (jnp.arange(modes) == 0)[None, :, None] & edge

    def dot(spec, a, b):
        return jnp.einsum(spec, a, b, precision=lax.Precision.HIGHEST)

    def angles(first, second, size):
        product = (first[:, None] * second[None, :]) % size
        angle = product.astype(F32) * (2.0 * math.pi / size)
        return jnp.cos(angle) / math.sqrt(size), jnp.sin(angle) / math.sqrt(size)

    def weights(band, values):
        result = jnp.zeros(values.shape[1:] + band.shape, F32)
        for b in range(bands):
            result = jnp.where(band == b, values[b][..., None, None], result)
        return result

    past = []
    for at in range(depth):
        w = weights(mode_band, table[:, lags - depth + at])[:, None]
        past.append(w * history[at].astype(F32))
    past = sum(past)
    back = row_back.reshape(depth, comps, 2, 1, wide)
    w = weights(row_mirror, table[:, lags - depth :])
    back = jnp.sum(w[:, :, None] * back, axis=0) * jnp.array([1.0, -1.0], F32)[:, None, None]
    past = jnp.where(top, 0.5 * (past + back), past)
    parity = jnp.where(jnp.arange(wide) % 2 == 1, flags[0], 1.0)

    def filters(values):
        whole = (weights(mode_band, values) + weights(mirror, values)) * parity
        other = (weights(extra[:1], values) + weights(extra[1:], values)) * parity
        return jnp.where(top, 0.5 * whole, whole), jnp.where(top, 0.5 * other, whole)

    own = jnp.arange(length, dtype=jnp.int32)
    y_cos, y_sin = angles(own, own[: length // 2], length)
    nyquist = jnp.where(own % 2 == 1, -1.0, 1.0).astype(F32) / math.sqrt(length)
    y_sin = y_sin.at[:, 0].set(-nyquist)
    across = jnp.arange(wide, dtype=jnp.int32)
    x_cos, x_sin = angles(across, across, wide)
    flip = jnp.where(own % 2 == 1, flags[0], 1.0)

    def y_forward(field):
        field = field * flip
        both = jnp.stack([dot("cxy,yk->ckx", field, y_cos), -dot("cxy,yk->ckx", field, y_sin)], 1)
        both = both.reshape(comps, 2, near, modes, rows).transpose(2, 0, 4, 1, 3)
        return lax.all_to_all(both, NEAR, 0, 0, tiled=True)

    def x_stage(given, filt, added):
        given = given.transpose(1, 3, 4, 0, 2).reshape(comps, 2, modes, near * rows)
        real = dot("cpkx,xm->cpkm", given, x_cos[: near * rows])
        imag = -dot("cpkx,xm->cpkm", given, x_sin[: near * rows])
        a, b = filt
        out_real = a * real[:, 0] - b * imag[:, 1]
        out_imag = a * imag[:, 0] + b * real[:, 1]
        if added is not None:
            out_real, out_imag = out_real + added[:, 0], out_imag + added[:, 1]
        first = dot("ckm,mx->ckx", out_real, x_cos) - dot("ckm,mx->ckx", out_imag, x_sin)
        second = dot("ckm,mx->ckx", out_real, x_sin) + dot("ckm,mx->ckx", out_imag, x_cos)
        both = jnp.stack([first, second], 1).reshape(comps, 2, modes, far, rows).transpose(3, 0, 4, 1, 2)
        return lax.all_to_all(both, AXES, 0, 0, tiled=True)

    def y_inverse(given):
        given = given.reshape(2, near, comps, rows, 2, modes).transpose(0, 4, 2, 3, 1, 5)
        given = given.reshape(2, 2, comps, rows, length // 2)
        half = dot("hcxk,yk->hcxy", given[:, 0], y_cos) - dot("hcxk,yk->hcxy", given[:, 1], y_sin)
        return half[0] + half[1] * jnp.where(own % 2 == 1, -1.0, 1.0)

    def phi(s):
        return jnp.stack(friction(s[0], s[1], s[2], slip_field[0], slip_field[1]))

    now = filters(table[:, 0] + table[:, 1])
    later = filters(table[:, 0])
    stress = prestress + y_inverse(x_stage(y_forward(slip_rate), now, past))
    shift = 0.5 * (phi(stress) - slip_rate)
    second = phi(stress + y_inverse(x_stage(y_forward(shift), later, None)))
    return second, slip_field + 0.25 * (slip_rate + second)


def solution(mesh):
    shape = mesh.devices.shape
    ours = Mesh(mesh.devices.reshape(2, shape[0] // 2, shape[1]), AXES)

    def on_device(slip_rate, slip_field, prestress, history, kernel, band_len, mode_band):
        args = (slip_rate, slip_field, prestress, history, kernel, band_len, mode_band)
        rows, modes = slip_rate.shape[1], mode_band.shape[0]
        if 2 * modes == LANES and 2 * rows == LANES:
            return with_kernels(*args)
        return plain(*args)

    rows = P(None, AXES, None)
    return jax.shard_map(
        on_device,
        mesh=ours,
        in_specs=(rows, rows, rows, P(None, None, None, AXES, None), P(), P(), P(AXES, None)),
        out_specs=(rows, rows),
        check_vma=False,
    )
```

```python
import functools
import math

import jax
import jax.numpy as jnp
import numpy as np
from jax import lax
from jax.experimental import pallas as pl
from jax.experimental.pallas import tpu as pltpu
from jax.sharding import Mesh, PartitionSpec as P


LANES = 128
RADIX = 8
SHORT = 4
AXES = ("half", "part", "ky")
NEAR = ("part", "ky")
F32 = jnp.float32
BF16 = jnp.bfloat16
ROOT = math.sqrt(0.5)

static_fric = 0.7
dynamic_fric = 0.35
weaken_slip = 0.5


def softplus(value):
    return jnp.maximum(value, 0.0) + jnp.log1p(jnp.exp(-jnp.abs(value)))


def friction(s0, s1, s2, u0, u1):
    worn = jnp.sqrt(u0 * u0 + u1 * u1 + 1.0) - 1.0
    coeff = dynamic_fric + (static_fric - dynamic_fric) * jnp.exp(worn * (-1.0 / weaken_slip))
    tail = jnp.log1p(jnp.exp(-jnp.abs(s2)))
    strength = coeff * (jnp.maximum(-s2, 0.0) + tail)
    magnitude = jnp.sqrt(s0 * s0 + s1 * s1 + 1.0)
    ratio = softplus(magnitude - strength) / magnitude
    return ratio * s0, ratio * s1, jnp.maximum(s2, 0.0) + tail


def split_table(values):
    high = values.astype(BF16)
    low = (values - high.astype(np.float64)).astype(BF16)
    return np.concatenate([high, low], axis=-1)


def tables(length):
    count = length // RADIX
    outer = np.arange(count)
    spots = RADIX * outer[None, :, None] + np.arange(RADIX)[:, None, None]
    angle = 2.0 * np.pi / length * ((spots * outer[None, None, :]) % length)
    cos = np.cos(angle) / math.sqrt(length)
    sin = np.sin(angle) / math.sqrt(length)
    forward = np.concatenate([cos.transpose(0, 2, 1), -sin.transpose(0, 2, 1)], axis=1)
    inverse = np.concatenate([cos, sin], axis=1)
    return forward, inverse


def dot3(table, values):
    depth = values.shape[0]
    high = values.astype(BF16)
    low = (values - high.astype(F32)).astype(BF16)
    left = jnp.concatenate([table, table[:, :depth]], axis=1)
    right = jnp.concatenate([high, high, low], axis=0)
    return jnp.dot(left, right, preferred_element_type=F32)


def c_add(a, b):
    return a[0] + b[0], a[1] + b[1]


def c_sub(a, b):
    return a[0] - b[0], a[1] - b[1]


def forward_eight(a, wanted):
    def four(p, q, r, s):
        t0, t1, t2 = c_add(p, r), c_sub(p, r), c_add(q, s)
        d = c_sub(q, s)
        t3 = (d[1], -d[0])
        return c_add(t0, t2), c_add(t1, t3), c_sub(t0, t2), c_sub(t1, t3)

    even = four(a[0], a[2], a[4], a[6])
    odd = four(a[1], a[3], a[5], a[7])
    o1 = ((odd[1][0] + odd[1][1]) * ROOT, (odd[1][1] - odd[1][0]) * ROOT)
    o2 = (odd[2][1], -odd[2][0])
    o3 = ((odd[3][1] - odd[3][0]) * ROOT, (odd[3][0] + odd[3][1]) * -ROOT)
    turned = (odd[0], o1, o2, o3)
    first = [c_add(even[k], turned[k]) for k in range(4)]
    if wanted <= 4:
        return first
    return first + [c_sub(even[k], turned[k]) for k in range(4)]


def low_half():
    return lax.broadcasted_iota(jnp.int32, (1, LANES), 1) % (LANES // 2) < LANES // 4


def join(a, b):
    return jnp.where(low_half(), a, pltpu.roll(b, LANES // 4, 1))


def join_second(a, b):
    return jnp.where(low_half(), pltpu.roll(a, LANES - LANES // 4, 1), b)


def blocks_of(packed, owner, comps, rows):
    whole = [packed[owner, :, t * LANES : (t + 1) * LANES].T for t in range(packed.shape[2] // LANES)]
    whole = jnp.concatenate(whole, axis=0)
    return [whole[c * rows : (c + 1) * rows] for c in range(comps)]


def deliver_near(packed, owner, out):
    _, comps, rows, _ = out.shape
    for c, block in enumerate(blocks_of(packed, owner, comps, rows)):
        out[owner, c] = block


def deliver_far(rows, packed, owner, out):
    far = out.shape[0]
    comps = 2 * out.shape[1] // rows
    for c, block in enumerate(blocks_of(packed, owner, comps, rows)):
        top, bottom = block[: rows // 2], block[rows // 2 :]
        for device, value in ((owner, join(top, bottom)), (far - 1 - owner, join_second(top, bottom))):
            for m in range(rows // 16):
                out[device, (m * comps + c) * 8 : (m * comps + c) * 8 + 8] = value[m * 8 : m * 8 + 8]


def forward_rows(turned, table, flag, sections, packed, out, ready, deliver):
    tiles, length, _ = turned.shape
    count = length // RADIX
    owners = packed.shape[0]
    modes = packed.shape[1] // 2
    ready()
    for j in range(RADIX):
        piece = jnp.concatenate([turned[t, pl.ds(j, count, stride=RADIX), :] for t in range(tiles)], axis=1)
        if flag is not None and j % 2:
            piece = piece * flag
        sections[j] = dot3(table[j], piece)
    per = modes // 8

    def chunk(q, carry):
        at = q // per
        off = pl.multiple_of((q % per) * 8, 8)
        row = pl.multiple_of(q * 8, 8)
        parts = [(sections[j, pl.ds(row, 8), :], sections[j, pl.ds(row + count, 8), :]) for j in range(RADIX)]
        found = forward_eight(parts, 4)
        for k2 in range(RADIX // 2):
            owner = at + k2 * (count // modes)
            packed[owner, pl.ds(off, 8), :] = found[k2][0]
            packed[owner, pl.ds(off + modes, 8), :] = found[k2][1]
        return carry

    lax.fori_loop(0, count // 8, chunk, 0, unroll=8)
    top = sections[0, 0:1, :]
    for j in range(1, RADIX):
        top = top - sections[j, 0:1, :] if j % 2 else top + sections[j, 0:1, :]
    packed[0, modes : modes + 1, :] = top

    def send(owner, carry):
        deliver(packed, owner, out)
        return carry

    lax.fori_loop(0, owners, send, 0, unroll=4)


def store_turned(store, owner, pieces):
    tiles = store.shape[2] // LANES
    used = sum(piece.shape[0] for piece in pieces)
    whole = jnp.concatenate(list(pieces) + [jnp.zeros((LANES * tiles - used, LANES), F32)], axis=0)
    for t in range(tiles):
        store[owner, :, t * LANES : (t + 1) * LANES] = whole[t * LANES : (t + 1) * LANES].T


def collect_halves(arrived, even, odd, owner):
    far, comps, _, _ = arrived.shape
    mine = [arrived[owner, c] for c in range(comps)]
    other = [arrived[owner + far // 2, c] for c in range(comps)]
    store_turned(even, owner, [a + b for a, b in zip(mine, other)])
    store_turned(odd, owner, [a - b for a, b in zip(mine, other)])


def collect_far(rows, arrived, even, odd, owner):
    far = arrived.shape[0]
    comps = 2 * arrived.shape[1] // rows
    first, second = arrived[owner], arrived[far - 1 - owner]
    halves = join(first, second), join_second(first, second)
    pieces = []
    for c in range(comps):
        for half in halves:
            pieces += [half[(m * comps + c) * 8 : (m * comps + c) * 8 + 8] for m in range(rows // 16)]
    store_turned(even, owner, pieces)


def inverse_rows(arrived, table, even, odd, mixed, turned, ready, collect):
    near = even.shape[0]
    modes = even.shape[1] // 2
    tiles, length, _ = turned.shape
    count = length // RADIX

    def gather(owner, carry):
        collect(arrived, even, odd, owner)
        return carry

    lax.fori_loop(0, near, gather, 0, unroll=4)
    per = modes // 8

    def chunk(q, carry):
        at = q // per
        off = pl.multiple_of((q % per) * 8, 8)
        row = pl.multiple_of(q * 8, 8)

        def four(s):
            t0, t1, t2 = c_add(s[0], s[2]), c_sub(s[0], s[2]), c_add(s[1], s[3])
            d = c_sub(s[1], s[3])
            t3 = (-d[1], d[0])
            return c_add(t0, t2), c_add(t1, t3), c_sub(t0, t2), c_sub(t1, t3)

        for first, store in ((0, even), (1, odd)):
            parts = []
            for k2 in range(RADIX // 2):
                owner = at + k2 * (count // modes)
                parts.append((store[owner, pl.ds(off, 8), :], store[owner, pl.ds(off + modes, 8), :]))
            if first:
                p1, p2, p3 = parts[1:]
                parts[1] = ((p1[0] - p1[1]) * ROOT, (p1[0] + p1[1]) * ROOT)
                parts[2] = (-p2[1], p2[0])
                parts[3] = ((p3[0] + p3[1]) * -ROOT, (p3[0] - p3[1]) * ROOT)
            for index, value in enumerate(four(parts)):
                mixed[2 * index + first, pl.ds(row, 8), :] = value[0]
                mixed[2 * index + first, pl.ds(row + count, 8), :] = value[1]
        return carry

    lax.fori_loop(0, count // 8, chunk, 0, unroll=8)
    scale = 1.0 / math.sqrt(length)
    ready()
    for j in range(RADIX):
        piece = dot3(table[j, :count], mixed[j, :count, :]) - dot3(table[j, count:], mixed[j, count:, :])
        if j % 2:
            piece = piece - odd[0, modes : modes + 1, :] * scale
        else:
            piece = piece + even[0, modes : modes + 1, :] * scale
        for t in range(tiles):
            turned[t, pl.ds(j, count, stride=RADIX), :] = piece[:, t * LANES : (t + 1) * LANES]


def turn_in(parts, turned, start):
    tiles = turned.shape[0]
    used = sum(part.shape[0] for part in parts)
    blank = jnp.zeros((LANES * tiles - used, LANES), F32)
    whole = jnp.concatenate(list(parts) + [blank], axis=0)
    for t in range(tiles):
        turned[t, pl.ds(start, LANES), :] = whole[t * LANES : (t + 1) * LANES].T


def turn_out(turned, start, rows, comps):
    tiles = turned.shape[0]
    whole = jnp.concatenate([turned[t, pl.ds(start, LANES), :].T for t in range(tiles)], axis=0)
    return [whole[c * rows : (c + 1) * rows] for c in range(comps)]


def fetch(sems, *pairs):
    copies = [pltpu.make_async_copy(source, target, sems.at[k]) for k, (source, target) in enumerate(pairs)]
    for copy in copies:
        copy.start()
    return copies


def y_forward_kernel(flags, field, table_far, out, turned, sections, packed, table, sems):
    comps, _, length = field.shape
    (got_table,) = fetch(sems, (table_far, table))

    def load(q, carry):
        start = pl.multiple_of(q * LANES, LANES)
        turn_in([field[c, :, pl.ds(start, LANES)] for c in range(comps)], turned, start)
        return carry

    lax.fori_loop(0, length // LANES, load, 0, unroll=4)
    forward_rows(turned, table, flags[0], sections, packed, out, got_table.wait, deliver_near)


def y_middle_kernel(prestress_far, slip_far, rate_far, inverse_far, forward_far, arrived, out, stress_far, *rest):
    turned, even, odd, mixed, sections, packed, inverse, forward, prestress, slip, rate, stress, sems = rest
    comps, rows, length = prestress.shape
    slip_used = slip_far.at[: slip.shape[0]]
    got_inverse, got_prestress, got_slip, got_rate, got_forward = fetch(
        sems,
        (inverse_far, inverse),
        (prestress_far, prestress),
        (slip_used, slip),
        (rate_far, rate),
        (forward_far, forward),
    )
    inverse_rows(arrived, inverse, even, odd, mixed, turned, got_inverse.wait, collect_halves)
    got_prestress.wait()
    got_slip.wait()
    got_rate.wait()

    def step(q, carry):
        start = pl.multiple_of(q * LANES, LANES)
        lanes = pl.ds(start, LANES)
        parts = turn_out(turned, start, rows, comps)
        s = [prestress[c, :, lanes] + parts[c] for c in range(comps)]
        for c in range(comps):
            stress[c, :, lanes] = s[c]
        first = friction(*s, slip[0, :, lanes], slip[1, :, lanes])
        turn_in([(first[c] - rate[c, :, lanes]) * 0.5 for c in range(comps)], turned, start)
        return carry

    lax.fori_loop(0, length // LANES, step, 0, unroll=2)
    give_stress = pltpu.make_async_copy(stress, stress_far, sems.at[5])
    give_stress.start()
    deliver = functools.partial(deliver_far, rows)
    forward_rows(turned, forward, None, sections, packed, out, got_forward.wait, deliver)
    give_stress.wait()


def y_final_kernel(stress_far, slip_far, rate_far, inverse_far, arrived, new_rate, new_slip, *rest):
    turned, even, mixed, inverse, stress, slip, rate, sems = rest
    comps, rows, length = stress.shape
    got_inverse, *got = fetch(sems, (inverse_far, inverse), (stress_far, stress), (slip_far, slip), (rate_far, rate))
    collect = functools.partial(collect_far, rows)
    inverse_rows(arrived, inverse, even, even, mixed, turned, got_inverse.wait, collect)
    for copy in got:
        copy.wait()

    def step(q, carry):
        start = pl.multiple_of(q * LANES, LANES)
        lanes = pl.ds(start, LANES)
        parts = turn_out(turned, start, rows, comps)
        s = [stress[c, :, lanes] + parts[c] for c in range(comps)]
        second = friction(*s, slip[0, :, lanes], slip[1, :, lanes])
        for c in range(comps):
            new_rate[c, :, lanes] = second[c]
            new_slip[c, :, lanes] = slip[c, :, lanes] + 0.25 * (rate[c, :, lanes] + second[c])
        return carry

    lax.fori_loop(0, length // LANES, step, 0, unroll=2)


def inverse_eight(z, turn):
    def four(a, b, c, d):
        t0, t1, t2, t3 = a + c, a - c, b + d, turn(b - d)
        return t0 + t2, t1 + t3, t0 - t2, t1 - t3

    e = four(z[0], z[2], z[4], z[6])
    o = four(z[1], z[3], z[5], z[7])
    o1 = (o[1] + turn(o[1])) * ROOT
    o3 = (turn(o[3]) - o[3]) * ROOT
    turned = (o[0], o1, turn(o[2]), o3)
    return [e[k] + turned[k] for k in range(4)] + [e[k] - turned[k] for k in range(4)]


def x_kernel(has_past, arrived, forward_far, inverse_far, weight, *rest):
    if has_past:
        past, out, sections, mixed, forward, inverse, sems = rest
    else:
        out, sections, mixed, forward, inverse, sems = rest
    got_forward = pltpu.make_async_copy(forward_far, forward, sems.at[0])
    got_inverse = pltpu.make_async_copy(inverse_far, inverse, sems.at[1])

    @pl.when(pl.program_id(0) == 0)
    def _():
        got_forward.start()
        got_inverse.start()
        got_forward.wait()

    near, _, rows, _ = arrived.shape
    far = out.shape[0]
    count = inverse.shape[2] // 2
    for j in range(RADIX):
        piece = jnp.concatenate(
            [arrived[src, 0, pl.ds(j, rows // RADIX, stride=RADIX), :] for src in range(near)], axis=0
        )
        sections[j] = dot3(forward[j], piece)
    sign = jnp.where(lax.broadcasted_iota(jnp.int32, (8, LANES), 1) < LANES // 2, -1.0, 1.0).astype(F32)

    def turn(value):
        return sign * pltpu.roll(value, LANES // 2, 1)

    def chunk(q, carry):
        row = pl.multiple_of(q * 8, 8)
        parts = [(sections[j, pl.ds(row, 8), :], sections[j, pl.ds(row + count, 8), :]) for j in range(RADIX)]
        outs = forward_eight(parts, RADIX)
        z = []
        for k2 in range(RADIX):
            spot = pl.ds(row + k2 * count, 8)
            w = weight[0, spot, :]
            value = w * outs[k2][0] + turn(w * outs[k2][1])
            if has_past:
                value = value + past[0, spot, :]
            z.append(value)

        for j, value in enumerate(inverse_eight(z, turn)):
            mixed[j, pl.ds(row, 8), :] = value
        return carry

    lax.fori_loop(0, count // 8, chunk, 0, unroll=8)

    @pl.when(pl.program_id(0) == 0)
    def _():
        got_inverse.wait()

    lanes = lax.broadcasted_iota(jnp.int32, (count, LANES), 1)
    wide = jnp.where(lanes < LANES // 2, -1.0, 1.0).astype(F32)
    step = rows // RADIX
    for j in range(RADIX):
        both = dot3(inverse[j], mixed[j])
        value = both[:count] + wide * pltpu.roll(both[count:], LANES // 2, 1)
        for dest in range(far):
            out[dest, 0, pl.ds(j, step, stride=RADIX), :] = value[dest * step : (dest + 1) * step]


def x_far_kernel(arrived, forward_far, inverse_far, weight_far, out, sections, mixed, forward, inverse, weight, sems):
    got_forward, got_weight, got_inverse = fetch(
        sems, (forward_far, forward), (weight_far, weight), (inverse_far, inverse)
    )
    tiles, wide, _ = weight.shape
    count = wide // RADIX
    stride = 3 * RADIX

    def spot_of(c, j):
        return pl.ds(c * RADIX + j, count // 2, stride=stride)

    got_forward.wait()
    for j in range(RADIX):
        x0, x1, x2 = (arrived[spot_of(c, j), :] for c in range(3))
        none = jnp.zeros_like(x2)
        left = jnp.concatenate([join(x0, x1), join_second(x0, x1)], axis=0)
        right = jnp.concatenate([join(x2, none), join_second(x2, none)], axis=0)
        sections[j] = dot3(forward[j], jnp.concatenate([left, right], axis=1))
    got_weight.wait()
    sign = jnp.where(lax.broadcasted_iota(jnp.int32, (1, LANES), 1) < LANES // 2, -1.0, 1.0).astype(F32)

    def turn(value):
        return sign * pltpu.roll(value, LANES // 2, 1)

    def chunk(q, carry):
        row = pl.multiple_of(q * 8, 8)
        for t in range(tiles):
            lanes = slice(t * LANES, (t + 1) * LANES)
            parts = [
                (sections[j, pl.ds(row, 8), lanes], sections[j, pl.ds(row + count, 8), lanes]) for j in range(RADIX)
            ]
            z = []
            for k2, found in enumerate(forward_eight(parts, RADIX)):
                w = weight[t, pl.ds(row + k2 * count, 8), :]
                z.append(w * found[0] + turn(w * found[1]))
            for j, value in enumerate(inverse_eight(z, turn)):
                mixed[j, pl.ds(row, 8), lanes] = value
        return carry

    lax.fori_loop(0, count // 8, chunk, 0, unroll=4)
    got_inverse.wait()
    half = count // 2
    for j in range(RADIX):
        both = dot3(inverse[j], mixed[j])
        found = []
        for t in range(tiles):
            lanes = slice(t * LANES, (t + 1) * LANES)
            value = both[:count, lanes] + turn(both[count:, lanes])
            found.append((value[:half], value[half:]))
        out[spot_of(0, j), :] = join(*found[0])
        out[spot_of(1, j), :] = join_second(*found[0])
        out[spot_of(2, j), :] = join(*found[1])


def pick(values, bits):
    level = 0
    while len(values) > 1:
        if len(values) % 2:
            values = values + [values[-1]]
        values = [jnp.where(bits[level], values[k + 1], values[k]) for k in range(0, len(values), 2)]
        level += 1
    return values[0]


def bits_of(band, bands):
    return [(band & (1 << level)) != 0 for level in range(max((bands - 1).bit_length(), 1))]


def weights_past(table, band, bits, c, depth):
    bands, lags, comps = table.shape[0], table.shape[1] // 3, 3
    found = []
    for at in range(depth):
        spot = (lags - depth + at) * comps + c
        if lags - depth + at < SHORT:
            found.append(pick([table[b, spot] for b in range(bands)], bits))
        else:
            found.append(jnp.where(band == 0, table[0, spot], 0.0))
    return found


def history_kernel(flags, table, band, band_back, band_edge, history, past_back, past_edge, flip, past, stacked):
    bands, comps = table.shape[0], 3
    depth = history.shape[0]
    rows, width = band.shape

    def group(q, carry):
        spot = pl.ds(pl.multiple_of(q * 16, 16), 16)
        own = band[spot, :]
        bits = bits_of(own, bands)
        for c in range(comps):
            sums = [jnp.zeros((16, width), F32) for _ in range(2)]
            for at, w in enumerate(weights_past(table, own, bits, c, depth)):
                for p in range(2):
                    sums[p] = sums[p] + w * history[at, c, p, spot, :].astype(F32)
            for p in range(2):
                stacked[c, pl.ds(pl.multiple_of(q * 16 + p * rows, 16), 16), :] = sums[p]
        return carry

    lax.fori_loop(0, rows // 16, group, 0)

    edge = flags[1] > 0.0
    there, beyond = [], []
    for at in range(depth):
        for c in range(comps):
            for p in range(2):
                there.append(past_back[at, c, p].astype(F32)[:1])
                beyond.append(past_edge[at, c, p].astype(F32)[:1])
    count = len(there)
    blank = -(count + 1) % 16
    there += [band_back[...].astype(F32)[:1], jnp.zeros((blank, width), F32)]
    beyond += [band_edge[...].astype(F32)[:1], jnp.zeros((blank, LANES), F32)]
    both = [jnp.concatenate(rows_of, axis=0).astype(BF16) for rows_of in (there, beyond)]
    row_back = jnp.dot(jnp.concatenate(both, axis=1), flip[...], preferred_element_type=F32)
    back = row_back[count : count + 1].astype(jnp.int32)
    bits = bits_of(back, bands)
    for c in range(comps):
        found = weights_past(table, back, bits, c, depth)
        for p in range(2):
            reverse = jnp.zeros((1, width), F32)
            for at, w in enumerate(found):
                spot = (at * comps + c) * 2 + p
                reverse = reverse + w * row_back[spot : spot + 1, :]
            if p:
                reverse = -reverse
            mine = stacked[c, p * rows : p * rows + 1, :]
            stacked[c, p * rows : p * rows + 1, :] = jnp.where(edge, 0.5 * (mine + reverse), mine)
        for t in range(width // LANES):
            spot = pl.ds(t * LANES, LANES)
            past[c, spot, :] = stacked[c, :, spot].T


def weight_kernel(flags, table, band, few, block, few_back, block_edge, few_edge, flip, swap, out, stacked):
    bands, comps = table.shape
    rows, width = band.shape
    odd = (lax.broadcasted_iota(jnp.int32, (1, width), 1) & 1) == 1
    parity = jnp.where(odd, flags[0], 1.0).astype(F32)
    edge = flags[1] > 0.0

    def exact(values):
        return values.astype(F32).astype(BF16)

    there = jnp.concatenate([exact(block[...]), exact(few_back[...])], axis=0)
    beyond = jnp.concatenate([exact(block_edge[...]), exact(few_edge[...])], axis=0)
    turned = jnp.dot(jnp.concatenate([there, beyond], axis=1), flip[...], preferred_element_type=F32)
    turned = jnp.dot(swap[...], turned.astype(BF16), preferred_element_type=F32).astype(jnp.int32)
    tiles = out.shape[0]
    slots = LANES // 2 // rows
    if tiles * slots > comps:
        stacked[tiles - 1] = jnp.zeros((LANES, width), F32)
    for c in range(comps):
        tile, re = c // slots, c % slots * rows
        im = re + LANES // 2
        values = [table[b, c] for b in range(bands)]
        for q in range(rows // 8):
            spot = slice(q * 8, q * 8 + 8)
            value = pick(values, bits_of(band[spot, :], bands)) + pick(values, bits_of(turned[spot], bands))
            value = value * parity
            if q == 0:
                first = lax.broadcasted_iota(jnp.int32, (8, width), 0) == 0
                other = pick(values, bits_of(few[1:2, :], bands))
                other = other + pick(values, bits_of(turned[rows : rows + 1], bands))
                other = jnp.where(edge, 0.5 * (other * parity), value[:1])
                value = jnp.where(first & edge, 0.5 * value, value)
                stacked[tile, im : im + 8, :] = jnp.where(first, other, value)
            else:
                stacked[tile, im + q * 8 : im + q * 8 + 8, :] = value
            stacked[tile, re + q * 8 : re + q * 8 + 8, :] = value
    for tile in range(tiles):
        for t in range(width // LANES):
            spot = slice(t * LANES, (t + 1) * LANES)
            out[tile, spot, :] = stacked[tile, :, spot].T


VMEM = pl.BlockSpec(memory_space=pltpu.VMEM)
SMEM = pl.BlockSpec(memory_space=pltpu.SMEM)
ANY = pl.BlockSpec(memory_space=pl.ANY)
PARAMS = pltpu.CompilerParams(vmem_limit_bytes=60 * 1024 * 1024)
SMALL = pltpu.CompilerParams(vmem_limit_bytes=60 * 1024 * 1024)


def y_scratch(length, modes):
    count = length // RADIX
    near = length // 2 // modes
    wide = 2 * LANES
    turned = pltpu.VMEM((2, length, LANES), F32)
    halves = pltpu.VMEM((near, 2 * modes, wide), F32)
    sections = pltpu.VMEM((RADIX, 2 * count, wide), F32)
    return turned, halves, sections


def took(microseconds):
    return pl.CostEstimate(flops=int(microseconds * 1e9), bytes_accessed=1, transcendentals=0)


def struct(*shape):
    return jax.ShapeDtypeStruct(shape, F32)


def flip_table(chunk):
    flip = np.zeros((chunk + LANES, chunk), np.float32)
    flip[chunk - np.arange(1, chunk), np.arange(1, chunk)] = 1.0
    flip[chunk, 0] = 1.0
    return jnp.asarray(flip.astype(BF16))


def swap_table(modes):
    swap = np.zeros((modes + 16, modes + 16), np.float32)
    swap[np.arange(1, modes), modes - np.arange(1, modes)] = 1.0
    swap[0, modes] = 1.0
    swap[modes, modes + 1] = 1.0
    return jnp.asarray(swap.astype(BF16))


def with_kernels(slip_rate, slip_field, prestress, history, kernel, band_len, mode_band):
    comps, rows, length = slip_rate.shape
    modes, wide = mode_band.shape
    far = lax.axis_size(AXES)
    near = lax.axis_size(NEAR)
    bands, lags = kernel.shape[:2]
    depth = history.shape[0]
    flags, coded, block, few = exchange_bands(kernel, band_len, mode_band)

    y_forward, y_inverse = (jnp.asarray(split_table(t)) for t in tables(length))
    x_forward, x_inverse = tables(wide)
    eights = rows // RADIX
    order = np.arange(wide // RADIX).reshape(far, 2, eights // 2).transpose(1, 0, 2).reshape(-1)
    far_forward = jnp.asarray(split_table(x_forward[:, :, order]))
    both = x_inverse.reshape(RADIX, 2, wide // RADIX, wide // RADIX)[:, :, order]
    far_inverse = jnp.asarray(split_table(both.reshape(x_inverse.shape)))
    x_forward = jnp.asarray(split_table(x_forward[:, :, : wide // RADIX // 2]))
    x_inverse = jnp.asarray(split_table(x_inverse))

    turned, halves, sections = y_scratch(length, modes)
    y_table = pltpu.VMEM(y_forward.shape, BF16)
    field = pltpu.VMEM((comps, rows, length), F32)
    sent = pl.pallas_call(
        y_forward_kernel,
        out_shape=struct(near, comps, rows, 2 * modes),
        in_specs=[SMEM, VMEM, ANY],
        out_specs=VMEM,
        scratch_shapes=[turned, sections, halves, y_table, pltpu.SemaphoreType.DMA((1,))],
        compiler_params=PARAMS,
        cost_estimate=took(6),
        name="y_forward",
    )(flags, slip_rate, y_forward)
    here = lax.all_to_all(sent, NEAR, 0, 0, tiled=True)

    chunk = 4 * LANES
    steps = wide // chunk
    back = lambda g: steps - 1 - g
    after = lambda g: (steps - g) % steps * (chunk // LANES)
    flip = flip_table(chunk)
    flip_spec = pl.BlockSpec(flip.shape, lambda g: (0, 0))
    past = pl.pallas_call(
        history_kernel,
        grid=(steps,),
        out_shape=struct(comps, wide, 2 * modes),
        in_specs=[
            SMEM,
            SMEM,
            pl.BlockSpec((modes, chunk), lambda g: (0, g)),
            pl.BlockSpec((8, chunk), lambda g: (0, back(g))),
            pl.BlockSpec((8, LANES), lambda g: (0, after(g))),
            pl.BlockSpec((depth, comps, 2, modes, chunk), lambda g: (0, 0, 0, 0, g)),
            pl.BlockSpec((depth, comps, 2, 16, chunk), lambda g: (0, 0, 0, 0, back(g))),
            pl.BlockSpec((depth, comps, 2, 16, LANES), lambda g: (0, 0, 0, 0, after(g))),
            flip_spec,
        ],
        out_specs=pl.BlockSpec((comps, chunk, 2 * modes), lambda g: (0, g, 0)),
        scratch_shapes=[pltpu.VMEM((comps, 2 * modes, chunk), F32)],
        compiler_params=SMALL,
        cost_estimate=took(7),
        name="history",
    )(flags, coded, mode_band, mode_band, mode_band, history, history, history, flip)

    def weights(marks, table, band, few, block):
        owned = band.shape[0]
        tiles = -(-comps // (LANES // 2 // owned))
        swap = swap_table(owned)
        own = lambda g: (0, g)
        return pl.pallas_call(
            weight_kernel,
            grid=(steps,),
            out_shape=struct(tiles, wide, LANES),
            in_specs=[
                SMEM,
                SMEM,
                pl.BlockSpec((owned, chunk), own),
                pl.BlockSpec((16, chunk), own),
                pl.BlockSpec((owned, chunk), lambda g: (0, back(g))),
                pl.BlockSpec((16, chunk), lambda g: (0, back(g))),
                pl.BlockSpec((owned, LANES), lambda g: (0, after(g))),
                pl.BlockSpec((16, LANES), lambda g: (0, after(g))),
                flip_spec,
                pl.BlockSpec(swap.shape, lambda g: (0, 0)),
            ],
            out_specs=pl.BlockSpec((tiles, chunk, LANES), lambda g: (0, g, 0)),
            scratch_shapes=[pltpu.VMEM((tiles, LANES, chunk), F32)],
            compiler_params=SMALL,
            cost_estimate=took(40),
            name="weights",
        )(marks, table, band, few, block, few, block, few, flip, swap)

    now_weight = weights(flags, coded[:, :comps] + coded[:, comps : 2 * comps], mode_band, few, block)
    lower = flags[0] > 0.0
    part = modes // 2
    band = jnp.where(lower, mode_band[:part], block[part:])
    other = jnp.where(lower, block[part:], mode_band[:part])
    few = jnp.concatenate([jnp.where(lower, few[:1], mode_band[part : part + 1]), few[1:]], axis=0)
    marks = jnp.stack([jnp.ones((), F32), jnp.where(lower, flags[1], 0.0)])
    later_weight = weights(marks, coded[:, :comps], band, few, other)

    def x_stage(given, weight, added):
        whole = pl.BlockSpec((1, wide, 2 * modes), lambda c: (c, 0, 0))
        operands = [given, x_forward, x_inverse, weight] + ([] if added is None else [added])
        count = wide // RADIX
        return pl.pallas_call(
            functools.partial(x_kernel, added is not None),
            grid=(comps,),
            out_shape=struct(far, comps, rows, 2 * modes),
            in_specs=[pl.BlockSpec((near, 1, rows, 2 * modes), lambda c: (0, c, 0, 0)), ANY, ANY]
            + [whole] * (len(operands) - 3),
            out_specs=pl.BlockSpec((far, 1, rows, 2 * modes), lambda c: (0, c, 0, 0)),
            scratch_shapes=[
                pltpu.VMEM((RADIX, 2 * count, LANES), F32),
                pltpu.VMEM((RADIX, count, LANES), F32),
                pltpu.VMEM(x_forward.shape, BF16),
                pltpu.VMEM(x_inverse.shape, BF16),
                pltpu.SemaphoreType.DMA((2,)),
            ],
            compiler_params=SMALL,
            cost_estimate=took(12),
            name="x_stage",
        )(*operands)

    fields = lax.all_to_all(x_stage(here, now_weight, past), AXES, 0, 0, tiled=True)
    sent, stress = pl.pallas_call(
        y_middle_kernel,
        out_shape=[struct(far, comps * rows // 2, LANES), struct(comps, rows, length)],
        in_specs=[ANY] * 5 + [VMEM],
        out_specs=[VMEM, ANY],
        scratch_shapes=[turned, halves, halves, sections, sections, halves, y_table, y_table]
        + [field, pltpu.VMEM((2, rows, length), F32), field, field, pltpu.SemaphoreType.DMA((6,))],
        compiler_params=PARAMS,
        cost_estimate=took(14),
        name="y_middle",
    )(prestress, slip_field, slip_rate, y_inverse, y_forward, fields)
    here = lax.all_to_all(sent, AXES, 0, 0, tiled=True)
    count = wide // RADIX
    sent = pl.pallas_call(
        x_far_kernel,
        out_shape=struct(far * comps * rows // 2, LANES),
        in_specs=[VMEM, ANY, ANY, ANY],
        out_specs=VMEM,
        scratch_shapes=[
            pltpu.VMEM((RADIX, 2 * count, 2 * LANES), F32),
            pltpu.VMEM((RADIX, count, 2 * LANES), F32),
            pltpu.VMEM(far_forward.shape, BF16),
            pltpu.VMEM(far_inverse.shape, BF16),
            pltpu.VMEM(later_weight.shape, F32),
            pltpu.SemaphoreType.DMA((3,)),
        ],
        compiler_params=SMALL,
        cost_estimate=took(8),
        name="x_far",
    )(here.reshape(-1, LANES), far_forward, far_inverse, later_weight)
    fields = lax.all_to_all(sent.reshape(here.shape), AXES, 0, 0, tiled=True)
    return tuple(
        pl.pallas_call(
            y_final_kernel,
            out_shape=[struct(comps, rows, length)] * 2,
            in_specs=[ANY] * 4 + [VMEM],
            out_specs=[VMEM] * 2,
            scratch_shapes=[turned, halves, sections, y_table, field, field, field]
            + [pltpu.SemaphoreType.DMA((4,))],
            compiler_params=PARAMS,
            cost_estimate=took(10),
            name="y_final",
        )(stress, slip_field, slip_rate, y_inverse, fields)
    )


def reverse_modes(values):
    return jnp.roll(jnp.flip(values, -1), 1, -1)


def exchange_bands(kernel, band_len, mode_band):
    bands, lags, comps = kernel.shape
    far = lax.axis_size(AXES)
    near = lax.axis_size(NEAR)
    me = lax.axis_index(AXES)
    first = me % near == 0
    flags = jnp.stack([jnp.where(me < near, 1.0, -1.0), jnp.where(first, 1.0, 0.0)]).astype(F32)
    live = (jnp.arange(lags, dtype=jnp.int32)[None, :] < band_len[:, None]).astype(F32)
    coded = (kernel * live[:, :, None]).reshape(bands, lags * comps)
    block = lax.ppermute(mode_band, AXES, [(d, far - 1 - d) for d in range(far)])
    pairs = [(d, (d + near) % far if d % near == 0 else far - d) for d in range(far)]
    row = lax.ppermute(mode_band[:1], AXES, pairs)
    edge = jnp.where(first, mode_band[:1], row)
    few = jnp.concatenate([edge, row, jnp.zeros((14, mode_band.shape[1]), jnp.int32)], axis=0)
    return flags, coded, block, few


def reverse_first(history, mode_band):
    row_back = reverse_modes(history[:, :, :, 0, :].astype(F32).reshape(-1, mode_band.shape[1]))
    return row_back, reverse_modes(mode_band[:1])


def plain(slip_rate, slip_field, prestress, history, kernel, band_len, mode_band):
    comps, rows, length = slip_rate.shape
    modes, wide = mode_band.shape
    far = lax.axis_size(AXES)
    near = lax.axis_size(NEAR)
    bands, lags = kernel.shape[:2]
    depth = history.shape[0]
    flags, coded, block, few = exchange_bands(kernel, band_len, mode_band)
    row_back, row_mirror = reverse_first(history, mode_band)
    mirror = reverse_modes(jnp.concatenate([few[:1], jnp.flip(block[1:], 0)], axis=0))
    extra = jnp.concatenate([few[1:2], reverse_modes(few[1:2])], axis=0)
    table = coded.reshape(bands, lags, comps)
    edge = flags[1] > 0.0
    top = (jnp.arange(modes) == 0)[None, :, None] & edge

    def dot(spec, a, b):
        return jnp.einsum(spec, a, b, precision=lax.Precision.HIGHEST)

    def angles(first, second, size):
        product = (first[:, None] * second[None, :]) % size
        angle = product.astype(F32) * (2.0 * math.pi / size)
        return jnp.cos(angle) / math.sqrt(size), jnp.sin(angle) / math.sqrt(size)

    def weights(band, values):
        result = jnp.zeros(values.shape[1:] + band.shape, F32)
        for b in range(bands):
            result = jnp.where(band == b, values[b][..., None, None], result)
        return result

    past = []
    for at in range(depth):
        w = weights(mode_band, table[:, lags - depth + at])[:, None]
        past.append(w * history[at].astype(F32))
    past = sum(past)
    back = row_back.reshape(depth, comps, 2, 1, wide)
    w = weights(row_mirror, table[:, lags - depth :])
    back = jnp.sum(w[:, :, None] * back, axis=0) * jnp.array([1.0, -1.0], F32)[:, None, None]
    past = jnp.where(top, 0.5 * (past + back), past)
    parity = jnp.where(jnp.arange(wide) % 2 == 1, flags[0], 1.0)

    def filters(values):
        whole = (weights(mode_band, values) + weights(mirror, values)) * parity
        other = (weights(extra[:1], values) + weights(extra[1:], values)) * parity
        return jnp.where(top, 0.5 * whole, whole), jnp.where(top, 0.5 * other, whole)

    own = jnp.arange(length, dtype=jnp.int32)
    y_cos, y_sin = angles(own, own[: length // 2], length)
    nyquist = jnp.where(own % 2 == 1, -1.0, 1.0).astype(F32) / math.sqrt(length)
    y_sin = y_sin.at[:, 0].set(-nyquist)
    across = jnp.arange(wide, dtype=jnp.int32)
    x_cos, x_sin = angles(across, across, wide)
    flip = jnp.where(own % 2 == 1, flags[0], 1.0)

    def y_forward(field):
        field = field * flip
        both = jnp.stack([dot("cxy,yk->ckx", field, y_cos), -dot("cxy,yk->ckx", field, y_sin)], 1)
        both = both.reshape(comps, 2, near, modes, rows).transpose(2, 0, 4, 1, 3)
        return lax.all_to_all(both, NEAR, 0, 0, tiled=True)

    def x_stage(given, filt, added):
        given = given.transpose(1, 3, 4, 0, 2).reshape(comps, 2, modes, near * rows)
        real = dot("cpkx,xm->cpkm", given, x_cos[: near * rows])
        imag = -dot("cpkx,xm->cpkm", given, x_sin[: near * rows])
        a, b = filt
        out_real = a * real[:, 0] - b * imag[:, 1]
        out_imag = a * imag[:, 0] + b * real[:, 1]
        if added is not None:
            out_real, out_imag = out_real + added[:, 0], out_imag + added[:, 1]
        first = dot("ckm,mx->ckx", out_real, x_cos) - dot("ckm,mx->ckx", out_imag, x_sin)
        second = dot("ckm,mx->ckx", out_real, x_sin) + dot("ckm,mx->ckx", out_imag, x_cos)
        both = jnp.stack([first, second], 1).reshape(comps, 2, modes, far, rows).transpose(3, 0, 4, 1, 2)
        return lax.all_to_all(both, AXES, 0, 0, tiled=True)

    def y_inverse(given):
        given = given.reshape(2, near, comps, rows, 2, modes).transpose(0, 4, 2, 3, 1, 5)
        given = given.reshape(2, 2, comps, rows, length // 2)
        half = dot("hcxk,yk->hcxy", given[:, 0], y_cos) - dot("hcxk,yk->hcxy", given[:, 1], y_sin)
        return half[0] + half[1] * jnp.where(own % 2 == 1, -1.0, 1.0)

    def phi(s):
        return jnp.stack(friction(s[0], s[1], s[2], slip_field[0], slip_field[1]))

    now = filters(table[:, 0] + table[:, 1])
    later = filters(table[:, 0])
    stress = prestress + y_inverse(x_stage(y_forward(slip_rate), now, past))
    shift = 0.5 * (phi(stress) - slip_rate)
    second = phi(stress + y_inverse(x_stage(y_forward(shift), later, None)))
    return second, slip_field + 0.25 * (slip_rate + second)


def solution(mesh):
    shape = mesh.devices.shape
    ours = Mesh(mesh.devices.reshape(2, shape[0] // 2, shape[1]), AXES)

    def on_device(slip_rate, slip_field, prestress, history, kernel, band_len, mode_band):
        args = (slip_rate, slip_field, prestress, history, kernel, band_len, mode_band)
        rows, modes = slip_rate.shape[1], mode_band.shape[0]
        if 2 * modes == LANES and 2 * rows == LANES and slip_rate.shape[0] == 3:
            return with_kernels(*args)
        return plain(*args)

    rows = P(None, AXES, None)
    return jax.shard_map(
        on_device,
        mesh=ours,
        in_specs=(rows, rows, rows, P(None, None, None, AXES, None), P(), P(), P(AXES, None)),
        out_specs=(rows, rows),
        check_vma=False,
    )
```

```python
import functools
import math

import jax
import jax.numpy as jnp
import numpy as np
from jax import lax
from jax.experimental import pallas as pl
from jax.experimental.pallas import tpu as pltpu
from jax.sharding import Mesh, PartitionSpec as P


LANES = 128
RADIX = 8
SHORT = 4
AXES = ("half", "part", "ky")
NEAR = ("part", "ky")
F32 = jnp.float32
BF16 = jnp.bfloat16
ROOT = math.sqrt(0.5)
PIECES = 4

static_fric = 0.7
dynamic_fric = 0.35
weaken_slip = 0.5


def softplus(value):
    return jnp.maximum(value, 0.0) + jnp.log1p(jnp.exp(-jnp.abs(value)))


def friction(s0, s1, s2, u0, u1):
    worn = jnp.sqrt(u0 * u0 + u1 * u1 + 1.0) - 1.0
    coeff = dynamic_fric + (static_fric - dynamic_fric) * jnp.exp(worn * (-1.0 / weaken_slip))
    tail = jnp.log1p(jnp.exp(-jnp.abs(s2)))
    strength = coeff * (jnp.maximum(-s2, 0.0) + tail)
    magnitude = jnp.sqrt(s0 * s0 + s1 * s1 + 1.0)
    ratio = softplus(magnitude - strength) / magnitude
    return ratio * s0, ratio * s1, jnp.maximum(s2, 0.0) + tail


def split_table(values):
    high = values.astype(BF16)
    low = (values - high.astype(np.float64)).astype(BF16)
    return np.concatenate([high, low], axis=-1)


def tables(length):
    count = length // RADIX
    outer = np.arange(count)
    spots = RADIX * outer[None, :, None] + np.arange(RADIX)[:, None, None]
    angle = 2.0 * np.pi / length * ((spots * outer[None, None, :]) % length)
    cos = np.cos(angle) / math.sqrt(length)
    sin = np.sin(angle) / math.sqrt(length)
    forward = np.concatenate([cos.transpose(0, 2, 1), -sin.transpose(0, 2, 1)], axis=1)
    inverse = np.concatenate([cos, sin], axis=1)
    return forward, inverse


def parts_of(sections, row, count, lanes):
    return [(sections[j, pl.ds(row, 8), lanes], sections[j, pl.ds(row + count, 8), lanes]) for j in range(RADIX)]


def dot3(table, values):
    depth = values.shape[0]
    high = values.astype(BF16)
    low = (values - high.astype(F32)).astype(BF16)
    left = jnp.concatenate([table, table[:, :depth]], axis=1)
    right = jnp.concatenate([high, high, low], axis=0)
    return jnp.dot(left, right, preferred_element_type=F32)


def c_add(a, b):
    return a[0] + b[0], a[1] + b[1]


def c_sub(a, b):
    return a[0] - b[0], a[1] - b[1]


def forward_eight(a, wanted):
    def four(p, q, r, s):
        t0, t1, t2 = c_add(p, r), c_sub(p, r), c_add(q, s)
        d = c_sub(q, s)
        t3 = (d[1], -d[0])
        return c_add(t0, t2), c_add(t1, t3), c_sub(t0, t2), c_sub(t1, t3)

    even = four(a[0], a[2], a[4], a[6])
    odd = four(a[1], a[3], a[5], a[7])
    o1 = ((odd[1][0] + odd[1][1]) * ROOT, (odd[1][1] - odd[1][0]) * ROOT)
    o2 = (odd[2][1], -odd[2][0])
    o3 = ((odd[3][1] - odd[3][0]) * ROOT, (odd[3][0] + odd[3][1]) * -ROOT)
    turned = (odd[0], o1, o2, o3)
    first = [c_add(even[k], turned[k]) for k in range(4)]
    if wanted <= 4:
        return first
    return first + [c_sub(even[k], turned[k]) for k in range(4)]


def low_half():
    return lax.broadcasted_iota(jnp.int32, (1, LANES), 1) % (LANES // 2) < LANES // 4


def join(a, b):
    return jnp.where(low_half(), a, pltpu.roll(b, LANES // 4, 1))


def join_second(a, b):
    return jnp.where(low_half(), pltpu.roll(a, LANES - LANES // 4, 1), b)


def blocks_of(packed, owner, comps, rows):
    whole = [packed[owner, :, t * LANES : (t + 1) * LANES].T for t in range(packed.shape[2] // LANES)]
    whole = jnp.concatenate(whole, axis=0)
    return [whole[c * rows : (c + 1) * rows] for c in range(comps)]


def deliver_near(packed, owner, out):
    _, comps, rows, _ = out.shape
    for c, block in enumerate(blocks_of(packed, owner, comps, rows)):
        out[owner, c] = block


def deliver_far(rows, packed, owner, out):
    far = out.shape[0]
    comps = 2 * out.shape[1] // rows
    for c, block in enumerate(blocks_of(packed, owner, comps, rows)):
        top, bottom = block[: rows // 2], block[rows // 2 :]
        for device, value in ((owner, join(top, bottom)), (far - 1 - owner, join_second(top, bottom))):
            for m in range(rows // 16):
                out[device, (m * comps + c) * 8 : (m * comps + c) * 8 + 8] = value[m * 8 : m * 8 + 8]


def forward_rows(turned, table, flag, sections, packed, out, ready, deliver, leave):
    tiles, length, _ = turned.shape
    count = length // RADIX
    owners = packed.shape[0]
    modes = packed.shape[1] // 2
    ready()
    for j in range(RADIX):
        piece = jnp.concatenate([turned[t, pl.ds(j, count, stride=RADIX), :] for t in range(tiles)], axis=1)
        if flag is not None and j % 2:
            piece = piece * flag
        sections[j] = dot3(table[j], piece)
    per = modes // 8

    def chunk(q, carry):
        at = q // per
        off = pl.multiple_of((q % per) * 8, 8)
        row = pl.multiple_of(q * 8, 8)
        found = forward_eight(parts_of(sections, row, count, slice(None)), 4)
        for k2 in range(RADIX // 2):
            owner = at + k2 * (count // modes)
            packed[owner, pl.ds(off, 8), :] = found[k2][0]
            packed[owner, pl.ds(off + modes, 8), :] = found[k2][1]
        return carry

    lax.fori_loop(0, count // 8, chunk, 0, unroll=8)
    top = sections[0, 0:1, :]
    for j in range(1, RADIX):
        top = top - sections[j, 0:1, :] if j % 2 else top + sections[j, 0:1, :]
    packed[0, modes : modes + 1, :] = top

    def send(owner, carry):
        deliver(packed, owner, out)
        return carry

    size = owners // PIECES
    for piece in range(PIECES):
        lax.fori_loop(piece * size, (piece + 1) * size, send, 0, unroll=True)
        leave(piece)


def store_turned(store, owner, pieces):
    tiles = store.shape[2] // LANES
    used = sum(piece.shape[0] for piece in pieces)
    whole = jnp.concatenate(list(pieces) + [jnp.zeros((LANES * tiles - used, LANES), F32)], axis=0)
    for t in range(tiles):
        store[owner, :, t * LANES : (t + 1) * LANES] = whole[t * LANES : (t + 1) * LANES].T


def collect_halves(arrived, even, odd, owner):
    far, comps, _, _ = arrived.shape
    mine = [arrived[owner, c] for c in range(comps)]
    other = [arrived[owner + far // 2, c] for c in range(comps)]
    store_turned(even, owner, [a + b for a, b in zip(mine, other)])
    store_turned(odd, owner, [a - b for a, b in zip(mine, other)])


def collect_far(rows, arrived, even, odd, owner):
    far = arrived.shape[0]
    comps = 2 * arrived.shape[1] // rows
    first, second = arrived[owner], arrived[far - 1 - owner]
    halves = join(first, second), join_second(first, second)
    pieces = []
    for c in range(comps):
        for half in halves:
            pieces += [half[(m * comps + c) * 8 : (m * comps + c) * 8 + 8] for m in range(rows // 16)]
    store_turned(even, owner, pieces)


def inverse_rows(arrived, table, even, odd, mixed, turned, ready, collect, arrive):
    near = even.shape[0]
    modes = even.shape[1] // 2
    tiles, length, _ = turned.shape
    count = length // RADIX

    def gather(owner, carry):
        collect(arrived, even, odd, owner)
        return carry

    size = near // PIECES
    for piece in range(PIECES):
        arrive(piece)
        lax.fori_loop(piece * size, (piece + 1) * size, gather, 0, unroll=True)
    per = modes // 8

    def chunk(q, carry):
        at = q // per
        off = pl.multiple_of((q % per) * 8, 8)
        row = pl.multiple_of(q * 8, 8)

        def four(s):
            t0, t1, t2 = c_add(s[0], s[2]), c_sub(s[0], s[2]), c_add(s[1], s[3])
            d = c_sub(s[1], s[3])
            t3 = (-d[1], d[0])
            return c_add(t0, t2), c_add(t1, t3), c_sub(t0, t2), c_sub(t1, t3)

        for first, store in ((0, even), (1, odd)):
            parts = []
            for k2 in range(RADIX // 2):
                owner = at + k2 * (count // modes)
                parts.append((store[owner, pl.ds(off, 8), :], store[owner, pl.ds(off + modes, 8), :]))
            if first:
                p1, p2, p3 = parts[1:]
                parts[1] = ((p1[0] - p1[1]) * ROOT, (p1[0] + p1[1]) * ROOT)
                parts[2] = (-p2[1], p2[0])
                parts[3] = ((p3[0] + p3[1]) * -ROOT, (p3[0] - p3[1]) * ROOT)
            for index, (re, im) in enumerate(four(parts)):
                j = 2 * index + first
                mixed[j, pl.ds(row, 8), :] = re
                mixed[j, pl.ds(row + count, 8), :] = im
        return carry

    lax.fori_loop(0, count // 8, chunk, 0, unroll=8)
    scale = 1.0 / math.sqrt(length)
    ready()
    for j in range(RADIX):
        piece = dot3(table[j, :count], mixed[j, :count, :]) - dot3(table[j, count:], mixed[j, count:, :])
        if j % 2:
            piece = piece - odd[0, modes : modes + 1, :] * scale
        else:
            piece = piece + even[0, modes : modes + 1, :] * scale
        for t in range(tiles):
            turned[t, pl.ds(j, count, stride=RADIX), :] = piece[:, t * LANES : (t + 1) * LANES]


def turn_in(parts, turned, start):
    tiles = turned.shape[0]
    used = sum(part.shape[0] for part in parts)
    blank = jnp.zeros((LANES * tiles - used, LANES), F32)
    whole = jnp.concatenate(list(parts) + [blank], axis=0)
    for t in range(tiles):
        turned[t, pl.ds(start, LANES), :] = whole[t * LANES : (t + 1) * LANES].T


def turn_out(turned, start, rows, comps):
    tiles = turned.shape[0]
    whole = jnp.concatenate([turned[t, pl.ds(start, LANES), :].T for t in range(tiles)], axis=0)
    return [whole[c * rows : (c + 1) * rows] for c in range(comps)]


def fetch(sems, *pairs, start=True):
    copies = [pltpu.make_async_copy(source, target, sems.at[k]) for k, (source, target) in enumerate(pairs)]
    if start:
        start_all(copies)
    return copies


def pieces_of(source, target, sems, mirrored):
    far = source.shape[0]
    size = far // PIECES if mirrored is None else far // 2 // PIECES
    found = []
    for piece in range(PIECES):
        starts = [piece * size]
        if mirrored is not None:
            starts.append(far - (piece + 1) * size if mirrored else far // 2 + piece * size)
        found.append(
            [
                pltpu.make_async_copy(
                    source.at[pl.ds(start, size)], target.at[pl.ds(start, size)], sems.at[piece + k * PIECES]
                )
                for k, start in enumerate(starts)
            ]
        )
    return found


def start_all(copies):
    for copy in copies:
        copy.start()


def wait_all(copies):
    for copy in copies:
        copy.wait()


def y_forward_kernel(flags, field, table_far, out_far, turned, sections, packed, table, out, table_sems, out_sems):
    comps, _, length = field.shape
    (got_table,) = fetch(table_sems, (table_far, table))

    def load(q, carry):
        start = pl.multiple_of(q * LANES, LANES)
        turn_in([field[c, :, pl.ds(start, LANES)] for c in range(comps)], turned, start)
        return carry

    lax.fori_loop(0, length // LANES, load, 0, unroll=4)
    give = pieces_of(out, out_far, out_sems, None)
    leave = lambda piece: start_all(give[piece])
    forward_rows(turned, table, flags[0], sections, packed, out, got_table.wait, deliver_near, leave)
    for copies in give:
        wait_all(copies)


def y_middle_kernel(
    prestress_far, slip_far, rate_far, inverse_far, forward_far, arrived_far, out_far, stress_far, *rest
):
    turned, even, odd, mixed, sections, packed, inverse, forward, prestress, slip, rate, stress, *rest = rest
    arrived, out, sems, in_sems, out_sems, inverse_sems, forward_sems = rest
    comps, rows, length = prestress.shape
    take = pieces_of(arrived_far, arrived, in_sems, False)
    for copies in take:
        start_all(copies)
    slip_used = slip_far.at[: slip.shape[0]]
    (got_inverse,) = fetch(inverse_sems, (inverse_far, inverse))
    got = fetch(sems, (prestress_far, prestress), (slip_used, slip), (rate_far, rate), start=False)
    (got_forward,) = fetch(forward_sems, (forward_far, forward), start=False)

    def arrive(piece):
        wait_all(take[piece])
        if piece == PIECES - 1:
            start_all(got)

    def ready():
        got_inverse.wait()
        got_forward.start()

    inverse_rows(arrived, inverse, even, odd, mixed, turned, ready, collect_halves, arrive)
    wait_all(got)

    def step(q, carry):
        start = pl.multiple_of(q * LANES, LANES)
        lanes = pl.ds(start, LANES)
        parts = turn_out(turned, start, rows, comps)
        s = [prestress[c, :, lanes] + parts[c] for c in range(comps)]
        for c in range(comps):
            stress[c, :, lanes] = s[c]
        first = friction(*s, slip[0, :, lanes], slip[1, :, lanes])
        turn_in([(first[c] - rate[c, :, lanes]) * 0.5 for c in range(comps)], turned, start)
        return carry

    lax.fori_loop(0, length // LANES, step, 0, unroll=2)
    give_stress = pltpu.make_async_copy(stress, stress_far, sems.at[3])
    give_stress.start()
    deliver = functools.partial(deliver_far, rows)
    give = pieces_of(out, out_far, out_sems, True)
    leave = lambda piece: start_all(give[piece])
    forward_rows(turned, forward, None, sections, packed, out, got_forward.wait, deliver, leave)
    give_stress.wait()
    for copies in give:
        wait_all(copies)


def y_final_kernel(stress_far, slip_far, rate_far, inverse_far, arrived_far, new_rate_far, new_slip_far, *rest):
    turned, even, mixed, inverse, stress, slip, rate, new_rate, new_slip, arrived, sems, in_sems, out_sems, inverse_sems = rest
    comps, rows, length = stress.shape
    take = pieces_of(arrived_far, arrived, in_sems, True)
    for copies in take:
        start_all(copies)
    (got_inverse,) = fetch(inverse_sems, (inverse_far, inverse))
    got = fetch(sems, (stress_far, stress), (slip_far, slip), (rate_far, rate), start=False)
    collect = functools.partial(collect_far, rows)

    def arrive(piece):
        wait_all(take[piece])
        if piece == PIECES - 1:
            start_all(got)

    inverse_rows(arrived, inverse, even, even, mixed, turned, got_inverse.wait, collect, arrive)
    wait_all(got)

    def step(q, carry):
        start = pl.multiple_of(q * LANES, LANES)
        lanes = pl.ds(start, LANES)
        parts = turn_out(turned, start, rows, comps)
        s = [stress[c, :, lanes] + parts[c] for c in range(comps)]
        second = friction(*s, slip[0, :, lanes], slip[1, :, lanes])
        for c in range(comps):
            new_rate[c, :, lanes] = second[c]
            new_slip[c, :, lanes] = slip[c, :, lanes] + 0.25 * (rate[c, :, lanes] + second[c])
        return carry

    size = length // LANES // PIECES
    give = []
    for piece in range(PIECES):
        lax.fori_loop(piece * size, (piece + 1) * size, step, 0, unroll=2)
        lanes = pl.ds(piece * size * LANES, size * LANES)
        for k, (near, far) in enumerate(((new_rate, new_rate_far), (new_slip, new_slip_far))):
            give.append(
                pltpu.make_async_copy(near.at[:, :, lanes], far.at[:, :, lanes], out_sems.at[2 * piece + k])
            )
            give[-1].start()
    wait_all(give)


def inverse_eight(z, turn):
    def four(a, b, c, d):
        t0, t1, t2, t3 = a + c, a - c, b + d, turn(b - d)
        return t0 + t2, t1 + t3, t0 - t2, t1 - t3

    e = four(z[0], z[2], z[4], z[6])
    o = four(z[1], z[3], z[5], z[7])
    o1 = (o[1] + turn(o[1])) * ROOT
    o3 = (turn(o[3]) - o[3]) * ROOT
    turned = (o[0], o1, turn(o[2]), o3)
    return [e[k] + turned[k] for k in range(4)] + [e[k] - turned[k] for k in range(4)]


def x_core(load, store, copies, forward, inverse, weight, past, sections, mixed):
    tiles, wide, _ = weight.shape
    count = wide // RADIX
    got_forward, got_filter, got_inverse = copies
    wait_all(got_forward)
    start_all(got_filter)
    for j in range(RADIX):
        sections[j] = dot3(forward[j], load(j))
    wait_all(got_filter)
    got_inverse.start()
    sign = jnp.where(lax.broadcasted_iota(jnp.int32, (1, LANES), 1) < LANES // 2, -1.0, 1.0).astype(F32)

    def turn(value):
        return sign * pltpu.roll(value, LANES // 2, 1)

    def chunk(q, carry):
        row = pl.multiple_of(q * 8, 8)
        for t in range(tiles):
            lanes = slice(t * LANES, (t + 1) * LANES)
            parts = parts_of(sections, row, count, lanes)
            z = []
            for k2, found in enumerate(forward_eight(parts, RADIX)):
                spot = pl.ds(row + k2 * count, 8)
                w = weight[t, spot, :]
                value = w * found[0] + turn(w * found[1])
                z.append(value if past is None else value + past[t, spot, :])
            for j, value in enumerate(inverse_eight(z, turn)):
                mixed[j, pl.ds(row, 8), lanes] = value
        return carry

    lax.fori_loop(0, count // 8, chunk, 0, unroll=4)
    got_inverse.wait()
    for j in range(RADIX):
        both = dot3(inverse[j], mixed[j])
        spots = [slice(t * LANES, (t + 1) * LANES) for t in range(tiles)]
        store(j, [both[:count, lanes] + turn(both[count:, lanes]) for lanes in spots])


def x_kernel(arrived_far, forward_far, inverse_far, weight_far, past_far, out, *rest):
    arrived, sections, mixed, forward, inverse, weight, past, sems, forward_sems, inverse_sems = rest
    near, comps, rows, _ = arrived.shape
    far = out.shape[0]
    got_forward = fetch(forward_sems, (forward_far, forward), (arrived_far, arrived))
    got = fetch(sems, (weight_far, weight), (past_far, past), start=False)
    (got_inverse,) = fetch(inverse_sems, (inverse_far, inverse), start=False)
    step = rows // RADIX

    def load(j):
        spot = pl.ds(j, step, stride=RADIX)
        parts = [jnp.concatenate([arrived[src, c, spot, :] for src in range(near)], axis=0) for c in range(comps)]
        return jnp.concatenate(parts, axis=1)

    def store(j, values):
        spot = pl.ds(j, step, stride=RADIX)
        for c, value in enumerate(values):
            for dest in range(far):
                out[dest, c, spot, :] = value[dest * step : (dest + 1) * step]

    x_core(load, store, (got_forward, got, got_inverse), forward, inverse, weight, past, sections, mixed)


def x_far_kernel(arrived_far, forward_far, inverse_far, weight_far, out, *rest):
    arrived, sections, mixed, forward, inverse, weight, sems, forward_sems, inverse_sems = rest
    got_forward = fetch(forward_sems, (forward_far, forward), (arrived_far, arrived))
    got = fetch(sems, (weight_far, weight), start=False)
    (got_inverse,) = fetch(inverse_sems, (inverse_far, inverse), start=False)
    half = weight.shape[1] // RADIX // 2

    def spot_of(c, j):
        return pl.ds(c * RADIX + j, half, stride=3 * RADIX)

    def load(j):
        x0, x1, x2 = (arrived[spot_of(c, j), :] for c in range(3))
        none = jnp.zeros_like(x2)
        left = jnp.concatenate([join(x0, x1), join_second(x0, x1)], axis=0)
        right = jnp.concatenate([join(x2, none), join_second(x2, none)], axis=0)
        return jnp.concatenate([left, right], axis=1)

    def store(j, values):
        (a, b), (c, d) = ((value[:half], value[half:]) for value in values)
        out[spot_of(0, j), :] = join(a, b)
        out[spot_of(1, j), :] = join_second(a, b)
        out[spot_of(2, j), :] = join(c, d)

    x_core(load, store, (got_forward, got, got_inverse), forward, inverse, weight, None, sections, mixed)


def pick(values, bits):
    level = 0
    while len(values) > 1:
        if len(values) % 2:
            values = values + [values[-1]]
        values = [jnp.where(bits[level], values[k + 1], values[k]) for k in range(0, len(values), 2)]
        level += 1
    return values[0]


def bits_of(band, bands):
    return [(band & (1 << level)) != 0 for level in range(max((bands - 1).bit_length(), 1))]


def weights_past(table, band, bits, c, depth):
    bands, lags, comps = table.shape[0], table.shape[1] // 3, 3
    found = []
    for at in range(depth):
        spot = (lags - depth + at) * comps + c
        if lags - depth + at < SHORT:
            found.append(pick([table[b, spot] for b in range(bands)], bits))
        else:
            found.append(jnp.where(band == 0, table[0, spot], 0.0))
    return found


def history_kernel(flags, table, band, band_back, band_edge, history, past_back, past_edge, flip, past, stacked):
    bands, comps = table.shape[0], 3
    depth = history.shape[0]
    rows, width = band.shape

    def group(q, carry):
        spot = pl.ds(pl.multiple_of(q * 16, 16), 16)
        own = band[spot, :]
        bits = bits_of(own, bands)
        for c in range(comps):
            sums = [jnp.zeros((16, width), F32) for _ in range(2)]
            for at, w in enumerate(weights_past(table, own, bits, c, depth)):
                for p in range(2):
                    sums[p] = sums[p] + w * history[at, c, p, spot, :].astype(F32)
            for p in range(2):
                stacked[c, pl.ds(pl.multiple_of(q * 16 + p * rows, 16), 16), :] = sums[p]
        return carry

    lax.fori_loop(0, rows // 16, group, 0)

    edge = flags[1] > 0.0
    there, beyond = [], []
    for at in range(depth):
        for c in range(comps):
            for p in range(2):
                there.append(past_back[at, c, p].astype(F32)[:1])
                beyond.append(past_edge[at, c, p].astype(F32)[:1])
    count = len(there)
    blank = -(count + 1) % 16
    there += [band_back[...].astype(F32)[:1], jnp.zeros((blank, width), F32)]
    beyond += [band_edge[...].astype(F32)[:1], jnp.zeros((blank, LANES), F32)]
    both = [jnp.concatenate(rows_of, axis=0).astype(BF16) for rows_of in (there, beyond)]
    row_back = jnp.dot(jnp.concatenate(both, axis=1), flip[...], preferred_element_type=F32)
    back = row_back[count : count + 1].astype(jnp.int32)
    bits = bits_of(back, bands)
    for c in range(comps):
        found = weights_past(table, back, bits, c, depth)
        for p in range(2):
            reverse = jnp.zeros((1, width), F32)
            for at, w in enumerate(found):
                spot = (at * comps + c) * 2 + p
                reverse = reverse + w * row_back[spot : spot + 1, :]
            if p:
                reverse = -reverse
            mine = stacked[c, p * rows : p * rows + 1, :]
            stacked[c, p * rows : p * rows + 1, :] = jnp.where(edge, 0.5 * (mine + reverse), mine)
        for t in range(width // LANES):
            spot = pl.ds(t * LANES, LANES)
            past[c, spot, :] = stacked[c, :, spot].T


def weight_kernel(flags, table, band, few, block, few_back, block_edge, few_edge, flip, swap, out, stacked):
    bands, comps = table.shape
    rows, width = band.shape
    odd = (lax.broadcasted_iota(jnp.int32, (1, width), 1) & 1) == 1
    parity = jnp.where(odd, flags[0], 1.0).astype(F32)
    edge = flags[1] > 0.0

    def exact(values):
        return values.astype(F32).astype(BF16)

    there = jnp.concatenate([exact(block[...]), exact(few_back[...])], axis=0)
    beyond = jnp.concatenate([exact(block_edge[...]), exact(few_edge[...])], axis=0)
    turned = jnp.dot(jnp.concatenate([there, beyond], axis=1), flip[...], preferred_element_type=F32)
    turned = jnp.dot(swap[...], turned.astype(BF16), preferred_element_type=F32).astype(jnp.int32)
    tiles = out.shape[0]
    slots = LANES // 2 // rows
    if tiles * slots > comps:
        stacked[tiles - 1] = jnp.zeros((LANES, width), F32)
    for c in range(comps):
        tile, re = c // slots, c % slots * rows
        im = re + LANES // 2
        values = [table[b, c] for b in range(bands)]
        for q in range(rows // 8):
            spot = slice(q * 8, q * 8 + 8)
            value = pick(values, bits_of(band[spot, :], bands)) + pick(values, bits_of(turned[spot], bands))
            value = value * parity
            if q == 0:
                first = lax.broadcasted_iota(jnp.int32, (8, width), 0) == 0
                other = pick(values, bits_of(few[1:2, :], bands))
                other = other + pick(values, bits_of(turned[rows : rows + 1], bands))
                other = jnp.where(edge, 0.5 * (other * parity), value[:1])
                value = jnp.where(first & edge, 0.5 * value, value)
                stacked[tile, im : im + 8, :] = jnp.where(first, other, value)
            else:
                stacked[tile, im + q * 8 : im + q * 8 + 8, :] = value
            stacked[tile, re + q * 8 : re + q * 8 + 8, :] = value
    for tile in range(tiles):
        for t in range(width // LANES):
            spot = slice(t * LANES, (t + 1) * LANES)
            out[tile, spot, :] = stacked[tile, :, spot].T


VMEM = pl.BlockSpec(memory_space=pltpu.VMEM)
SMEM = pl.BlockSpec(memory_space=pltpu.SMEM)
ANY = pl.BlockSpec(memory_space=pl.ANY)
PARAMS = pltpu.CompilerParams(vmem_limit_bytes=52 * 1024 * 1024)
SMALL = pltpu.CompilerParams(vmem_limit_bytes=52 * 1024 * 1024)


def y_scratch(length, modes):
    count = length // RADIX
    near = length // 2 // modes
    wide = 2 * LANES
    turned = pltpu.VMEM((2, length, LANES), F32)
    halves = pltpu.VMEM((near, 2 * modes, wide), F32)
    sections = pltpu.VMEM((RADIX, 2 * count, wide), F32)
    return turned, halves, sections


def took(microseconds):
    return pl.CostEstimate(flops=int(microseconds * 1e9), bytes_accessed=1, transcendentals=0)


def struct(*shape):
    return jax.ShapeDtypeStruct(shape, F32)


def flip_table(chunk):
    flip = np.zeros((chunk + LANES, chunk), np.float32)
    flip[chunk - np.arange(1, chunk), np.arange(1, chunk)] = 1.0
    flip[chunk, 0] = 1.0
    return jnp.asarray(flip.astype(BF16))


def swap_table(modes):
    swap = np.zeros((modes + 16, modes + 16), np.float32)
    swap[np.arange(1, modes), modes - np.arange(1, modes)] = 1.0
    swap[0, modes] = 1.0
    swap[modes, modes + 1] = 1.0
    return jnp.asarray(swap.astype(BF16))


def with_kernels(slip_rate, slip_field, prestress, history, kernel, band_len, mode_band):
    comps, rows, length = slip_rate.shape
    modes, wide = mode_band.shape
    far = lax.axis_size(AXES)
    near = lax.axis_size(NEAR)
    bands, lags = kernel.shape[:2]
    depth = history.shape[0]
    flags, coded, block, few = exchange_bands(kernel, band_len, mode_band)

    y_forward, y_inverse = (jnp.asarray(split_table(t)) for t in tables(length))
    x_forward, x_inverse = tables(wide)
    eights = rows // RADIX
    order = np.arange(wide // RADIX).reshape(far, 2, eights // 2).transpose(1, 0, 2).reshape(-1)
    far_forward = jnp.asarray(split_table(x_forward[:, :, order]))
    both = x_inverse.reshape(RADIX, 2, wide // RADIX, wide // RADIX)[:, :, order]
    far_inverse = jnp.asarray(split_table(both.reshape(x_inverse.shape)))
    x_forward = jnp.asarray(split_table(x_forward[:, :, : wide // RADIX // 2]))
    x_inverse = jnp.asarray(split_table(x_inverse))

    turned, halves, sections = y_scratch(length, modes)
    y_table = pltpu.VMEM(y_forward.shape, BF16)
    field = pltpu.VMEM((comps, rows, length), F32)
    sent = pl.pallas_call(
        y_forward_kernel,
        out_shape=struct(near, comps, rows, 2 * modes),
        in_specs=[SMEM, VMEM, ANY],
        out_specs=ANY,
        scratch_shapes=[turned, sections, halves, y_table, pltpu.VMEM((near, comps, rows, 2 * modes), F32)]
        + [pltpu.SemaphoreType.DMA((1,)), pltpu.SemaphoreType.DMA((PIECES,))],
        compiler_params=PARAMS,
        cost_estimate=took(6),
        name="y_forward",
    )(flags, slip_rate, y_forward)
    here = lax.all_to_all(sent, NEAR, 0, 0, tiled=True)

    chunk = 4 * LANES
    steps = wide // chunk
    back = lambda g: steps - 1 - g
    after = lambda g: (steps - g) % steps * (chunk // LANES)
    flip = flip_table(chunk)
    flip_spec = pl.BlockSpec(flip.shape, lambda g: (0, 0))
    past = pl.pallas_call(
        history_kernel,
        grid=(steps,),
        out_shape=struct(comps, wide, 2 * modes),
        in_specs=[
            SMEM,
            SMEM,
            pl.BlockSpec((modes, chunk), lambda g: (0, g)),
            pl.BlockSpec((8, chunk), lambda g: (0, back(g))),
            pl.BlockSpec((8, LANES), lambda g: (0, after(g))),
            pl.BlockSpec((depth, comps, 2, modes, chunk), lambda g: (0, 0, 0, 0, g)),
            pl.BlockSpec((depth, comps, 2, 16, chunk), lambda g: (0, 0, 0, 0, back(g))),
            pl.BlockSpec((depth, comps, 2, 16, LANES), lambda g: (0, 0, 0, 0, after(g))),
            flip_spec,
        ],
        out_specs=pl.BlockSpec((comps, chunk, 2 * modes), lambda g: (0, g, 0)),
        scratch_shapes=[pltpu.VMEM((comps, 2 * modes, chunk), F32)],
        compiler_params=SMALL,
        cost_estimate=took(7),
        name="history",
    )(flags, coded, mode_band, mode_band, mode_band, history, history, history, flip)

    def weights(marks, table, band, few, block):
        owned = band.shape[0]
        tiles = -(-comps // (LANES // 2 // owned))
        swap = swap_table(owned)
        own = lambda g: (0, g)
        return pl.pallas_call(
            weight_kernel,
            grid=(steps,),
            out_shape=struct(tiles, wide, LANES),
            in_specs=[
                SMEM,
                SMEM,
                pl.BlockSpec((owned, chunk), own),
                pl.BlockSpec((16, chunk), own),
                pl.BlockSpec((owned, chunk), lambda g: (0, back(g))),
                pl.BlockSpec((16, chunk), lambda g: (0, back(g))),
                pl.BlockSpec((owned, LANES), lambda g: (0, after(g))),
                pl.BlockSpec((16, LANES), lambda g: (0, after(g))),
                flip_spec,
                pl.BlockSpec(swap.shape, lambda g: (0, 0)),
            ],
            out_specs=pl.BlockSpec((tiles, chunk, LANES), lambda g: (0, g, 0)),
            scratch_shapes=[pltpu.VMEM((tiles, LANES, chunk), F32)],
            compiler_params=SMALL,
            cost_estimate=took(40),
            name="weights",
        )(marks, table, band, few, block, few, block, few, flip, swap)

    now_weight = weights(flags, coded[:, :comps] + coded[:, comps : 2 * comps], mode_band, few, block)
    lower = flags[0] > 0.0
    part = modes // 2
    band = jnp.where(lower, mode_band[:part], block[part:])
    other = jnp.where(lower, block[part:], mode_band[:part])
    few = jnp.concatenate([jnp.where(lower, few[:1], mode_band[part : part + 1]), few[1:]], axis=0)
    marks = jnp.stack([jnp.ones((), F32), jnp.where(lower, flags[1], 0.0)])
    later_weight = weights(marks, coded[:, :comps], band, few, other)

    count = wide // RADIX

    def x_scratch(given, lanes, *tables):
        return [
            pltpu.VMEM(given.shape, F32),
            pltpu.VMEM((RADIX, 2 * count, lanes), F32),
            pltpu.VMEM((RADIX, count, lanes), F32),
            *(pltpu.VMEM(table.shape, table.dtype) for table in tables),
            pltpu.SemaphoreType.DMA((len(tables) - 2,)),
            pltpu.SemaphoreType.DMA((2,)),
            pltpu.SemaphoreType.DMA((1,)),
        ]

    operands = x_forward, x_inverse, now_weight, past
    sent = pl.pallas_call(
        x_kernel,
        out_shape=struct(far, comps, rows, 2 * modes),
        in_specs=[ANY] * 5,
        out_specs=VMEM,
        scratch_shapes=x_scratch(here, comps * LANES, *operands),
        compiler_params=SMALL,
        cost_estimate=took(12),
        name="x_stage",
    )(here, *operands)
    fields = lax.all_to_all(sent, AXES, 0, 0, tiled=True)
    sent, stress = pl.pallas_call(
        y_middle_kernel,
        out_shape=[struct(far, comps * rows // 2, LANES), struct(comps, rows, length)],
        in_specs=[ANY] * 6,
        out_specs=[ANY] * 2,
        scratch_shapes=[turned, halves, halves, sections, sections, halves, y_table, y_table]
        + [field, pltpu.VMEM((2, rows, length), F32), field, field, pltpu.VMEM(fields.shape, F32)]
        + [pltpu.VMEM((far, comps * rows // 2, LANES), F32), pltpu.SemaphoreType.DMA((4,))]
        + [pltpu.SemaphoreType.DMA((2 * PIECES,))] * 2
        + [pltpu.SemaphoreType.DMA((1,))] * 2,
        compiler_params=PARAMS,
        cost_estimate=took(14),
        name="y_middle",
    )(prestress, slip_field, slip_rate, y_inverse, y_forward, fields)
    here = lax.all_to_all(sent, AXES, 0, 0, tiled=True)
    operands = far_forward, far_inverse, later_weight
    given = here.reshape(-1, LANES)
    sent = pl.pallas_call(
        x_far_kernel,
        out_shape=struct(far * comps * rows // 2, LANES),
        in_specs=[ANY] * 4,
        out_specs=VMEM,
        scratch_shapes=x_scratch(given, 2 * LANES, *operands),
        compiler_params=SMALL,
        cost_estimate=took(8),
        name="x_far",
    )(given, *operands)
    fields = lax.all_to_all(sent.reshape(here.shape), AXES, 0, 0, tiled=True)
    return tuple(
        pl.pallas_call(
            y_final_kernel,
            out_shape=[struct(comps, rows, length)] * 2,
            in_specs=[ANY] * 5,
            out_specs=[ANY] * 2,
            scratch_shapes=[turned, halves, sections, y_table, field, field, field, field, field]
            + [pltpu.VMEM(fields.shape, F32), pltpu.SemaphoreType.DMA((3,))]
            + [pltpu.SemaphoreType.DMA((2 * PIECES,))] * 2
            + [pltpu.SemaphoreType.DMA((1,))],
            compiler_params=PARAMS,
            cost_estimate=took(10),
            name="y_final",
        )(stress, slip_field, slip_rate, y_inverse, fields)
    )


def reverse_modes(values):
    return jnp.roll(jnp.flip(values, -1), 1, -1)


def exchange_bands(kernel, band_len, mode_band):
    bands, lags, comps = kernel.shape
    far = lax.axis_size(AXES)
    near = lax.axis_size(NEAR)
    me = lax.axis_index(AXES)
    first = me % near == 0
    flags = jnp.stack([jnp.where(me < near, 1.0, -1.0), jnp.where(first, 1.0, 0.0)]).astype(F32)
    live = (jnp.arange(lags, dtype=jnp.int32)[None, :] < band_len[:, None]).astype(F32)
    coded = (kernel * live[:, :, None]).reshape(bands, lags * comps)
    block = lax.ppermute(mode_band, AXES, [(d, far - 1 - d) for d in range(far)])
    pairs = [(d, (d + near) % far if d % near == 0 else far - d) for d in range(far)]
    row = lax.ppermute(mode_band[:1], AXES, pairs)
    edge = jnp.where(first, mode_band[:1], row)
    few = jnp.concatenate([edge, row, jnp.zeros((14, mode_band.shape[1]), jnp.int32)], axis=0)
    return flags, coded, block, few


def reverse_first(history, mode_band):
    row_back = reverse_modes(history[:, :, :, 0, :].astype(F32).reshape(-1, mode_band.shape[1]))
    return row_back, reverse_modes(mode_band[:1])


def plain(slip_rate, slip_field, prestress, history, kernel, band_len, mode_band):
    comps, rows, length = slip_rate.shape
    modes, wide = mode_band.shape
    far = lax.axis_size(AXES)
    near = lax.axis_size(NEAR)
    bands, lags = kernel.shape[:2]
    depth = history.shape[0]
    flags, coded, block, few = exchange_bands(kernel, band_len, mode_band)
    row_back, row_mirror = reverse_first(history, mode_band)
    mirror = reverse_modes(jnp.concatenate([few[:1], jnp.flip(block[1:], 0)], axis=0))
    extra = jnp.concatenate([few[1:2], reverse_modes(few[1:2])], axis=0)
    table = coded.reshape(bands, lags, comps)
    edge = flags[1] > 0.0
    top = (jnp.arange(modes) == 0)[None, :, None] & edge

    def dot(spec, a, b):
        return jnp.einsum(spec, a, b, precision=lax.Precision.HIGHEST)

    def angles(first, second, size):
        product = (first[:, None] * second[None, :]) % size
        angle = product.astype(F32) * (2.0 * math.pi / size)
        return jnp.cos(angle) / math.sqrt(size), jnp.sin(angle) / math.sqrt(size)

    def weights(band, values):
        result = jnp.zeros(values.shape[1:] + band.shape, F32)
        for b in range(bands):
            result = jnp.where(band == b, values[b][..., None, None], result)
        return result

    past = []
    for at in range(depth):
        w = weights(mode_band, table[:, lags - depth + at])[:, None]
        past.append(w * history[at].astype(F32))
    past = sum(past)
    back = row_back.reshape(depth, comps, 2, 1, wide)
    w = weights(row_mirror, table[:, lags - depth :])
    back = jnp.sum(w[:, :, None] * back, axis=0) * jnp.array([1.0, -1.0], F32)[:, None, None]
    past = jnp.where(top, 0.5 * (past + back), past)
    parity = jnp.where(jnp.arange(wide) % 2 == 1, flags[0], 1.0)

    def filters(values):
        whole = (weights(mode_band, values) + weights(mirror, values)) * parity
        other = (weights(extra[:1], values) + weights(extra[1:], values)) * parity
        return jnp.where(top, 0.5 * whole, whole), jnp.where(top, 0.5 * other, whole)

    own = jnp.arange(length, dtype=jnp.int32)
    y_cos, y_sin = angles(own, own[: length // 2], length)
    nyquist = jnp.where(own % 2 == 1, -1.0, 1.0).astype(F32) / math.sqrt(length)
    y_sin = y_sin.at[:, 0].set(-nyquist)
    across = jnp.arange(wide, dtype=jnp.int32)
    x_cos, x_sin = angles(across, across, wide)
    flip = jnp.where(own % 2 == 1, flags[0], 1.0)

    def y_forward(field):
        field = field * flip
        both = jnp.stack([dot("cxy,yk->ckx", field, y_cos), -dot("cxy,yk->ckx", field, y_sin)], 1)
        both = both.reshape(comps, 2, near, modes, rows).transpose(2, 0, 4, 1, 3)
        return lax.all_to_all(both, NEAR, 0, 0, tiled=True)

    def x_stage(given, filt, added):
        given = given.transpose(1, 3, 4, 0, 2).reshape(comps, 2, modes, near * rows)
        real = dot("cpkx,xm->cpkm", given, x_cos[: near * rows])
        imag = -dot("cpkx,xm->cpkm", given, x_sin[: near * rows])
        a, b = filt
        out_real = a * real[:, 0] - b * imag[:, 1]
        out_imag = a * imag[:, 0] + b * real[:, 1]
        if added is not None:
            out_real, out_imag = out_real + added[:, 0], out_imag + added[:, 1]
        first = dot("ckm,mx->ckx", out_real, x_cos) - dot("ckm,mx->ckx", out_imag, x_sin)
        second = dot("ckm,mx->ckx", out_real, x_sin) + dot("ckm,mx->ckx", out_imag, x_cos)
        both = jnp.stack([first, second], 1).reshape(comps, 2, modes, far, rows).transpose(3, 0, 4, 1, 2)
        return lax.all_to_all(both, AXES, 0, 0, tiled=True)

    def y_inverse(given):
        given = given.reshape(2, near, comps, rows, 2, modes).transpose(0, 4, 2, 3, 1, 5)
        given = given.reshape(2, 2, comps, rows, length // 2)
        half = dot("hcxk,yk->hcxy", given[:, 0], y_cos) - dot("hcxk,yk->hcxy", given[:, 1], y_sin)
        return half[0] + half[1] * jnp.where(own % 2 == 1, -1.0, 1.0)

    def phi(s):
        return jnp.stack(friction(s[0], s[1], s[2], slip_field[0], slip_field[1]))

    now = filters(table[:, 0] + table[:, 1])
    later = filters(table[:, 0])
    stress = prestress + y_inverse(x_stage(y_forward(slip_rate), now, past))
    shift = 0.5 * (phi(stress) - slip_rate)
    second = phi(stress + y_inverse(x_stage(y_forward(shift), later, None)))
    return second, slip_field + 0.25 * (slip_rate + second)


def solution(mesh):
    shape = mesh.devices.shape
    ours = Mesh(mesh.devices.reshape(2, shape[0] // 2, shape[1]), AXES)

    def on_device(slip_rate, slip_field, prestress, history, kernel, band_len, mode_band):
        args = (slip_rate, slip_field, prestress, history, kernel, band_len, mode_band)
        rows, modes = slip_rate.shape[1], mode_band.shape[0]
        near = lax.axis_size(NEAR)
        if 2 * modes == LANES and 2 * rows == LANES and near % PIECES == 0 and slip_rate.shape[0] == 3:
            return with_kernels(*args)
        return plain(*args)

    rows = P(None, AXES, None)
    return jax.shard_map(
        on_device,
        mesh=ours,
        in_specs=(rows, rows, rows, P(None, None, None, AXES, None), P(), P(), P(AXES, None)),
        out_specs=(rows, rows),
        check_vma=False,
    )
```

```python
import functools
import math

import jax
import jax.numpy as jnp
import numpy as np
from jax import lax
from jax.experimental import pallas as pl
from jax.experimental.pallas import tpu as pltpu
from jax.sharding import Mesh, PartitionSpec as P


LANES = 128
RADIX = 8
SHORT = 4
AXES = ("half", "part", "ky")
NEAR = ("part", "ky")
F32 = jnp.float32
BF16 = jnp.bfloat16
ROOT = math.sqrt(0.5)
PIECES = 4

static_fric = 0.7
dynamic_fric = 0.35
weaken_slip = 0.5


def softplus(value):
    return jnp.maximum(value, 0.0) + jnp.log1p(jnp.exp(-jnp.abs(value)))


def friction(s0, s1, s2, u0, u1):
    worn = jnp.sqrt(u0 * u0 + u1 * u1 + 1.0) - 1.0
    coeff = dynamic_fric + (static_fric - dynamic_fric) * jnp.exp(worn * (-1.0 / weaken_slip))
    tail = jnp.log1p(jnp.exp(-jnp.abs(s2)))
    strength = coeff * (jnp.maximum(-s2, 0.0) + tail)
    magnitude = jnp.sqrt(s0 * s0 + s1 * s1 + 1.0)
    ratio = softplus(magnitude - strength) / magnitude
    return ratio * s0, ratio * s1, jnp.maximum(s2, 0.0) + tail


def split_table(values):
    high = values.astype(BF16)
    low = (values - high.astype(np.float64)).astype(BF16)
    return np.concatenate([high, low], axis=-1)


def tables(length):
    count = length // RADIX
    outer = np.arange(count)
    spots = RADIX * outer[None, :, None] + np.arange(RADIX)[:, None, None]
    angle = 2.0 * np.pi / length * ((spots * outer[None, None, :]) % length)
    cos = np.cos(angle) / math.sqrt(length)
    sin = np.sin(angle) / math.sqrt(length)
    forward = np.concatenate([cos.transpose(0, 2, 1), -sin.transpose(0, 2, 1)], axis=1)
    inverse = np.concatenate([cos, sin], axis=1)
    return forward, inverse


def parts_of(sections, row, count, lanes):
    return [(sections[j, pl.ds(row, 8), lanes], sections[j, pl.ds(row + count, 8), lanes]) for j in range(RADIX)]


def dot3(table, values):
    depth = values.shape[0]
    high = values.astype(BF16)
    low = (values - high.astype(F32)).astype(BF16)
    left = jnp.concatenate([table, table[:, :depth]], axis=1)
    right = jnp.concatenate([high, high, low], axis=0)
    return jnp.dot(left, right, preferred_element_type=F32)


def c_add(a, b):
    return a[0] + b[0], a[1] + b[1]


def c_sub(a, b):
    return a[0] - b[0], a[1] - b[1]


def forward_eight(a, wanted):
    def four(p, q, r, s):
        t0, t1, t2 = c_add(p, r), c_sub(p, r), c_add(q, s)
        d = c_sub(q, s)
        t3 = (d[1], -d[0])
        return c_add(t0, t2), c_add(t1, t3), c_sub(t0, t2), c_sub(t1, t3)

    even = four(a[0], a[2], a[4], a[6])
    odd = four(a[1], a[3], a[5], a[7])
    o1 = ((odd[1][0] + odd[1][1]) * ROOT, (odd[1][1] - odd[1][0]) * ROOT)
    o2 = (odd[2][1], -odd[2][0])
    o3 = ((odd[3][1] - odd[3][0]) * ROOT, (odd[3][0] + odd[3][1]) * -ROOT)
    turned = (odd[0], o1, o2, o3)
    first = [c_add(even[k], turned[k]) for k in range(4)]
    if wanted <= 4:
        return first
    return first + [c_sub(even[k], turned[k]) for k in range(4)]


def low_half():
    return lax.broadcasted_iota(jnp.int32, (1, LANES), 1) % (LANES // 2) < LANES // 4


def join(a, b):
    return jnp.where(low_half(), a, pltpu.roll(b, LANES // 4, 1))


def join_second(a, b):
    return jnp.where(low_half(), pltpu.roll(a, LANES - LANES // 4, 1), b)


def blocks_of(packed, owner, comps, rows):
    whole = [packed[owner, :, t * LANES : (t + 1) * LANES].T for t in range(packed.shape[2] // LANES)]
    whole = jnp.concatenate(whole, axis=0)
    return [whole[c * rows : (c + 1) * rows] for c in range(comps)]


def deliver_near(packed, owner, out):
    _, comps, rows, _ = out.shape
    for c, block in enumerate(blocks_of(packed, owner, comps, rows)):
        out[owner, c] = block


def deliver_far(rows, packed, owner, out):
    far = out.shape[0]
    comps = 2 * out.shape[1] // rows
    for c, block in enumerate(blocks_of(packed, owner, comps, rows)):
        top, bottom = block[: rows // 2], block[rows // 2 :]
        for device, value in ((owner, join(top, bottom)), (far - 1 - owner, join_second(top, bottom))):
            for m in range(rows // 16):
                out[device, (m * comps + c) * 8 : (m * comps + c) * 8 + 8] = value[m * 8 : m * 8 + 8]


def forward_rows(turned, table, flag, sections, packed, out, ready, deliver, leave):
    tiles, length, _ = turned.shape
    count = length // RADIX
    owners = packed.shape[0]
    modes = packed.shape[1] // 2
    ready()
    for j in range(RADIX):
        piece = jnp.concatenate([turned[t, pl.ds(j, count, stride=RADIX), :] for t in range(tiles)], axis=1)
        if flag is not None and j % 2:
            piece = piece * flag
        sections[j] = dot3(table[j], piece)
    per = modes // 8

    def chunk(q, carry):
        at = q // per
        off = pl.multiple_of((q % per) * 8, 8)
        row = pl.multiple_of(q * 8, 8)
        found = forward_eight(parts_of(sections, row, count, slice(None)), 4)
        for k2 in range(RADIX // 2):
            owner = at + k2 * (count // modes)
            packed[owner, pl.ds(off, 8), :] = found[k2][0]
            packed[owner, pl.ds(off + modes, 8), :] = found[k2][1]
        return carry

    lax.fori_loop(0, count // 8, chunk, 0, unroll=8)
    top = sections[0, 0:1, :]
    for j in range(1, RADIX):
        top = top - sections[j, 0:1, :] if j % 2 else top + sections[j, 0:1, :]
    packed[0, modes : modes + 1, :] = top

    def send(owner, carry):
        deliver(packed, owner, out)
        return carry

    size = owners // PIECES
    for piece in range(PIECES):
        lax.fori_loop(piece * size, (piece + 1) * size, send, 0, unroll=True)
        leave(piece)


def store_turned(store, owner, pieces):
    tiles = store.shape[2] // LANES
    used = sum(piece.shape[0] for piece in pieces)
    whole = jnp.concatenate(list(pieces) + [jnp.zeros((LANES * tiles - used, LANES), F32)], axis=0)
    for t in range(tiles):
        store[owner, :, t * LANES : (t + 1) * LANES] = whole[t * LANES : (t + 1) * LANES].T


def collect_halves(arrived, even, odd, owner):
    far, comps, _, _ = arrived.shape
    mine = [arrived[owner, c] for c in range(comps)]
    other = [arrived[owner + far // 2, c] for c in range(comps)]
    store_turned(even, owner, [a + b for a, b in zip(mine, other)])
    store_turned(odd, owner, [a - b for a, b in zip(mine, other)])


def collect_far(rows, arrived, even, odd, owner):
    far = arrived.shape[0]
    comps = 2 * arrived.shape[1] // rows
    first, second = arrived[owner], arrived[far - 1 - owner]
    halves = join(first, second), join_second(first, second)
    pieces = []
    for c in range(comps):
        for half in halves:
            pieces += [half[(m * comps + c) * 8 : (m * comps + c) * 8 + 8] for m in range(rows // 16)]
    store_turned(even, owner, pieces)


def inverse_rows(arrived, table, even, odd, mixed, turned, ready, collect, arrive):
    near = even.shape[0]
    modes = even.shape[1] // 2
    tiles, length, _ = turned.shape
    count = length // RADIX

    def gather(owner, carry):
        collect(arrived, even, odd, owner)
        return carry

    size = near // PIECES
    for piece in range(PIECES):
        arrive(piece)
        lax.fori_loop(piece * size, (piece + 1) * size, gather, 0, unroll=True)
    per = modes // 8

    def chunk(q, carry):
        at = q // per
        off = pl.multiple_of((q % per) * 8, 8)
        row = pl.multiple_of(q * 8, 8)

        def four(s):
            t0, t1, t2 = c_add(s[0], s[2]), c_sub(s[0], s[2]), c_add(s[1], s[3])
            d = c_sub(s[1], s[3])
            t3 = (-d[1], d[0])
            return c_add(t0, t2), c_add(t1, t3), c_sub(t0, t2), c_sub(t1, t3)

        for first, store in ((0, even), (1, odd)):
            parts = []
            for k2 in range(RADIX // 2):
                owner = at + k2 * (count // modes)
                parts.append((store[owner, pl.ds(off, 8), :], store[owner, pl.ds(off + modes, 8), :]))
            if first:
                p1, p2, p3 = parts[1:]
                parts[1] = ((p1[0] - p1[1]) * ROOT, (p1[0] + p1[1]) * ROOT)
                parts[2] = (-p2[1], p2[0])
                parts[3] = ((p3[0] + p3[1]) * -ROOT, (p3[0] - p3[1]) * ROOT)
            for index, (re, im) in enumerate(four(parts)):
                j = 2 * index + first
                mixed[j, pl.ds(row, 8), :] = re
                mixed[j, pl.ds(row + count, 8), :] = im
        return carry

    lax.fori_loop(0, count // 8, chunk, 0, unroll=8)
    scale = 1.0 / math.sqrt(length)
    ready()
    for j in range(RADIX):
        piece = dot3(table[j, :count], mixed[j, :count, :]) - dot3(table[j, count:], mixed[j, count:, :])
        if j % 2:
            piece = piece - odd[0, modes : modes + 1, :] * scale
        else:
            piece = piece + even[0, modes : modes + 1, :] * scale
        for t in range(tiles):
            turned[t, pl.ds(j, count, stride=RADIX), :] = piece[:, t * LANES : (t + 1) * LANES]


def turn_in(parts, turned, start):
    tiles = turned.shape[0]
    used = sum(part.shape[0] for part in parts)
    blank = jnp.zeros((LANES * tiles - used, LANES), F32)
    whole = jnp.concatenate(list(parts) + [blank], axis=0)
    for t in range(tiles):
        turned[t, pl.ds(start, LANES), :] = whole[t * LANES : (t + 1) * LANES].T


def turn_out(turned, start, rows, comps):
    tiles = turned.shape[0]
    whole = jnp.concatenate([turned[t, pl.ds(start, LANES), :].T for t in range(tiles)], axis=0)
    return [whole[c * rows : (c + 1) * rows] for c in range(comps)]


def fetch(sems, *pairs, start=True):
    copies = [pltpu.make_async_copy(source, target, sems.at[k]) for k, (source, target) in enumerate(pairs)]
    if start:
        start_all(copies)
    return copies


def pieces_of(source, target, sems, mirrored):
    far = source.shape[0]
    size = far // PIECES if mirrored is None else far // 2 // PIECES
    found = []
    for piece in range(PIECES):
        starts = [piece * size]
        if mirrored is not None:
            starts.append(far - (piece + 1) * size if mirrored else far // 2 + piece * size)
        found.append(
            [
                pltpu.make_async_copy(
                    source.at[pl.ds(start, size)], target.at[pl.ds(start, size)], sems.at[piece + k * PIECES]
                )
                for k, start in enumerate(starts)
            ]
        )
    return found


def start_all(copies):
    for copy in copies:
        copy.start()


def wait_all(copies):
    for copy in copies:
        copy.wait()


def y_forward_kernel(flags, field_far, table_far, out_far, turned, sections, packed, table, out, field, *sems):
    table_sems, out_sems = sems
    comps, _, length = field.shape
    got_field, got_table = fetch(table_sems, (field_far, field), (table_far, table))
    got_field.wait()

    def load(q, carry):
        start = pl.multiple_of(q * LANES, LANES)
        turn_in([field[c, :, pl.ds(start, LANES)] for c in range(comps)], turned, start)
        return carry

    lax.fori_loop(0, length // LANES, load, 0, unroll=4)
    give = pieces_of(out, out_far, out_sems, None)
    leave = lambda piece: start_all(give[piece])
    forward_rows(turned, table, flags[0], sections, packed, out, got_table.wait, deliver_near, leave)
    for copies in give:
        wait_all(copies)


def y_middle_kernel(
    prestress_far, slip_far, rate_far, inverse_far, forward_far, arrived_far, out_far, stress_far, *rest
):
    turned, even, odd, mixed, sections, packed, inverse, forward, prestress, slip, rate, stress, *rest = rest
    arrived, out, sems, in_sems, out_sems, inverse_sems, forward_sems = rest
    comps, rows, length = prestress.shape
    take = pieces_of(arrived_far, arrived, in_sems, False)
    for copies in take:
        start_all(copies)
    slip_used = slip_far.at[: slip.shape[0]]
    (got_inverse,) = fetch(inverse_sems, (inverse_far, inverse))
    got = fetch(sems, (prestress_far, prestress), (slip_used, slip), (rate_far, rate), start=False)
    (got_forward,) = fetch(forward_sems, (forward_far, forward), start=False)

    def arrive(piece):
        wait_all(take[piece])
        if piece == PIECES - 1:
            start_all(got)

    def ready():
        got_inverse.wait()
        got_forward.start()

    inverse_rows(arrived, inverse, even, odd, mixed, turned, ready, collect_halves, arrive)
    wait_all(got)

    def step(q, carry):
        start = pl.multiple_of(q * LANES, LANES)
        lanes = pl.ds(start, LANES)
        parts = turn_out(turned, start, rows, comps)
        s = [prestress[c, :, lanes] + parts[c] for c in range(comps)]
        for c in range(comps):
            stress[c, :, lanes] = s[c]
        first = friction(*s, slip[0, :, lanes], slip[1, :, lanes])
        turn_in([(first[c] - rate[c, :, lanes]) * 0.5 for c in range(comps)], turned, start)
        return carry

    lax.fori_loop(0, length // LANES, step, 0, unroll=2)
    give_stress = pltpu.make_async_copy(stress, stress_far, sems.at[3])
    give_stress.start()
    deliver = functools.partial(deliver_far, rows)
    give = pieces_of(out, out_far, out_sems, True)
    leave = lambda piece: start_all(give[piece])
    forward_rows(turned, forward, None, sections, packed, out, got_forward.wait, deliver, leave)
    give_stress.wait()
    for copies in give:
        wait_all(copies)


def y_final_kernel(stress_far, slip_far, rate_far, inverse_far, arrived_far, new_rate_far, new_slip_far, *rest):
    turned, even, mixed, inverse, stress, slip, rate, new_rate, new_slip, arrived, sems, in_sems, out_sems, inverse_sems = rest
    comps, rows, length = stress.shape
    take = pieces_of(arrived_far, arrived, in_sems, True)
    for copies in take:
        start_all(copies)
    (got_inverse,) = fetch(inverse_sems, (inverse_far, inverse))
    got = fetch(sems, (stress_far, stress), (slip_far, slip), (rate_far, rate), start=False)
    collect = functools.partial(collect_far, rows)

    def arrive(piece):
        wait_all(take[piece])
        if piece == PIECES - 1:
            start_all(got)

    inverse_rows(arrived, inverse, even, even, mixed, turned, got_inverse.wait, collect, arrive)
    wait_all(got)

    def step(q, carry):
        start = pl.multiple_of(q * LANES, LANES)
        lanes = pl.ds(start, LANES)
        parts = turn_out(turned, start, rows, comps)
        s = [stress[c, :, lanes] + parts[c] for c in range(comps)]
        second = friction(*s, slip[0, :, lanes], slip[1, :, lanes])
        for c in range(comps):
            new_rate[c, :, lanes] = second[c]
            new_slip[c, :, lanes] = slip[c, :, lanes] + 0.25 * (rate[c, :, lanes] + second[c])
        return carry

    size = length // LANES // PIECES
    give = []
    for piece in range(PIECES):
        lax.fori_loop(piece * size, (piece + 1) * size, step, 0, unroll=2)
        lanes = pl.ds(piece * size * LANES, size * LANES)
        for k, (near, far) in enumerate(((new_rate, new_rate_far), (new_slip, new_slip_far))):
            give.append(
                pltpu.make_async_copy(near.at[:, :, lanes], far.at[:, :, lanes], out_sems.at[2 * piece + k])
            )
            give[-1].start()
    wait_all(give)


def inverse_eight(z, turn):
    def four(a, b, c, d):
        t0, t1, t2, t3 = a + c, a - c, b + d, turn(b - d)
        return t0 + t2, t1 + t3, t0 - t2, t1 - t3

    e = four(z[0], z[2], z[4], z[6])
    o = four(z[1], z[3], z[5], z[7])
    o1 = (o[1] + turn(o[1])) * ROOT
    o3 = (turn(o[3]) - o[3]) * ROOT
    turned = (o[0], o1, turn(o[2]), o3)
    return [e[k] + turned[k] for k in range(4)] + [e[k] - turned[k] for k in range(4)]


def x_core(load, store, leave, copies, forward, inverse, weight, past, sections, mixed):
    tiles, wide, _ = weight.shape
    count = wide // RADIX
    got_forward, got_filter, got_inverse = copies
    wait_all(got_forward)
    start_all(got_filter)
    for j in range(RADIX):
        sections[j] = dot3(forward[j], load(j))
    wait_all(got_filter)
    got_inverse.start()
    sign = jnp.where(lax.broadcasted_iota(jnp.int32, (1, LANES), 1) < LANES // 2, -1.0, 1.0).astype(F32)

    def turn(value):
        return sign * pltpu.roll(value, LANES // 2, 1)

    def chunk(q, carry):
        row = pl.multiple_of(q * 8, 8)
        for t in range(tiles):
            lanes = slice(t * LANES, (t + 1) * LANES)
            parts = parts_of(sections, row, count, lanes)
            z = []
            for k2, found in enumerate(forward_eight(parts, RADIX)):
                spot = pl.ds(row + k2 * count, 8)
                w = weight[t, spot, :]
                value = w * found[0] + turn(w * found[1])
                z.append(value if past is None else value + past[t, spot, :])
            for j, value in enumerate(inverse_eight(z, turn)):
                mixed[j, pl.ds(row, 8), lanes] = value
        return carry

    lax.fori_loop(0, count // 8, chunk, 0, unroll=4)
    got_inverse.wait()
    for first in range(0, tiles, 2):
        last = min(first + 2, tiles)
        for j in range(RADIX):
            both = dot3(inverse[j], mixed[j, :, first * LANES : last * LANES])
            spots = [slice(t * LANES, (t + 1) * LANES) for t in range(last - first)]
            store(j, first, [both[:count, lanes] + turn(both[count:, lanes]) for lanes in spots])
        leave(first)


def x_kernel(arrived_far, forward_far, inverse_far, weight_far, past_far, out_far, *rest):
    arrived, sections, mixed, forward, inverse, weight, past, sems, forward_sems, inverse_sems, out, out_sems = rest
    near, comps, rows, _ = arrived.shape
    far = out.shape[0]
    got_forward = fetch(forward_sems, (forward_far, forward), (arrived_far, arrived))
    got = fetch(sems, (weight_far, weight), (past_far, past), start=False)
    (got_inverse,) = fetch(inverse_sems, (inverse_far, inverse), start=False)
    step = rows // RADIX

    def load(j):
        spot = pl.ds(j, step, stride=RADIX)
        parts = [jnp.concatenate([arrived[src, c, spot, :] for src in range(near)], axis=0) for c in range(comps)]
        return jnp.concatenate(parts, axis=1)

    def store(j, first, values):
        spot = pl.ds(j, step, stride=RADIX)
        for c, value in enumerate(values, first):
            for dest in range(far):
                out[dest, c, spot, :] = value[dest * step : (dest + 1) * step]

    give = []

    def leave(first):
        group = pl.ds(first, min(2, comps - first))
        give.append(pltpu.make_async_copy(out.at[:, group], out_far.at[:, group], out_sems.at[len(give)]))
        give[-1].start()

    x_core(load, store, leave, (got_forward, got, got_inverse), forward, inverse, weight, past, sections, mixed)
    wait_all(give)


def x_far_kernel(arrived_far, forward_far, inverse_far, weight_far, out, *rest):
    arrived, sections, mixed, forward, inverse, weight, sems, forward_sems, inverse_sems = rest
    got_forward = fetch(forward_sems, (forward_far, forward), (arrived_far, arrived))
    got = fetch(sems, (weight_far, weight), start=False)
    (got_inverse,) = fetch(inverse_sems, (inverse_far, inverse), start=False)
    half = weight.shape[1] // RADIX // 2

    def spot_of(c, j):
        return pl.ds(c * RADIX + j, half, stride=3 * RADIX)

    def load(j):
        x0, x1, x2 = (arrived[spot_of(c, j), :] for c in range(3))
        none = jnp.zeros_like(x2)
        left = jnp.concatenate([join(x0, x1), join_second(x0, x1)], axis=0)
        right = jnp.concatenate([join(x2, none), join_second(x2, none)], axis=0)
        return jnp.concatenate([left, right], axis=1)

    def leave(first):
        pass

    def store(j, first, values):
        (a, b), (c, d) = ((value[:half], value[half:]) for value in values)
        out[spot_of(0, j), :] = join(a, b)
        out[spot_of(1, j), :] = join_second(a, b)
        out[spot_of(2, j), :] = join(c, d)

    x_core(load, store, leave, (got_forward, got, got_inverse), forward, inverse, weight, None, sections, mixed)


def pick(values, bits):
    level = 0
    while len(values) > 1:
        if len(values) % 2:
            values = values + [values[-1]]
        values = [jnp.where(bits[level], values[k + 1], values[k]) for k in range(0, len(values), 2)]
        level += 1
    return values[0]


def bits_of(band, bands):
    return [(band & (1 << level)) != 0 for level in range(max((bands - 1).bit_length(), 1))]


def weights_past(table, band, bits, c, depth):
    bands, lags, comps = table.shape[0], table.shape[1] // 3, 3
    found = []
    for at in range(depth):
        spot = (lags - depth + at) * comps + c
        if lags - depth + at < SHORT:
            found.append(pick([table[b, spot] for b in range(bands)], bits))
        else:
            found.append(jnp.where(band == 0, table[0, spot], 0.0))
    return found


def history_kernel(flags, table, band, band_back, band_edge, history, past_back, past_edge, flip, past, stacked):
    bands, comps = table.shape[0], 3
    depth = history.shape[0]
    rows, width = band.shape

    def group(q, carry):
        spot = pl.ds(pl.multiple_of(q * 16, 16), 16)
        own = band[spot, :]
        bits = bits_of(own, bands)
        for c in range(comps):
            sums = [jnp.zeros((16, width), F32) for _ in range(2)]
            for at, w in enumerate(weights_past(table, own, bits, c, depth)):
                for p in range(2):
                    sums[p] = sums[p] + w * history[at, c, p, spot, :].astype(F32)
            for p in range(2):
                stacked[c, pl.ds(pl.multiple_of(q * 16 + p * rows, 16), 16), :] = sums[p]
        return carry

    lax.fori_loop(0, rows // 16, group, 0)

    edge = flags[1] > 0.0
    there, beyond = [], []
    for at in range(depth):
        for c in range(comps):
            for p in range(2):
                there.append(past_back[at, c, p].astype(F32)[:1])
                beyond.append(past_edge[at, c, p].astype(F32)[:1])
    count = len(there)
    blank = -(count + 1) % 16
    there += [band_back[...].astype(F32)[:1], jnp.zeros((blank, width), F32)]
    beyond += [band_edge[...].astype(F32)[:1], jnp.zeros((blank, LANES), F32)]
    both = [jnp.concatenate(rows_of, axis=0).astype(BF16) for rows_of in (there, beyond)]
    row_back = jnp.dot(jnp.concatenate(both, axis=1), flip[...], preferred_element_type=F32)
    back = row_back[count : count + 1].astype(jnp.int32)
    bits = bits_of(back, bands)
    for c in range(comps):
        found = weights_past(table, back, bits, c, depth)
        for p in range(2):
            reverse = jnp.zeros((1, width), F32)
            for at, w in enumerate(found):
                spot = (at * comps + c) * 2 + p
                reverse = reverse + w * row_back[spot : spot + 1, :]
            if p:
                reverse = -reverse
            mine = stacked[c, p * rows : p * rows + 1, :]
            stacked[c, p * rows : p * rows + 1, :] = jnp.where(edge, 0.5 * (mine + reverse), mine)
        for t in range(width // LANES):
            spot = pl.ds(t * LANES, LANES)
            past[c, spot, :] = stacked[c, :, spot].T


def weight_kernel(flags, table, band, few, block, few_back, block_edge, few_edge, flip, swap, out, stacked):
    bands, comps = table.shape
    rows, width = band.shape
    odd = (lax.broadcasted_iota(jnp.int32, (1, width), 1) & 1) == 1
    parity = jnp.where(odd, flags[0], 1.0).astype(F32)
    edge = flags[1] > 0.0

    def exact(values):
        return values.astype(F32).astype(BF16)

    there = jnp.concatenate([exact(block[...]), exact(few_back[...])], axis=0)
    beyond = jnp.concatenate([exact(block_edge[...]), exact(few_edge[...])], axis=0)
    turned = jnp.dot(jnp.concatenate([there, beyond], axis=1), flip[...], preferred_element_type=F32)
    turned = jnp.dot(swap[...], turned.astype(BF16), preferred_element_type=F32).astype(jnp.int32)
    tiles = out.shape[0]
    slots = LANES // 2 // rows
    if tiles * slots > comps:
        stacked[tiles - 1] = jnp.zeros((LANES, width), F32)
    for c in range(comps):
        tile, re = c // slots, c % slots * rows
        im = re + LANES // 2
        values = [table[b, c] for b in range(bands)]
        for q in range(rows // 8):
            spot = slice(q * 8, q * 8 + 8)
            value = pick(values, bits_of(band[spot, :], bands)) + pick(values, bits_of(turned[spot], bands))
            value = value * parity
            if q == 0:
                first = lax.broadcasted_iota(jnp.int32, (8, width), 0) == 0
                other = pick(values, bits_of(few[1:2, :], bands))
                other = other + pick(values, bits_of(turned[rows : rows + 1], bands))
                other = jnp.where(edge, 0.5 * (other * parity), value[:1])
                value = jnp.where(first & edge, 0.5 * value, value)
                stacked[tile, im : im + 8, :] = jnp.where(first, other, value)
            else:
                stacked[tile, im + q * 8 : im + q * 8 + 8, :] = value
            stacked[tile, re + q * 8 : re + q * 8 + 8, :] = value
    for tile in range(tiles):
        for t in range(width // LANES):
            spot = slice(t * LANES, (t + 1) * LANES)
            out[tile, spot, :] = stacked[tile, :, spot].T


VMEM = pl.BlockSpec(memory_space=pltpu.VMEM)
SMEM = pl.BlockSpec(memory_space=pltpu.SMEM)
ANY = pl.BlockSpec(memory_space=pl.ANY)
PARAMS = pltpu.CompilerParams(vmem_limit_bytes=60 * 1024 * 1024)
SMALL = pltpu.CompilerParams(vmem_limit_bytes=52 * 1024 * 1024)


def y_scratch(length, modes):
    count = length // RADIX
    near = length // 2 // modes
    wide = 2 * LANES
    turned = pltpu.VMEM((2, length, LANES), F32)
    halves = pltpu.VMEM((near, 2 * modes, wide), F32)
    sections = pltpu.VMEM((RADIX, 2 * count, wide), F32)
    return turned, halves, sections


def took(microseconds):
    return pl.CostEstimate(flops=int(microseconds * 1e9), bytes_accessed=1, transcendentals=0)


def struct(*shape):
    return jax.ShapeDtypeStruct(shape, F32)


def flip_table(chunk):
    flip = np.zeros((chunk + LANES, chunk), np.float32)
    flip[chunk - np.arange(1, chunk), np.arange(1, chunk)] = 1.0
    flip[chunk, 0] = 1.0
    return jnp.asarray(flip.astype(BF16))


def swap_table(modes):
    swap = np.zeros((modes + 16, modes + 16), np.float32)
    swap[np.arange(1, modes), modes - np.arange(1, modes)] = 1.0
    swap[0, modes] = 1.0
    swap[modes, modes + 1] = 1.0
    return jnp.asarray(swap.astype(BF16))


def with_kernels(slip_rate, slip_field, prestress, history, kernel, band_len, mode_band):
    comps, rows, length = slip_rate.shape
    modes, wide = mode_band.shape
    far = lax.axis_size(AXES)
    near = lax.axis_size(NEAR)
    bands, lags = kernel.shape[:2]
    depth = history.shape[0]
    flags, coded, block = exchange_bands(kernel, band_len, mode_band)
    few = exchange_edges(mode_band[:1])

    y_forward, y_inverse = (jnp.asarray(split_table(t)) for t in tables(length))
    x_forward, x_inverse = tables(wide)
    eights = rows // RADIX
    order = np.arange(wide // RADIX).reshape(far, 2, eights // 2).transpose(1, 0, 2).reshape(-1)
    far_forward = jnp.asarray(split_table(x_forward[:, :, order]))
    both = x_inverse.reshape(RADIX, 2, wide // RADIX, wide // RADIX)[:, :, order]
    far_inverse = jnp.asarray(split_table(both.reshape(x_inverse.shape)))
    x_forward = jnp.asarray(split_table(x_forward[:, :, : wide // RADIX // 2]))
    x_inverse = jnp.asarray(split_table(x_inverse))

    turned, halves, sections = y_scratch(length, modes)
    y_table = pltpu.VMEM(y_forward.shape, BF16)
    field = pltpu.VMEM((comps, rows, length), F32)
    sent = pl.pallas_call(
        y_forward_kernel,
        out_shape=struct(near, comps, rows, 2 * modes),
        in_specs=[SMEM, ANY, ANY],
        out_specs=ANY,
        scratch_shapes=[turned, sections, halves, y_table, pltpu.VMEM((near, comps, rows, 2 * modes), F32)]
        + [field, pltpu.SemaphoreType.DMA((2,)), pltpu.SemaphoreType.DMA((PIECES,))],
        compiler_params=PARAMS,
        cost_estimate=took(6),
        name="y_forward",
    )(flags, slip_rate, y_forward)
    here = lax.all_to_all(sent, NEAR, 0, 0, tiled=True)

    chunk = 4 * LANES
    steps = wide // chunk
    back = lambda g: steps - 1 - g
    after = lambda g: (steps - g) % steps * (chunk // LANES)
    flip = flip_table(chunk)
    flip_spec = pl.BlockSpec(flip.shape, lambda g: (0, 0))
    past = pl.pallas_call(
        history_kernel,
        grid=(steps,),
        out_shape=struct(comps, wide, 2 * modes),
        in_specs=[
            SMEM,
            SMEM,
            pl.BlockSpec((modes, chunk), lambda g: (0, g)),
            pl.BlockSpec((8, chunk), lambda g: (0, back(g))),
            pl.BlockSpec((8, LANES), lambda g: (0, after(g))),
            pl.BlockSpec((depth, comps, 2, modes, chunk), lambda g: (0, 0, 0, 0, g)),
            pl.BlockSpec((depth, comps, 2, 16, chunk), lambda g: (0, 0, 0, 0, back(g))),
            pl.BlockSpec((depth, comps, 2, 16, LANES), lambda g: (0, 0, 0, 0, after(g))),
            flip_spec,
        ],
        out_specs=pl.BlockSpec((comps, chunk, 2 * modes), lambda g: (0, g, 0)),
        scratch_shapes=[pltpu.VMEM((comps, 2 * modes, chunk), F32)],
        compiler_params=SMALL,
        cost_estimate=took(7),
        name="history",
    )(flags, coded, mode_band, mode_band, mode_band, history, history, history, flip)

    def weights(marks, table, band, few, block):
        owned = band.shape[0]
        tiles = -(-comps // (LANES // 2 // owned))
        swap = swap_table(owned)
        own = lambda g: (0, g)
        return pl.pallas_call(
            weight_kernel,
            grid=(steps,),
            out_shape=struct(tiles, wide, LANES),
            in_specs=[
                SMEM,
                SMEM,
                pl.BlockSpec((owned, chunk), own),
                pl.BlockSpec((16, chunk), own),
                pl.BlockSpec((owned, chunk), lambda g: (0, back(g))),
                pl.BlockSpec((16, chunk), lambda g: (0, back(g))),
                pl.BlockSpec((owned, LANES), lambda g: (0, after(g))),
                pl.BlockSpec((16, LANES), lambda g: (0, after(g))),
                flip_spec,
                pl.BlockSpec(swap.shape, lambda g: (0, 0)),
            ],
            out_specs=pl.BlockSpec((tiles, chunk, LANES), lambda g: (0, g, 0)),
            scratch_shapes=[pltpu.VMEM((tiles, LANES, chunk), F32)],
            compiler_params=SMALL,
            cost_estimate=took(40),
            name="weights",
        )(marks, table, band, few, block, few, block, few, flip, swap)

    now_weight = weights(flags, coded[:, :comps] + coded[:, comps : 2 * comps], mode_band, few, block)
    lower = flags[0] > 0.0
    part = modes // 2
    band = jnp.where(lower, mode_band[:part], block[part:])
    other = jnp.where(lower, block[part:], mode_band[:part])
    few = jnp.concatenate([jnp.where(lower, few[:1], mode_band[part : part + 1]), few[1:]], axis=0)
    marks = jnp.stack([jnp.ones((), F32), jnp.where(lower, flags[1], 0.0)])
    later_weight = weights(marks, coded[:, :comps], band, few, other)

    count = wide // RADIX

    def x_scratch(given, lanes, *tables):
        return [
            pltpu.VMEM(given.shape, F32),
            pltpu.VMEM((RADIX, 2 * count, lanes), F32),
            pltpu.VMEM((RADIX, count, lanes), F32),
            *(pltpu.VMEM(table.shape, table.dtype) for table in tables),
            pltpu.SemaphoreType.DMA((len(tables) - 2,)),
            pltpu.SemaphoreType.DMA((2,)),
            pltpu.SemaphoreType.DMA((1,)),
        ]

    operands = x_forward, x_inverse, now_weight, past
    sent = pl.pallas_call(
        x_kernel,
        out_shape=struct(far, comps, rows, 2 * modes),
        in_specs=[ANY] * 5,
        out_specs=ANY,
        scratch_shapes=x_scratch(here, comps * LANES, *operands)
        + [pltpu.VMEM((far, comps, rows, 2 * modes), F32), pltpu.SemaphoreType.DMA((-(-comps // 2),))],
        compiler_params=SMALL,
        cost_estimate=took(12),
        name="x_stage",
    )(here, *operands)
    fields = lax.all_to_all(sent, AXES, 0, 0, tiled=True)
    sent, stress = pl.pallas_call(
        y_middle_kernel,
        out_shape=[struct(far, comps * rows // 2, LANES), struct(comps, rows, length)],
        in_specs=[ANY] * 6,
        out_specs=[ANY] * 2,
        scratch_shapes=[turned, halves, halves, sections, sections, halves, y_table, y_table]
        + [field, pltpu.VMEM((2, rows, length), F32), field, field, pltpu.VMEM(fields.shape, F32)]
        + [pltpu.VMEM((far, comps * rows // 2, LANES), F32), pltpu.SemaphoreType.DMA((4,))]
        + [pltpu.SemaphoreType.DMA((2 * PIECES,))] * 2
        + [pltpu.SemaphoreType.DMA((1,))] * 2,
        compiler_params=PARAMS,
        cost_estimate=took(14),
        name="y_middle",
    )(prestress, slip_field, slip_rate, y_inverse, y_forward, fields)
    here = lax.all_to_all(sent, AXES, 0, 0, tiled=True)
    operands = far_forward, far_inverse, later_weight
    given = here.reshape(-1, LANES)
    sent = pl.pallas_call(
        x_far_kernel,
        out_shape=struct(far * comps * rows // 2, LANES),
        in_specs=[ANY] * 4,
        out_specs=VMEM,
        scratch_shapes=x_scratch(given, 2 * LANES, *operands),
        compiler_params=SMALL,
        cost_estimate=took(8),
        name="x_far",
    )(given, *operands)
    fields = lax.all_to_all(sent.reshape(here.shape), AXES, 0, 0, tiled=True)
    return tuple(
        pl.pallas_call(
            y_final_kernel,
            out_shape=[struct(comps, rows, length)] * 2,
            in_specs=[ANY] * 5,
            out_specs=[ANY] * 2,
            scratch_shapes=[turned, halves, sections, y_table, field, field, field, field, field]
            + [pltpu.VMEM(fields.shape, F32), pltpu.SemaphoreType.DMA((3,))]
            + [pltpu.SemaphoreType.DMA((2 * PIECES,))] * 2
            + [pltpu.SemaphoreType.DMA((1,))],
            compiler_params=PARAMS,
            cost_estimate=took(10),
            name="y_final",
        )(stress, slip_field, slip_rate, y_inverse, fields)
    )


def reverse_modes(values):
    return jnp.roll(jnp.flip(values, -1), 1, -1)


def exchange_bands(kernel, band_len, mode_band):
    bands, lags, comps = kernel.shape
    far = lax.axis_size(AXES)
    near = lax.axis_size(NEAR)
    me = lax.axis_index(AXES)
    first = me % near == 0
    flags = jnp.stack([jnp.where(me < near, 1.0, -1.0), jnp.where(first, 1.0, 0.0)]).astype(F32)
    live = (jnp.arange(lags, dtype=jnp.int32)[None, :] < band_len[:, None]).astype(F32)
    coded = (kernel * live[:, :, None]).reshape(bands, lags * comps)
    block = lax.ppermute(mode_band, AXES, [(d, far - 1 - d) for d in range(far)])
    return flags, coded, block


def exchange_edges(first_row):
    far = lax.axis_size(AXES)
    near = lax.axis_size(NEAR)
    first = lax.axis_index(AXES) % near == 0
    pairs = [(d, (d + near) % far if d % near == 0 else far - d) for d in range(far)]
    row = lax.ppermute(first_row, AXES, pairs)
    edge = jnp.where(first, first_row, row)
    return jnp.concatenate([edge, row, jnp.zeros((14, first_row.shape[1]), jnp.int32)], axis=0)


def reverse_first(history, mode_band):
    row_back = reverse_modes(history[:, :, :, 0, :].astype(F32).reshape(-1, mode_band.shape[1]))
    return row_back, reverse_modes(mode_band[:1])


def plain(slip_rate, slip_field, prestress, history, kernel, band_len, mode_band):
    comps, rows, length = slip_rate.shape
    modes, wide = mode_band.shape
    far = lax.axis_size(AXES)
    near = lax.axis_size(NEAR)
    bands, lags = kernel.shape[:2]
    depth = history.shape[0]
    flags, coded, block = exchange_bands(kernel, band_len, mode_band)
    few = exchange_edges(mode_band[:1])
    row_back, row_mirror = reverse_first(history, mode_band)
    mirror = reverse_modes(jnp.concatenate([few[:1], jnp.flip(block[1:], 0)], axis=0))
    extra = jnp.concatenate([few[1:2], reverse_modes(few[1:2])], axis=0)
    table = coded.reshape(bands, lags, comps)
    edge = flags[1] > 0.0
    top = (jnp.arange(modes) == 0)[None, :, None] & edge

    def dot(spec, a, b):
        return jnp.einsum(spec, a, b, precision=lax.Precision.HIGHEST)

    def angles(first, second, size):
        product = (first[:, None] * second[None, :]) % size
        angle = product.astype(F32) * (2.0 * math.pi / size)
        return jnp.cos(angle) / math.sqrt(size), jnp.sin(angle) / math.sqrt(size)

    def weights(band, values):
        result = jnp.zeros(values.shape[1:] + band.shape, F32)
        for b in range(bands):
            result = jnp.where(band == b, values[b][..., None, None], result)
        return result

    past = []
    for at in range(depth):
        w = weights(mode_band, table[:, lags - depth + at])[:, None]
        past.append(w * history[at].astype(F32))
    past = sum(past)
    back = row_back.reshape(depth, comps, 2, 1, wide)
    w = weights(row_mirror, table[:, lags - depth :])
    back = jnp.sum(w[:, :, None] * back, axis=0) * jnp.array([1.0, -1.0], F32)[:, None, None]
    past = jnp.where(top, 0.5 * (past + back), past)
    parity = jnp.where(jnp.arange(wide) % 2 == 1, flags[0], 1.0)

    def filters(values):
        whole = (weights(mode_band, values) + weights(mirror, values)) * parity
        other = (weights(extra[:1], values) + weights(extra[1:], values)) * parity
        return jnp.where(top, 0.5 * whole, whole), jnp.where(top, 0.5 * other, whole)

    own = jnp.arange(length, dtype=jnp.int32)
    y_cos, y_sin = angles(own, own[: length // 2], length)
    nyquist = jnp.where(own % 2 == 1, -1.0, 1.0).astype(F32) / math.sqrt(length)
    y_sin = y_sin.at[:, 0].set(-nyquist)
    across = jnp.arange(wide, dtype=jnp.int32)
    x_cos, x_sin = angles(across, across, wide)
    flip = jnp.where(own % 2 == 1, flags[0], 1.0)

    def y_forward(field):
        field = field * flip
        both = jnp.stack([dot("cxy,yk->ckx", field, y_cos), -dot("cxy,yk->ckx", field, y_sin)], 1)
        both = both.reshape(comps, 2, near, modes, rows).transpose(2, 0, 4, 1, 3)
        return lax.all_to_all(both, NEAR, 0, 0, tiled=True)

    def x_stage(given, filt, added):
        given = given.transpose(1, 3, 4, 0, 2).reshape(comps, 2, modes, near * rows)
        real = dot("cpkx,xm->cpkm", given, x_cos[: near * rows])
        imag = -dot("cpkx,xm->cpkm", given, x_sin[: near * rows])
        a, b = filt
        out_real = a * real[:, 0] - b * imag[:, 1]
        out_imag = a * imag[:, 0] + b * real[:, 1]
        if added is not None:
            out_real, out_imag = out_real + added[:, 0], out_imag + added[:, 1]
        first = dot("ckm,mx->ckx", out_real, x_cos) - dot("ckm,mx->ckx", out_imag, x_sin)
        second = dot("ckm,mx->ckx", out_real, x_sin) + dot("ckm,mx->ckx", out_imag, x_cos)
        both = jnp.stack([first, second], 1).reshape(comps, 2, modes, far, rows).transpose(3, 0, 4, 1, 2)
        return lax.all_to_all(both, AXES, 0, 0, tiled=True)

    def y_inverse(given):
        given = given.reshape(2, near, comps, rows, 2, modes).transpose(0, 4, 2, 3, 1, 5)
        given = given.reshape(2, 2, comps, rows, length // 2)
        half = dot("hcxk,yk->hcxy", given[:, 0], y_cos) - dot("hcxk,yk->hcxy", given[:, 1], y_sin)
        return half[0] + half[1] * jnp.where(own % 2 == 1, -1.0, 1.0)

    def phi(s):
        return jnp.stack(friction(s[0], s[1], s[2], slip_field[0], slip_field[1]))

    now = filters(table[:, 0] + table[:, 1])
    later = filters(table[:, 0])
    stress = prestress + y_inverse(x_stage(y_forward(slip_rate), now, past))
    shift = 0.5 * (phi(stress) - slip_rate)
    second = phi(stress + y_inverse(x_stage(y_forward(shift), later, None)))
    return second, slip_field + 0.25 * (slip_rate + second)


def solution(mesh):
    shape = mesh.devices.shape
    ours = Mesh(mesh.devices.reshape(2, shape[0] // 2, shape[1]), AXES)

    def on_device(slip_rate, slip_field, prestress, history, kernel, band_len, mode_band):
        args = (slip_rate, slip_field, prestress, history, kernel, band_len, mode_band)
        rows, modes = slip_rate.shape[1], mode_band.shape[0]
        near = lax.axis_size(NEAR)
        if 2 * modes == LANES and 2 * rows == LANES and near % PIECES == 0 and slip_rate.shape[0] == 3:
            return with_kernels(*args)
        return plain(*args)

    rows = P(None, AXES, None)
    return jax.shard_map(
        on_device,
        mesh=ours,
        in_specs=(rows, rows, rows, P(None, None, None, AXES, None), P(), P(), P(AXES, None)),
        out_specs=(rows, rows),
        check_vma=False,
    )
```

```python
import functools
import math

import jax
import jax.numpy as jnp
import numpy as np
from jax import lax
from jax.experimental import pallas as pl
from jax.experimental.pallas import tpu as pltpu
from jax.sharding import Mesh, PartitionSpec as P


LANES = 128
RADIX = 8
SHORT = 4
AXES = ("half", "part", "ky")
NEAR = ("part", "ky")
F32 = jnp.float32
BF16 = jnp.bfloat16
ROOT = math.sqrt(0.5)
PIECES = 4

static_fric = 0.7
dynamic_fric = 0.35
weaken_slip = 0.5


def softplus(value):
    return jnp.maximum(value, 0.0) + jnp.log1p(jnp.exp(-jnp.abs(value)))


def friction(s0, s1, s2, u0, u1):
    worn = jnp.sqrt(u0 * u0 + u1 * u1 + 1.0) - 1.0
    coeff = dynamic_fric + (static_fric - dynamic_fric) * jnp.exp(worn * (-1.0 / weaken_slip))
    tail = jnp.log1p(jnp.exp(-jnp.abs(s2)))
    strength = coeff * (jnp.maximum(-s2, 0.0) + tail)
    magnitude = jnp.sqrt(s0 * s0 + s1 * s1 + 1.0)
    ratio = softplus(magnitude - strength) / magnitude
    return ratio * s0, ratio * s1, jnp.maximum(s2, 0.0) + tail


def split_table(values):
    high = values.astype(BF16)
    low = (values - high.astype(np.float64)).astype(BF16)
    return np.concatenate([high, low], axis=-1)


def tables(length):
    count = length // RADIX
    outer = np.arange(count)
    spots = RADIX * outer[None, :, None] + np.arange(RADIX)[:, None, None]
    angle = 2.0 * np.pi / length * ((spots * outer[None, None, :]) % length)
    cos = np.cos(angle) / math.sqrt(length)
    sin = np.sin(angle) / math.sqrt(length)
    forward = np.concatenate([cos.transpose(0, 2, 1), -sin.transpose(0, 2, 1)], axis=1)
    inverse = np.concatenate([cos, sin], axis=1)
    return forward, inverse


def parts_of(sections, row, count, lanes):
    return [(sections[j, pl.ds(row, 8), lanes], sections[j, pl.ds(row + count, 8), lanes]) for j in range(RADIX)]


def dot3(table, values):
    depth = values.shape[0]
    high = values.astype(BF16)
    low = (values - high.astype(F32)).astype(BF16)
    left = jnp.concatenate([table, table[:, :depth]], axis=1)
    right = jnp.concatenate([high, high, low], axis=0)
    return jnp.dot(left, right, preferred_element_type=F32)


def c_add(a, b):
    return a[0] + b[0], a[1] + b[1]


def c_sub(a, b):
    return a[0] - b[0], a[1] - b[1]


def forward_eight(a, wanted):
    def four(p, q, r, s):
        t0, t1, t2 = c_add(p, r), c_sub(p, r), c_add(q, s)
        d = c_sub(q, s)
        t3 = (d[1], -d[0])
        return c_add(t0, t2), c_add(t1, t3), c_sub(t0, t2), c_sub(t1, t3)

    even = four(a[0], a[2], a[4], a[6])
    odd = four(a[1], a[3], a[5], a[7])
    o1 = ((odd[1][0] + odd[1][1]) * ROOT, (odd[1][1] - odd[1][0]) * ROOT)
    o2 = (odd[2][1], -odd[2][0])
    o3 = ((odd[3][1] - odd[3][0]) * ROOT, (odd[3][0] + odd[3][1]) * -ROOT)
    turned = (odd[0], o1, o2, o3)
    first = [c_add(even[k], turned[k]) for k in range(4)]
    if wanted <= 4:
        return first
    return first + [c_sub(even[k], turned[k]) for k in range(4)]


def low_half():
    return lax.broadcasted_iota(jnp.int32, (1, LANES), 1) % (LANES // 2) < LANES // 4


def join(a, b):
    return jnp.where(low_half(), a, pltpu.roll(b, LANES // 4, 1))


def join_second(a, b):
    return jnp.where(low_half(), pltpu.roll(a, LANES - LANES // 4, 1), b)


def blocks_of(packed, owner, comps, rows):
    whole = [packed[owner, :, t * LANES : (t + 1) * LANES].T for t in range(packed.shape[2] // LANES)]
    whole = jnp.concatenate(whole, axis=0)
    return [whole[c * rows : (c + 1) * rows] for c in range(comps)]


def deliver_near(packed, owner, out):
    _, comps, rows, _ = out.shape
    for c, block in enumerate(blocks_of(packed, owner, comps, rows)):
        out[owner, c] = block


def deliver_far(rows, packed, owner, out):
    far = out.shape[0]
    comps = 2 * out.shape[1] // rows
    for c, block in enumerate(blocks_of(packed, owner, comps, rows)):
        top, bottom = block[: rows // 2], block[rows // 2 :]
        for device, value in ((owner, join(top, bottom)), (far - 1 - owner, join_second(top, bottom))):
            for m in range(rows // 16):
                out[device, (m * comps + c) * 8 : (m * comps + c) * 8 + 8] = value[m * 8 : m * 8 + 8]


def forward_rows(turned, table, flag, sections, packed, out, ready, deliver, leave):
    tiles, length, _ = turned.shape
    count = length // RADIX
    owners = packed.shape[0]
    modes = packed.shape[1] // 2
    ready()
    for j in range(RADIX):
        piece = jnp.concatenate([turned[t, pl.ds(j, count, stride=RADIX), :] for t in range(tiles)], axis=1)
        if flag is not None and j % 2:
            piece = piece * flag
        sections[j] = dot3(table[j], piece)
    per = modes // 8

    def chunk(q, carry):
        at = q // per
        off = pl.multiple_of((q % per) * 8, 8)
        row = pl.multiple_of(q * 8, 8)
        found = forward_eight(parts_of(sections, row, count, slice(None)), 4)
        for k2 in range(RADIX // 2):
            owner = at + k2 * (count // modes)
            packed[owner, pl.ds(off, 8), :] = found[k2][0]
            packed[owner, pl.ds(off + modes, 8), :] = found[k2][1]
        return carry

    lax.fori_loop(0, count // 8, chunk, 0, unroll=8)
    top = sections[0, 0:1, :]
    for j in range(1, RADIX):
        top = top - sections[j, 0:1, :] if j % 2 else top + sections[j, 0:1, :]
    packed[0, modes : modes + 1, :] = top

    def send(owner, carry):
        deliver(packed, owner, out)
        return carry

    size = owners // PIECES
    for piece in range(PIECES):
        lax.fori_loop(piece * size, (piece + 1) * size, send, 0, unroll=True)
        leave(piece)


def store_turned(store, owner, pieces):
    tiles = store.shape[2] // LANES
    used = sum(piece.shape[0] for piece in pieces)
    whole = jnp.concatenate(list(pieces) + [jnp.zeros((LANES * tiles - used, LANES), F32)], axis=0)
    for t in range(tiles):
        store[owner, :, t * LANES : (t + 1) * LANES] = whole[t * LANES : (t + 1) * LANES].T


def collect_halves(arrived, even, odd, owner):
    far, comps, _, _ = arrived.shape
    mine = [arrived[owner, c] for c in range(comps)]
    other = [arrived[owner + far // 2, c] for c in range(comps)]
    store_turned(even, owner, [a + b for a, b in zip(mine, other)])
    store_turned(odd, owner, [a - b for a, b in zip(mine, other)])


def collect_far(rows, arrived, even, odd, owner):
    far = arrived.shape[0]
    comps = 2 * arrived.shape[1] // rows
    first, second = arrived[owner], arrived[far - 1 - owner]
    halves = join(first, second), join_second(first, second)
    pieces = []
    for c in range(comps):
        for half in halves:
            pieces += [half[(m * comps + c) * 8 : (m * comps + c) * 8 + 8] for m in range(rows // 16)]
    store_turned(even, owner, pieces)


def inverse_rows(arrived, table, even, odd, mixed, turned, ready, collect, arrive):
    near = even.shape[0]
    modes = even.shape[1] // 2
    tiles, length, _ = turned.shape
    count = length // RADIX

    def gather(owner, carry):
        collect(arrived, even, odd, owner)
        return carry

    size = near // PIECES
    for piece in range(PIECES):
        arrive(piece)
        lax.fori_loop(piece * size, (piece + 1) * size, gather, 0, unroll=True)
    per = modes // 8

    def chunk(q, carry):
        at = q // per
        off = pl.multiple_of((q % per) * 8, 8)
        row = pl.multiple_of(q * 8, 8)

        def four(s):
            t0, t1, t2 = c_add(s[0], s[2]), c_sub(s[0], s[2]), c_add(s[1], s[3])
            d = c_sub(s[1], s[3])
            t3 = (-d[1], d[0])
            return c_add(t0, t2), c_add(t1, t3), c_sub(t0, t2), c_sub(t1, t3)

        for first, store in ((0, even), (1, odd)):
            parts = []
            for k2 in range(RADIX // 2):
                owner = at + k2 * (count // modes)
                parts.append((store[owner, pl.ds(off, 8), :], store[owner, pl.ds(off + modes, 8), :]))
            if first:
                p1, p2, p3 = parts[1:]
                parts[1] = ((p1[0] - p1[1]) * ROOT, (p1[0] + p1[1]) * ROOT)
                parts[2] = (-p2[1], p2[0])
                parts[3] = ((p3[0] + p3[1]) * -ROOT, (p3[0] - p3[1]) * ROOT)
            for index, (re, im) in enumerate(four(parts)):
                j = 2 * index + first
                mixed[j, pl.ds(row, 8), :] = re
                mixed[j, pl.ds(row + count, 8), :] = im
        return carry

    lax.fori_loop(0, count // 8, chunk, 0, unroll=8)
    scale = 1.0 / math.sqrt(length)
    ready()
    for j in range(RADIX):
        piece = dot3(table[j, :count], mixed[j, :count, :]) - dot3(table[j, count:], mixed[j, count:, :])
        if j % 2:
            piece = piece - odd[0, modes : modes + 1, :] * scale
        else:
            piece = piece + even[0, modes : modes + 1, :] * scale
        for t in range(tiles):
            turned[t, pl.ds(j, count, stride=RADIX), :] = piece[:, t * LANES : (t + 1) * LANES]


def turn_in(parts, turned, start):
    tiles = turned.shape[0]
    used = sum(part.shape[0] for part in parts)
    blank = jnp.zeros((LANES * tiles - used, LANES), F32)
    whole = jnp.concatenate(list(parts) + [blank], axis=0)
    for t in range(tiles):
        turned[t, pl.ds(start, LANES), :] = whole[t * LANES : (t + 1) * LANES].T


def turn_out(turned, start, rows, comps):
    tiles = turned.shape[0]
    whole = jnp.concatenate([turned[t, pl.ds(start, LANES), :].T for t in range(tiles)], axis=0)
    return [whole[c * rows : (c + 1) * rows] for c in range(comps)]


def fetch(sems, *pairs, start=True):
    copies = [pltpu.make_async_copy(source, target, sems.at[k]) for k, (source, target) in enumerate(pairs)]
    if start:
        start_all(copies)
    return copies


def pieces_of(source, target, sems, mirrored):
    far = source.shape[0]
    size = far // PIECES if mirrored is None else far // 2 // PIECES
    found = []
    for piece in range(PIECES):
        starts = [piece * size]
        if mirrored is not None:
            starts.append(far - (piece + 1) * size if mirrored else far // 2 + piece * size)
        found.append(
            [
                pltpu.make_async_copy(
                    source.at[pl.ds(start, size)], target.at[pl.ds(start, size)], sems.at[piece + k * PIECES]
                )
                for k, start in enumerate(starts)
            ]
        )
    return found


def start_all(copies):
    for copy in copies:
        copy.start()


def wait_all(copies):
    for copy in copies:
        copy.wait()


def y_forward_kernel(field_far, table_far, out_far, turned, sections, packed, table, out, field, *sems):
    table_sems, out_sems = sems
    comps, _, length = field.shape
    got_field, got_table = fetch(table_sems, (field_far, field), (table_far, table))
    got_field.wait()

    def load(q, carry):
        start = pl.multiple_of(q * LANES, LANES)
        turn_in([field[c, :, pl.ds(start, LANES)] for c in range(comps)], turned, start)
        return carry

    lax.fori_loop(0, length // LANES, load, 0, unroll=4)
    give = pieces_of(out, out_far, out_sems, None)
    leave = lambda piece: start_all(give[piece])
    sign = 1.0 - 2.0 * lax.axis_index(AXES[0]).astype(F32)
    forward_rows(turned, table, sign, sections, packed, out, got_table.wait, deliver_near, leave)
    for copies in give:
        wait_all(copies)


def y_middle_kernel(
    prestress_far, slip_far, rate_far, inverse_far, forward_far, arrived_far, out_far, stress_far, *rest
):
    turned, even, odd, mixed, sections, packed, inverse, forward, prestress, slip, rate, stress, *rest = rest
    arrived, out, sems, in_sems, out_sems, inverse_sems, forward_sems = rest
    comps, rows, length = prestress.shape
    take = pieces_of(arrived_far, arrived, in_sems, False)
    for copies in take:
        start_all(copies)
    slip_used = slip_far.at[: slip.shape[0]]
    (got_inverse,) = fetch(inverse_sems, (inverse_far, inverse))
    got = fetch(sems, (prestress_far, prestress), (slip_used, slip), (rate_far, rate), start=False)
    (got_forward,) = fetch(forward_sems, (forward_far, forward), start=False)

    def arrive(piece):
        wait_all(take[piece])
        if piece == PIECES - 1:
            start_all(got)

    def ready():
        got_inverse.wait()
        got_forward.start()

    inverse_rows(arrived, inverse, even, odd, mixed, turned, ready, collect_halves, arrive)
    wait_all(got)

    def step(q, carry):
        start = pl.multiple_of(q * LANES, LANES)
        lanes = pl.ds(start, LANES)
        parts = turn_out(turned, start, rows, comps)
        s = [prestress[c, :, lanes] + parts[c] for c in range(comps)]
        for c in range(comps):
            stress[c, :, lanes] = s[c]
        first = friction(*s, slip[0, :, lanes], slip[1, :, lanes])
        turn_in([(first[c] - rate[c, :, lanes]) * 0.5 for c in range(comps)], turned, start)
        return carry

    lax.fori_loop(0, length // LANES, step, 0, unroll=2)
    give_stress = pltpu.make_async_copy(stress, stress_far, sems.at[3])
    give_stress.start()
    deliver = functools.partial(deliver_far, rows)
    give = pieces_of(out, out_far, out_sems, True)
    leave = lambda piece: start_all(give[piece])
    forward_rows(turned, forward, None, sections, packed, out, got_forward.wait, deliver, leave)
    give_stress.wait()
    for copies in give:
        wait_all(copies)


def y_final_kernel(stress_far, slip_far, rate_far, inverse_far, arrived_far, new_rate_far, new_slip_far, *rest):
    turned, even, mixed, inverse, stress, slip, rate, new_rate, new_slip, arrived, sems, in_sems, out_sems, inverse_sems = rest
    comps, rows, length = stress.shape
    take = pieces_of(arrived_far, arrived, in_sems, True)
    for copies in take:
        start_all(copies)
    (got_inverse,) = fetch(inverse_sems, (inverse_far, inverse))
    got = fetch(sems, (stress_far, stress), (slip_far, slip), (rate_far, rate), start=False)
    collect = functools.partial(collect_far, rows)

    def arrive(piece):
        wait_all(take[piece])
        if piece == PIECES - 1:
            start_all(got)

    inverse_rows(arrived, inverse, even, even, mixed, turned, got_inverse.wait, collect, arrive)
    wait_all(got)

    def step(q, carry):
        start = pl.multiple_of(q * LANES, LANES)
        lanes = pl.ds(start, LANES)
        parts = turn_out(turned, start, rows, comps)
        s = [stress[c, :, lanes] + parts[c] for c in range(comps)]
        second = friction(*s, slip[0, :, lanes], slip[1, :, lanes])
        for c in range(comps):
            new_rate[c, :, lanes] = second[c]
            new_slip[c, :, lanes] = slip[c, :, lanes] + 0.25 * (rate[c, :, lanes] + second[c])
        return carry

    size = length // LANES // PIECES
    give = []
    for piece in range(PIECES):
        lax.fori_loop(piece * size, (piece + 1) * size, step, 0, unroll=2)
        lanes = pl.ds(piece * size * LANES, size * LANES)
        for k, (near, far) in enumerate(((new_rate, new_rate_far), (new_slip, new_slip_far))):
            give.append(
                pltpu.make_async_copy(near.at[:, :, lanes], far.at[:, :, lanes], out_sems.at[2 * piece + k])
            )
            give[-1].start()
    wait_all(give)


def inverse_eight(z, turn):
    def four(a, b, c, d):
        t0, t1, t2, t3 = a + c, a - c, b + d, turn(b - d)
        return t0 + t2, t1 + t3, t0 - t2, t1 - t3

    e = four(z[0], z[2], z[4], z[6])
    o = four(z[1], z[3], z[5], z[7])
    o1 = (o[1] + turn(o[1])) * ROOT
    o3 = (turn(o[3]) - o[3]) * ROOT
    turned = (o[0], o1, turn(o[2]), o3)
    return [e[k] + turned[k] for k in range(4)] + [e[k] - turned[k] for k in range(4)]


def x_core(load, store, leave, copies, forward, inverse, weight, past, sections, mixed):
    tiles, wide, _ = weight.shape
    count = wide // RADIX
    got_forward, got_filter, got_inverse = copies
    wait_all(got_forward)
    start_all(got_filter)
    for j in range(RADIX):
        sections[j] = dot3(forward[j], load(j))
    wait_all(got_filter)
    got_inverse.start()
    sign = jnp.where(lax.broadcasted_iota(jnp.int32, (1, LANES), 1) < LANES // 2, -1.0, 1.0).astype(F32)

    def turn(value):
        return sign * pltpu.roll(value, LANES // 2, 1)

    def chunk(q, carry):
        row = pl.multiple_of(q * 8, 8)
        for t in range(tiles):
            lanes = slice(t * LANES, (t + 1) * LANES)
            parts = parts_of(sections, row, count, lanes)
            z = []
            for k2, found in enumerate(forward_eight(parts, RADIX)):
                spot = pl.ds(row + k2 * count, 8)
                w = weight[t, spot, :]
                value = w * found[0] + turn(w * found[1])
                z.append(value if past is None else value + past[t, spot, :])
            for j, value in enumerate(inverse_eight(z, turn)):
                mixed[j, pl.ds(row, 8), lanes] = value
        return carry

    lax.fori_loop(0, count // 8, chunk, 0, unroll=4)
    got_inverse.wait()
    for first in range(0, tiles, 2):
        last = min(first + 2, tiles)
        for j in range(RADIX):
            both = dot3(inverse[j], mixed[j, :, first * LANES : last * LANES])
            spots = [slice(t * LANES, (t + 1) * LANES) for t in range(last - first)]
            store(j, first, [both[:count, lanes] + turn(both[count:, lanes]) for lanes in spots])
        leave(first)


def x_kernel(arrived_far, forward_far, inverse_far, weight_far, past_far, out_far, *rest):
    arrived, sections, mixed, forward, inverse, weight, past, sems, forward_sems, inverse_sems, out, out_sems = rest
    near, comps, rows, _ = arrived.shape
    far = out.shape[0]
    got_forward = fetch(forward_sems, (forward_far, forward), (arrived_far, arrived))
    got = fetch(sems, (weight_far, weight), (past_far, past), start=False)
    (got_inverse,) = fetch(inverse_sems, (inverse_far, inverse), start=False)
    step = rows // RADIX

    def load(j):
        spot = pl.ds(j, step, stride=RADIX)
        parts = [jnp.concatenate([arrived[src, c, spot, :] for src in range(near)], axis=0) for c in range(comps)]
        return jnp.concatenate(parts, axis=1)

    def store(j, first, values):
        spot = pl.ds(j, step, stride=RADIX)
        for c, value in enumerate(values, first):
            for dest in range(far):
                out[dest, c, spot, :] = value[dest * step : (dest + 1) * step]

    give = []

    def leave(first):
        group = pl.ds(first, min(2, comps - first))
        give.append(pltpu.make_async_copy(out.at[:, group], out_far.at[:, group], out_sems.at[len(give)]))
        give[-1].start()

    x_core(load, store, leave, (got_forward, got, got_inverse), forward, inverse, weight, past, sections, mixed)
    wait_all(give)


def x_far_kernel(arrived_far, forward_far, inverse_far, weight_far, out, *rest):
    arrived, sections, mixed, forward, inverse, weight, sems, forward_sems, inverse_sems = rest
    got_forward = fetch(forward_sems, (forward_far, forward), (arrived_far, arrived))
    got = fetch(sems, (weight_far, weight), start=False)
    (got_inverse,) = fetch(inverse_sems, (inverse_far, inverse), start=False)
    half = weight.shape[1] // RADIX // 2

    def spot_of(c, j):
        return pl.ds(c * RADIX + j, half, stride=3 * RADIX)

    def load(j):
        x0, x1, x2 = (arrived[spot_of(c, j), :] for c in range(3))
        none = jnp.zeros_like(x2)
        left = jnp.concatenate([join(x0, x1), join_second(x0, x1)], axis=0)
        right = jnp.concatenate([join(x2, none), join_second(x2, none)], axis=0)
        return jnp.concatenate([left, right], axis=1)

    def leave(first):
        pass

    def store(j, first, values):
        (a, b), (c, d) = ((value[:half], value[half:]) for value in values)
        out[spot_of(0, j), :] = join(a, b)
        out[spot_of(1, j), :] = join_second(a, b)
        out[spot_of(2, j), :] = join(c, d)

    x_core(load, store, leave, (got_forward, got, got_inverse), forward, inverse, weight, None, sections, mixed)


def pick(values, bits):
    level = 0
    while len(values) > 1:
        if len(values) % 2:
            values = values + [values[-1]]
        values = [jnp.where(bits[level], values[k + 1], values[k]) for k in range(0, len(values), 2)]
        level += 1
    return values[0]


def bits_of(band, bands):
    return [(band & (1 << level)) != 0 for level in range(max((bands - 1).bit_length(), 1))]


def weights_past(table, band, bits, c, depth):
    bands, lags, comps = table.shape[0], table.shape[1] // 3, 3
    found = []
    for at in range(depth):
        spot = (lags - depth + at) * comps + c
        if lags - depth + at < SHORT:
            found.append(pick([table[b, spot] for b in range(bands)], bits))
        else:
            found.append(jnp.where(band == 0, table[0, spot], 0.0))
    return found


def history_kernel(flags, table, band, band_back, band_edge, history, past_back, past_edge, flip, past, stacked):
    bands, comps = table.shape[0], 3
    depth = history.shape[0]
    rows, width = band.shape

    def group(q, carry):
        spot = pl.ds(pl.multiple_of(q * 16, 16), 16)
        own = band[spot, :]
        bits = bits_of(own, bands)
        for c in range(comps):
            sums = [jnp.zeros((16, width), F32) for _ in range(2)]
            for at, w in enumerate(weights_past(table, own, bits, c, depth)):
                for p in range(2):
                    sums[p] = sums[p] + w * history[at, c, p, spot, :].astype(F32)
            for p in range(2):
                stacked[c, pl.ds(pl.multiple_of(q * 16 + p * rows, 16), 16), :] = sums[p]
        return carry

    lax.fori_loop(0, rows // 16, group, 0)

    edge = flags[1] > 0.0
    there, beyond = [], []
    for at in range(depth):
        for c in range(comps):
            for p in range(2):
                there.append(past_back[at, c, p].astype(F32)[:1])
                beyond.append(past_edge[at, c, p].astype(F32)[:1])
    count = len(there)
    blank = -(count + 1) % 16
    there += [band_back[...].astype(F32)[:1], jnp.zeros((blank, width), F32)]
    beyond += [band_edge[...].astype(F32)[:1], jnp.zeros((blank, LANES), F32)]
    both = [jnp.concatenate(rows_of, axis=0).astype(BF16) for rows_of in (there, beyond)]
    row_back = jnp.dot(jnp.concatenate(both, axis=1), flip[...], preferred_element_type=F32)
    back = row_back[count : count + 1].astype(jnp.int32)
    bits = bits_of(back, bands)
    for c in range(comps):
        found = weights_past(table, back, bits, c, depth)
        for p in range(2):
            reverse = jnp.zeros((1, width), F32)
            for at, w in enumerate(found):
                spot = (at * comps + c) * 2 + p
                reverse = reverse + w * row_back[spot : spot + 1, :]
            if p:
                reverse = -reverse
            mine = stacked[c, p * rows : p * rows + 1, :]
            stacked[c, p * rows : p * rows + 1, :] = jnp.where(edge, 0.5 * (mine + reverse), mine)
        for t in range(width // LANES):
            spot = pl.ds(t * LANES, LANES)
            past[c, spot, :] = stacked[c, :, spot].T


def weight_kernel(flags, table, band, few, block, few_back, block_edge, few_edge, flip, swap, out, stacked):
    bands, comps = table.shape
    rows, width = band.shape
    odd = (lax.broadcasted_iota(jnp.int32, (1, width), 1) & 1) == 1
    parity = jnp.where(odd, flags[0], 1.0).astype(F32)
    edge = flags[1] > 0.0

    def exact(values):
        return values.astype(F32).astype(BF16)

    there = jnp.concatenate([exact(block[...]), exact(few_back[...])], axis=0)
    beyond = jnp.concatenate([exact(block_edge[...]), exact(few_edge[...])], axis=0)
    turned = jnp.dot(jnp.concatenate([there, beyond], axis=1), flip[...], preferred_element_type=F32)
    turned = jnp.dot(swap[...], turned.astype(BF16), preferred_element_type=F32).astype(jnp.int32)
    tiles = out.shape[0]
    slots = LANES // 2 // rows
    if tiles * slots > comps:
        stacked[tiles - 1] = jnp.zeros((LANES, width), F32)
    for c in range(comps):
        tile, re = c // slots, c % slots * rows
        im = re + LANES // 2
        values = [table[b, c] for b in range(bands)]
        for q in range(rows // 8):
            spot = slice(q * 8, q * 8 + 8)
            value = pick(values, bits_of(band[spot, :], bands)) + pick(values, bits_of(turned[spot], bands))
            value = value * parity
            if q == 0:
                first = lax.broadcasted_iota(jnp.int32, (8, width), 0) == 0
                other = pick(values, bits_of(few[1:2, :], bands))
                other = other + pick(values, bits_of(turned[rows : rows + 1], bands))
                other = jnp.where(edge, 0.5 * (other * parity), value[:1])
                value = jnp.where(first & edge, 0.5 * value, value)
                stacked[tile, im : im + 8, :] = jnp.where(first, other, value)
            else:
                stacked[tile, im + q * 8 : im + q * 8 + 8, :] = value
            stacked[tile, re + q * 8 : re + q * 8 + 8, :] = value
    for tile in range(tiles):
        for t in range(width // LANES):
            spot = slice(t * LANES, (t + 1) * LANES)
            out[tile, spot, :] = stacked[tile, :, spot].T


VMEM = pl.BlockSpec(memory_space=pltpu.VMEM)
SMEM = pl.BlockSpec(memory_space=pltpu.SMEM)
ANY = pl.BlockSpec(memory_space=pl.ANY)
PARAMS = pltpu.CompilerParams(vmem_limit_bytes=60 * 1024 * 1024)
SMALL = pltpu.CompilerParams(vmem_limit_bytes=52 * 1024 * 1024)


def y_scratch(length, modes):
    count = length // RADIX
    near = length // 2 // modes
    wide = 2 * LANES
    turned = pltpu.VMEM((2, length, LANES), F32)
    halves = pltpu.VMEM((near, 2 * modes, wide), F32)
    sections = pltpu.VMEM((RADIX, 2 * count, wide), F32)
    return turned, halves, sections


def took(microseconds):
    return pl.CostEstimate(flops=int(microseconds * 1e9), bytes_accessed=1, transcendentals=0)


def struct(*shape):
    return jax.ShapeDtypeStruct(shape, F32)


def flip_table(chunk):
    flip = np.zeros((chunk + LANES, chunk), np.float32)
    flip[chunk - np.arange(1, chunk), np.arange(1, chunk)] = 1.0
    flip[chunk, 0] = 1.0
    return jnp.asarray(flip.astype(BF16))


def swap_table(modes):
    swap = np.zeros((modes + 16, modes + 16), np.float32)
    swap[np.arange(1, modes), modes - np.arange(1, modes)] = 1.0
    swap[0, modes] = 1.0
    swap[modes, modes + 1] = 1.0
    return jnp.asarray(swap.astype(BF16))


def with_kernels(slip_rate, slip_field, prestress, history, kernel, band_len, mode_band):
    comps, rows, length = slip_rate.shape
    modes, wide = mode_band.shape
    far = lax.axis_size(AXES)
    near = lax.axis_size(NEAR)
    bands, lags = kernel.shape[:2]
    depth = history.shape[0]
    flags, coded, block = exchange_bands(kernel, band_len, mode_band)
    few = exchange_edges(mode_band[:1])

    y_forward, y_inverse = (jnp.asarray(split_table(t)) for t in tables(length))
    x_forward, x_inverse = tables(wide)
    eights = rows // RADIX
    order = np.arange(wide // RADIX).reshape(far, 2, eights // 2).transpose(1, 0, 2).reshape(-1)
    far_forward = jnp.asarray(split_table(x_forward[:, :, order]))
    both = x_inverse.reshape(RADIX, 2, wide // RADIX, wide // RADIX)[:, :, order]
    far_inverse = jnp.asarray(split_table(both.reshape(x_inverse.shape)))
    x_forward = jnp.asarray(split_table(x_forward[:, :, : wide // RADIX // 2]))
    x_inverse = jnp.asarray(split_table(x_inverse))

    turned, halves, sections = y_scratch(length, modes)
    y_table = pltpu.VMEM(y_forward.shape, BF16)
    field = pltpu.VMEM((comps, rows, length), F32)
    sent = pl.pallas_call(
        y_forward_kernel,
        out_shape=struct(near, comps, rows, 2 * modes),
        in_specs=[ANY, ANY],
        out_specs=ANY,
        scratch_shapes=[turned, sections, halves, y_table, pltpu.VMEM((near, comps, rows, 2 * modes), F32)]
        + [field, pltpu.SemaphoreType.DMA((2,)), pltpu.SemaphoreType.DMA((PIECES,))],
        compiler_params=PARAMS,
        cost_estimate=took(6),
        name="y_forward",
    )(slip_rate, y_forward)
    here = lax.all_to_all(sent, NEAR, 0, 0, tiled=True)

    chunk = 4 * LANES
    steps = wide // chunk
    back = lambda g: steps - 1 - g
    after = lambda g: (steps - g) % steps * (chunk // LANES)
    flip = flip_table(chunk)
    flip_spec = pl.BlockSpec(flip.shape, lambda g: (0, 0))
    past = pl.pallas_call(
        history_kernel,
        grid=(steps,),
        out_shape=struct(comps, wide, 2 * modes),
        in_specs=[
            SMEM,
            SMEM,
            pl.BlockSpec((modes, chunk), lambda g: (0, g)),
            pl.BlockSpec((8, chunk), lambda g: (0, back(g))),
            pl.BlockSpec((8, LANES), lambda g: (0, after(g))),
            pl.BlockSpec((depth, comps, 2, modes, chunk), lambda g: (0, 0, 0, 0, g)),
            pl.BlockSpec((depth, comps, 2, 16, chunk), lambda g: (0, 0, 0, 0, back(g))),
            pl.BlockSpec((depth, comps, 2, 16, LANES), lambda g: (0, 0, 0, 0, after(g))),
            flip_spec,
        ],
        out_specs=pl.BlockSpec((comps, chunk, 2 * modes), lambda g: (0, g, 0)),
        scratch_shapes=[pltpu.VMEM((comps, 2 * modes, chunk), F32)],
        compiler_params=SMALL,
        cost_estimate=took(7),
        name="history",
    )(flags, coded, mode_band, mode_band, mode_band, history, history, history, flip)

    def weights(marks, table, band, few, block):
        owned = band.shape[0]
        tiles = -(-comps // (LANES // 2 // owned))
        swap = swap_table(owned)
        own = lambda g: (0, g)
        return pl.pallas_call(
            weight_kernel,
            grid=(steps,),
            out_shape=struct(tiles, wide, LANES),
            in_specs=[
                SMEM,
                SMEM,
                pl.BlockSpec((owned, chunk), own),
                pl.BlockSpec((16, chunk), own),
                pl.BlockSpec((owned, chunk), lambda g: (0, back(g))),
                pl.BlockSpec((16, chunk), lambda g: (0, back(g))),
                pl.BlockSpec((owned, LANES), lambda g: (0, after(g))),
                pl.BlockSpec((16, LANES), lambda g: (0, after(g))),
                flip_spec,
                pl.BlockSpec(swap.shape, lambda g: (0, 0)),
            ],
            out_specs=pl.BlockSpec((tiles, chunk, LANES), lambda g: (0, g, 0)),
            scratch_shapes=[pltpu.VMEM((tiles, LANES, chunk), F32)],
            compiler_params=SMALL,
            cost_estimate=took(40),
            name="weights",
        )(marks, table, band, few, block, few, block, few, flip, swap)

    now_weight = weights(flags, coded[:, :comps] + coded[:, comps : 2 * comps], mode_band, few, block)
    lower = flags[0] > 0.0
    part = modes // 2
    band = jnp.where(lower, mode_band[:part], block[part:])
    other = jnp.where(lower, block[part:], mode_band[:part])
    few = jnp.concatenate([jnp.where(lower, few[:1], mode_band[part : part + 1]), few[1:]], axis=0)
    marks = jnp.stack([jnp.ones((), F32), jnp.where(lower, flags[1], 0.0)])
    later_weight = weights(marks, coded[:, :comps], band, few, other)

    count = wide // RADIX

    def x_scratch(given, lanes, *tables):
        return [
            pltpu.VMEM(given.shape, F32),
            pltpu.VMEM((RADIX, 2 * count, lanes), F32),
            pltpu.VMEM((RADIX, count, lanes), F32),
            *(pltpu.VMEM(table.shape, table.dtype) for table in tables),
            pltpu.SemaphoreType.DMA((len(tables) - 2,)),
            pltpu.SemaphoreType.DMA((2,)),
            pltpu.SemaphoreType.DMA((1,)),
        ]

    operands = x_forward, x_inverse, now_weight, past
    sent = pl.pallas_call(
        x_kernel,
        out_shape=struct(far, comps, rows, 2 * modes),
        in_specs=[ANY] * 5,
        out_specs=ANY,
        scratch_shapes=x_scratch(here, comps * LANES, *operands)
        + [pltpu.VMEM((far, comps, rows, 2 * modes), F32), pltpu.SemaphoreType.DMA((-(-comps // 2),))],
        compiler_params=SMALL,
        cost_estimate=took(12),
        name="x_stage",
    )(here, *operands)
    fields = lax.all_to_all(sent, AXES, 0, 0, tiled=True)
    sent, stress = pl.pallas_call(
        y_middle_kernel,
        out_shape=[struct(far, comps * rows // 2, LANES), struct(comps, rows, length)],
        in_specs=[ANY] * 6,
        out_specs=[ANY] * 2,
        scratch_shapes=[turned, halves, halves, sections, sections, halves, y_table, y_table]
        + [field, pltpu.VMEM((2, rows, length), F32), field, field, pltpu.VMEM(fields.shape, F32)]
        + [pltpu.VMEM((far, comps * rows // 2, LANES), F32), pltpu.SemaphoreType.DMA((4,))]
        + [pltpu.SemaphoreType.DMA((2 * PIECES,))] * 2
        + [pltpu.SemaphoreType.DMA((1,))] * 2,
        compiler_params=PARAMS,
        cost_estimate=took(14),
        name="y_middle",
    )(prestress, slip_field, slip_rate, y_inverse, y_forward, fields)
    here = lax.all_to_all(sent, AXES, 0, 0, tiled=True)
    operands = far_forward, far_inverse, later_weight
    given = here.reshape(-1, LANES)
    sent = pl.pallas_call(
        x_far_kernel,
        out_shape=struct(far * comps * rows // 2, LANES),
        in_specs=[ANY] * 4,
        out_specs=VMEM,
        scratch_shapes=x_scratch(given, 2 * LANES, *operands),
        compiler_params=SMALL,
        cost_estimate=took(8),
        name="x_far",
    )(given, *operands)
    fields = lax.all_to_all(sent.reshape(here.shape), AXES, 0, 0, tiled=True)
    return tuple(
        pl.pallas_call(
            y_final_kernel,
            out_shape=[struct(comps, rows, length)] * 2,
            in_specs=[ANY] * 5,
            out_specs=[ANY] * 2,
            scratch_shapes=[turned, halves, sections, y_table, field, field, field, field, field]
            + [pltpu.VMEM(fields.shape, F32), pltpu.SemaphoreType.DMA((3,))]
            + [pltpu.SemaphoreType.DMA((2 * PIECES,))] * 2
            + [pltpu.SemaphoreType.DMA((1,))],
            compiler_params=PARAMS,
            cost_estimate=took(10),
            name="y_final",
        )(stress, slip_field, slip_rate, y_inverse, fields)
    )


def reverse_modes(values):
    return jnp.roll(jnp.flip(values, -1), 1, -1)


def exchange_bands(kernel, band_len, mode_band):
    bands, lags, comps = kernel.shape
    far = lax.axis_size(AXES)
    near = lax.axis_size(NEAR)
    me = lax.axis_index(AXES)
    first = me % near == 0
    flags = jnp.stack([jnp.where(me < near, 1.0, -1.0), jnp.where(first, 1.0, 0.0)]).astype(F32)
    live = (jnp.arange(lags, dtype=jnp.int32)[None, :] < band_len[:, None]).astype(F32)
    coded = (kernel * live[:, :, None]).reshape(bands, lags * comps)
    block = lax.ppermute(mode_band, AXES, [(d, far - 1 - d) for d in range(far)])
    return flags, coded, block


def exchange_edges(first_row):
    far = lax.axis_size(AXES)
    near = lax.axis_size(NEAR)
    first = lax.axis_index(AXES) % near == 0
    pairs = [(d, (d + near) % far if d % near == 0 else far - d) for d in range(far)]
    row = lax.ppermute(first_row, AXES, pairs)
    edge = jnp.where(first, first_row, row)
    return jnp.concatenate([edge, row, jnp.zeros((14, first_row.shape[1]), jnp.int32)], axis=0)


def reverse_first(history, mode_band):
    row_back = reverse_modes(history[:, :, :, 0, :].astype(F32).reshape(-1, mode_band.shape[1]))
    return row_back, reverse_modes(mode_band[:1])


def plain(slip_rate, slip_field, prestress, history, kernel, band_len, mode_band):
    comps, rows, length = slip_rate.shape
    modes, wide = mode_band.shape
    far = lax.axis_size(AXES)
    near = lax.axis_size(NEAR)
    bands, lags = kernel.shape[:2]
    depth = history.shape[0]
    flags, coded, block = exchange_bands(kernel, band_len, mode_band)
    few = exchange_edges(mode_band[:1])
    row_back, row_mirror = reverse_first(history, mode_band)
    mirror = reverse_modes(jnp.concatenate([few[:1], jnp.flip(block[1:], 0)], axis=0))
    extra = jnp.concatenate([few[1:2], reverse_modes(few[1:2])], axis=0)
    table = coded.reshape(bands, lags, comps)
    edge = flags[1] > 0.0
    top = (jnp.arange(modes) == 0)[None, :, None] & edge

    def dot(spec, a, b):
        return jnp.einsum(spec, a, b, precision=lax.Precision.HIGHEST)

    def angles(first, second, size):
        product = (first[:, None] * second[None, :]) % size
        angle = product.astype(F32) * (2.0 * math.pi / size)
        return jnp.cos(angle) / math.sqrt(size), jnp.sin(angle) / math.sqrt(size)

    def weights(band, values):
        result = jnp.zeros(values.shape[1:] + band.shape, F32)
        for b in range(bands):
            result = jnp.where(band == b, values[b][..., None, None], result)
        return result

    past = []
    for at in range(depth):
        w = weights(mode_band, table[:, lags - depth + at])[:, None]
        past.append(w * history[at].astype(F32))
    past = sum(past)
    back = row_back.reshape(depth, comps, 2, 1, wide)
    w = weights(row_mirror, table[:, lags - depth :])
    back = jnp.sum(w[:, :, None] * back, axis=0) * jnp.array([1.0, -1.0], F32)[:, None, None]
    past = jnp.where(top, 0.5 * (past + back), past)
    parity = jnp.where(jnp.arange(wide) % 2 == 1, flags[0], 1.0)

    def filters(values):
        whole = (weights(mode_band, values) + weights(mirror, values)) * parity
        other = (weights(extra[:1], values) + weights(extra[1:], values)) * parity
        return jnp.where(top, 0.5 * whole, whole), jnp.where(top, 0.5 * other, whole)

    own = jnp.arange(length, dtype=jnp.int32)
    y_cos, y_sin = angles(own, own[: length // 2], length)
    nyquist = jnp.where(own % 2 == 1, -1.0, 1.0).astype(F32) / math.sqrt(length)
    y_sin = y_sin.at[:, 0].set(-nyquist)
    across = jnp.arange(wide, dtype=jnp.int32)
    x_cos, x_sin = angles(across, across, wide)
    flip = jnp.where(own % 2 == 1, flags[0], 1.0)

    def y_forward(field):
        field = field * flip
        both = jnp.stack([dot("cxy,yk->ckx", field, y_cos), -dot("cxy,yk->ckx", field, y_sin)], 1)
        both = both.reshape(comps, 2, near, modes, rows).transpose(2, 0, 4, 1, 3)
        return lax.all_to_all(both, NEAR, 0, 0, tiled=True)

    def x_stage(given, filt, added):
        given = given.transpose(1, 3, 4, 0, 2).reshape(comps, 2, modes, near * rows)
        real = dot("cpkx,xm->cpkm", given, x_cos[: near * rows])
        imag = -dot("cpkx,xm->cpkm", given, x_sin[: near * rows])
        a, b = filt
        out_real = a * real[:, 0] - b * imag[:, 1]
        out_imag = a * imag[:, 0] + b * real[:, 1]
        if added is not None:
            out_real, out_imag = out_real + added[:, 0], out_imag + added[:, 1]
        first = dot("ckm,mx->ckx", out_real, x_cos) - dot("ckm,mx->ckx", out_imag, x_sin)
        second = dot("ckm,mx->ckx", out_real, x_sin) + dot("ckm,mx->ckx", out_imag, x_cos)
        both = jnp.stack([first, second], 1).reshape(comps, 2, modes, far, rows).transpose(3, 0, 4, 1, 2)
        return lax.all_to_all(both, AXES, 0, 0, tiled=True)

    def y_inverse(given):
        given = given.reshape(2, near, comps, rows, 2, modes).transpose(0, 4, 2, 3, 1, 5)
        given = given.reshape(2, 2, comps, rows, length // 2)
        half = dot("hcxk,yk->hcxy", given[:, 0], y_cos) - dot("hcxk,yk->hcxy", given[:, 1], y_sin)
        return half[0] + half[1] * jnp.where(own % 2 == 1, -1.0, 1.0)

    def phi(s):
        return jnp.stack(friction(s[0], s[1], s[2], slip_field[0], slip_field[1]))

    now = filters(table[:, 0] + table[:, 1])
    later = filters(table[:, 0])
    stress = prestress + y_inverse(x_stage(y_forward(slip_rate), now, past))
    shift = 0.5 * (phi(stress) - slip_rate)
    second = phi(stress + y_inverse(x_stage(y_forward(shift), later, None)))
    return second, slip_field + 0.25 * (slip_rate + second)


def solution(mesh):
    shape = mesh.devices.shape
    ours = Mesh(mesh.devices.reshape(2, shape[0] // 2, shape[1]), AXES)

    def on_device(slip_rate, slip_field, prestress, history, kernel, band_len, mode_band):
        args = (slip_rate, slip_field, prestress, history, kernel, band_len, mode_band)
        rows, modes = slip_rate.shape[1], mode_band.shape[0]
        near = lax.axis_size(NEAR)
        if 2 * modes == LANES and 2 * rows == LANES and near % PIECES == 0 and slip_rate.shape[0] == 3:
            return with_kernels(*args)
        return plain(*args)

    rows = P(None, AXES, None)
    return jax.shard_map(
        on_device,
        mesh=ours,
        in_specs=(rows, rows, rows, P(None, None, None, AXES, None), P(), P(), P(AXES, None)),
        out_specs=(rows, rows),
        check_vma=False,
    )
```
